32 devices in a mesh: groups: 2 (over y), pool: 16 (over z, x, core).
Axes of the slice: x: 2, y: 2, z: 4, core: 2. Of those that a mesh axis runs over, the one named last changes fastest.
Arguments:
- anchors: bfloat16 [4096, 1024], P(('groups', 'pool')), parts along dimension 0, may hold values from -7 to 7
- deltas: bfloat16 [4096, 15, 1024], P(('groups', 'pool')), parts along dimension 0, may hold values from -5 to 5
- scales: float32 [4096, 8], P(('groups', 'pool')), parts along dimension 0, may hold values from 0.15 to 0.8
- queries: bfloat16 [32, 8, 8192], P('groups'), parts along dimension 0, may hold values from -7 to 7
- lengths: int32 [32], P('groups'), parts along dimension 0, may hold values from 64 to 192, as said below
- page_owner: int32 [4096], P('groups'), parts along dimension 0, may hold values from 0 to 15, as said below
Outputs:
- decoded_cache: bfloat16 [4096, 16, 1024], P(('groups', 'pool')), parts along dimension 0
- attention: bfloat16 [32, 8, 8192], P('groups', None, 'pool'), parts along dimension 0
The draws below stay inside these ranges and needn't reach their ends.
There are 2 independent parts, one for each index of `groups`. The reference program is written for one: setup_inputs(seed, part) draws one part's arguments, and reference() takes and returns one part's arrays. A program takes and returns all parts, laid end to end along the dimension named above; each array names one. Nothing has to cross between parts.
Inputs may be any that keep to these rules, and one draw needn't show every extreme that they name: `lengths`: pages of each request; together they cover all 2048 pages of the group. `page_owner`: each prefill device sends either none or exactly 16 of its pages to each decode device, and each decode device owns exactly 128 pages.
All inputs are finite; a program needn't handle non-finite values.
Results may differ from the reference program's by a relative error of at most 0.0046.
Values may be sent and summed in bfloat16 or wider, within the bound.
No kernel may reach another device: no remote copies, remote signals or barrier semaphores. Data moves between devices by JAX's collectives and lax.ppermute only.
A program may use at most 192 MiB of HBM per device.

```python
import math
import jax
import jax.numpy as jnp
from jax import lax

QH = 64
KVH = 4
HD = 128
PAGE = 16
STEPS = 8
REQS = 16
PG_DEV = 128
KVW = 1024
CAPS = 16
PAGES = 2048
LMOST = 192
LMIN = 64
N_POOL = 16


def draw_anchors(key, part):
    key = jax.random.fold_in(key, 5)
    key_base = jax.random.fold_in(key, 1)
    values = 1.5 * jax.random.truncated_normal(key_base, -4.0, 4.0, (PAGES, KVW), jnp.float32)
    return values.astype(jnp.bfloat16)


def draw_queries(key, part):
    key = jax.random.fold_in(key, 7)
    key_base = jax.random.fold_in(key, 1)
    values = 1.5 * jax.random.truncated_normal(key_base, -4.0, 4.0, (REQS, STEPS, QH, HD), jnp.float32)
    return values.reshape(REQS, STEPS, QH * HD).astype(jnp.bfloat16)


def draw_lengths(key, part):
    key = jax.random.fold_in(key, 13)
    spare = LMOST - LMIN
    others = REQS - 2
    rest = PAGES - REQS * LMIN - spare
    base = rest // others
    extra = rest % others
    shares = base + (jnp.arange(others, dtype=jnp.int32) < extra).astype(jnp.int32)
    half = others // 2
    left = shares[0:2 * half:2]
    right = shares[1:2 * half:2]
    lowest = jnp.maximum(-left, right - spare)
    highest = jnp.minimum(spare - left, right)
    moved = jax.random.randint(jax.random.fold_in(key, 1), (half,), lowest, highest + 1, dtype=jnp.int32)
    paired = jnp.stack([left + moved, right - moved], axis=1).reshape(2 * half)
    shares = jnp.concatenate([paired, shares[2 * half:]])
    every = jnp.concatenate([jnp.array([spare, 0], dtype=jnp.int32), shares]) + LMIN
    order = jax.random.permutation(jax.random.fold_in(key, 2), REQS)
    return every[order].astype(jnp.int32)


def draw_page_owner(key, part):
    key = jax.random.fold_in(key, 11)
    group_count = PG_DEV // CAPS
    outer = jax.random.permutation(jax.random.fold_in(key, 1), N_POOL)
    inner = jax.random.permutation(jax.random.fold_in(key, 2), N_POOL)
    offsets = jax.random.permutation(jax.random.fold_in(key, 3), N_POOL)[:group_count]
    sender_keys = jax.random.split(jax.random.fold_in(key, 4), N_POOL)
    local_order = jax.vmap(lambda each_key: jax.random.permutation(each_key, PG_DEV))(sender_keys)
    group_index = local_order // CAPS
    senders = jnp.arange(N_POOL)[:, None]
    owners = outer[(inner[senders] + offsets[group_index]) % N_POOL]
    return owners.reshape(PAGES).astype(jnp.int32)


def level_of(own_key, dims, cuts, low, largest):
    def one(position, shards_of):
        heights = jax.random.uniform(jax.random.fold_in(jax.random.fold_in(own_key, 6), position), (shards_of,), jnp.float32, low / len(cuts), largest / len(cuts))
        return jnp.repeat(jnp.exp(heights), dims[position] // shards_of).reshape((-1,) + (1,) * (len(dims) - position - 1))

    loudness = one(*cuts[0])
    for cut in cuts[1:]:
        loudness = loudness * one(*cut)
    return loudness


def gaussian(own_key, extent, scale, most, cuts=(), held_as=jnp.bfloat16):
    values = jax.random.normal(own_key, extent, jnp.float32) * scale
    if len(cuts) > 0:
        values = level_of(own_key, extent, cuts, -0.22, 0.18) * values
    return jnp.clip(values, min=-most, max=most).astype(held_as)


def setup_inputs(seed: int = 0, part: int = 0) -> dict:
    streams_of = jax.random.split(jax.random.key(seed), 7)
    own_keys = jax.random.split(jax.random.fold_in(streams_of[6], part), 7)
    return {
        "anchors": draw_anchors(jax.random.fold_in(jax.random.fold_in(streams_of[6], part), 71), part),
        "deltas": gaussian(own_keys[1], (PAGES, PAGE - 1, KVW), 1.0, 5.0, ((0, 16),)),
        "scales": jnp.clip(jnp.exp(math.log(0.8) - 1.6739764 * jax.random.uniform(own_keys[2], (PAGES, 2 * KVH), jnp.float32) ** level_of(own_keys[2], (PAGES, 2 * KVH), ((0, 16),), -0.2, 0.2)), 0.15, 0.8),
        "queries": draw_queries(jax.random.fold_in(jax.random.fold_in(streams_of[6], part), 71), part),
        "lengths": draw_lengths(jax.random.fold_in(jax.random.fold_in(streams_of[6], part), 71), part),
        "page_owner": draw_page_owner(jax.random.fold_in(jax.random.fold_in(streams_of[6], part), 71), part),
    }


def decode_pages(anchors, deltas, scales):
    block_scale = jnp.repeat(scales, HD, axis=1)
    rebuilt = anchors[:, None, :].astype(jnp.float32) + block_scale[:, None, :] * deltas.astype(jnp.float32)
    return jnp.concatenate([anchors[:, None, :], rebuilt.astype(jnp.bfloat16)], axis=1)


def reference(anchors, deltas, scales, queries, lengths, page_owner):
    ordering = jnp.argsort(page_owner, stable=True).astype(jnp.int32)
    decoded_cache = decode_pages(anchors[ordering], deltas[ordering], scales[ordering])
    request_ends = jnp.cumsum(lengths).astype(jnp.int32)
    group_size = QH // KVH

    def block_step(running, block_index):
        run_max, run_totals, run_numer = running
        start = (block_index * PG_DEV).astype(jnp.int32)
        page_ids = start + jnp.arange(PG_DEV, dtype=jnp.int32)
        pages = decode_pages(lax.dynamic_slice_in_dim(anchors, start, PG_DEV, 0),
                             lax.dynamic_slice_in_dim(deltas, start, PG_DEV, 0),
                             lax.dynamic_slice_in_dim(scales, start, PG_DEV, 0))
        requests = jnp.sum((page_ids[:, None] >= request_ends[None, :]).astype(jnp.int32), axis=1)
        key_rows = pages[:, :, :KVH * HD].reshape(PG_DEV, PAGE, KVH, HD).astype(jnp.float32)
        value_rows = pages[:, :, KVH * HD:].reshape(PG_DEV, PAGE, KVH, HD).astype(jnp.float32)
        picked = queries[requests].reshape(PG_DEV, STEPS, KVH, group_size, HD).astype(jnp.float32)
        scores = jnp.einsum("nskgd,ntkd->nskgt", picked, key_rows) * (HD ** -0.5)
        page_max = jnp.max(scores, axis=4)
        exponent = jnp.exp(scores - page_max[..., None])
        page_sum = jnp.sum(exponent, axis=4)
        weights = lax.optimization_barrier(exponent.astype(jnp.bfloat16)).astype(jnp.float32)
        page_out = jnp.einsum("nskgt,ntkd->nskgd", weights, value_rows)
        onehot = requests[None, :] == jnp.arange(REQS, dtype=jnp.int32)[:, None]
        block_max = jnp.max(jnp.where(onehot[:, :, None, None, None], page_max[None], -1e30), axis=1)
        new_max = jnp.maximum(run_max, block_max)
        keeping = jnp.exp(run_max - new_max)
        factor = jnp.exp(page_max - new_max[requests])
        spread = onehot.astype(jnp.float32)[:, :, None, None, None] * factor[None]
        run_totals = run_totals * keeping + jnp.sum(spread * page_sum[None], axis=1)
        run_numer = run_numer * keeping[..., None] + jnp.einsum(
            "rnskg,nskgd->rskgd", spread, page_out, precision=lax.Precision.HIGHEST)
        return (new_max, run_totals, run_numer), None

    start_max = jnp.full((REQS, STEPS, KVH, group_size), -1e30, jnp.float32)
    start_totals = jnp.zeros((REQS, STEPS, KVH, group_size), jnp.float32)
    start_numer = jnp.zeros((REQS, STEPS, KVH, group_size, HD), jnp.float32)
    finals, ignored = lax.scan(block_step, (start_max, start_totals, start_numer),
                               jnp.arange(PAGES // PG_DEV, dtype=jnp.int32))
    totals, numerator = finals[1], finals[2]
    attention = (numerator / totals[..., None]).reshape(REQS, STEPS, QH * HD).astype(jnp.bfloat16)
    return decoded_cache, attention
```

```python
import functools
import jax
import jax.numpy as jnp
from jax import lax
from jax.experimental import pallas as pl
from jax.experimental.pallas import tpu as pltpu
from jax.sharding import PartitionSpec as P

QH = 64
KVH = 4
HD = 128
PAGE = 16
STEPS = 8
REQS = 16
KVW = 2 * KVH * HD
SPAN = 3
LOW = -1e30
VMEM_LIMIT = 48 * 1024 * 1024
F32 = jnp.float32
BF16 = jnp.bfloat16
I32 = jnp.int32


def decode_kernel(chunk, place, flags, blocks, anchors, deltas, scales, out, rows, staged, sems):
    step = pl.program_id(0)
    for head in range(2 * KVH):
        cols = slice(head * HD, (head + 1) * HD)
        scale = jnp.broadcast_to(scales[:, head : head + 1], (chunk, HD))
        anchor = anchors[:, cols].astype(F32)
        rows[head * PAGE * chunk : head * PAGE * chunk + chunk, :] = anchor
        for token in range(1, PAGE):
            start = (head * PAGE + token) * chunk
            rows[start : start + chunk, :] = anchor + scale * deltas[token - 1, :, cols].astype(F32)
    for page in range(chunk):
        picked = [
            rows[pl.ds(head * PAGE * chunk + page, PAGE, stride=chunk), :]
            for head in range(2 * KVH)
        ]
        staged[place[step * chunk + page]] = jnp.concatenate(picked, axis=1).astype(BF16)

    @pl.when(step == pl.num_programs(0) - 1)
    def flush():
        copies = []
        for owner in range(16):
            copy = pltpu.make_async_copy(
                staged.at[pl.ds(blocks[owner] * PAGE, PAGE)],
                out.at[pl.ds(owner * PAGE, PAGE)],
                sems.at[owner],
            )
            pl.when(flags[owner] > 0)(copy.start)
            copies.append(copy)
        for owner in range(16):
            pl.when(flags[owner] > 0)(copies[owner].wait)


def decode_sorted(place, flags, blocks, anchors, deltas, scales):
    number = anchors.shape[0]
    chunk = 16
    return pl.pallas_call(
        functools.partial(decode_kernel, chunk),
        grid_spec=pltpu.PrefetchScalarGridSpec(
            num_scalar_prefetch=3,
            grid=(number // chunk,),
            in_specs=[
                pl.BlockSpec((chunk, KVW), lambda i, *_: (i, 0)),
                pl.BlockSpec((PAGE - 1, chunk, KVW), lambda i, *_: (0, i, 0)),
                pl.BlockSpec((chunk, 2 * KVH), lambda i, *_: (i, 0)),
            ],
            out_specs=pl.BlockSpec(memory_space=pl.ANY),
            scratch_shapes=[
                pltpu.VMEM((2 * KVH * PAGE * chunk, HD), F32),
                pltpu.VMEM((number, PAGE, KVW), BF16),
                pltpu.SemaphoreType.DMA((16,)),
            ],
        ),
        out_shape=jax.ShapeDtypeStruct((16 * PAGE, PAGE, KVW), BF16),
        compiler_params=pltpu.CompilerParams(vmem_limit_bytes=VMEM_LIMIT),
        name="decode_sorted",
    )(place, flags, blocks, anchors, deltas, scales)


def attend_kernel(base, requests, queries, key_anchor, val_anchor, key_delta, val_delta, scales, out, keys, vals):
    head = pl.program_id(0)
    number = key_anchor.shape[0]
    lane = lax.broadcasted_iota(I32, scales.shape, 1)
    table = scales[...]
    key_scale = jnp.sum(jnp.where(lane == head, table, 0.0), axis=1, keepdims=True)
    val_scale = jnp.sum(jnp.where(lane == head + KVH, table, 0.0), axis=1, keepdims=True)
    for anchor, delta, scale, kept in (
        (key_anchor, key_delta, key_scale, keys),
        (val_anchor, val_delta, val_scale, vals),
    ):
        first = anchor[...]
        kept[0:number, :] = first
        wide = first.astype(F32)
        for token in range(1, PAGE):
            kept[token * number : (token + 1) * number, :] = (
                wide + scale * delta[token - 1].astype(F32)
            ).astype(BF16)
    token_request = jnp.concatenate([requests[...]] * PAGE, axis=1) - base[0]
    rows = STEPS * QH // KVH
    eye = lax.broadcasted_iota(I32, (rows, rows), 0) == lax.broadcasted_iota(I32, (rows, rows), 1)
    pieces = []
    for slot in range(SPAN):
        scores = lax.dot_general(
            queries[slot], keys[...], (((1,), (1,)), ((), ())), preferred_element_type=F32
        ) * HD ** (-0.5)
        inside = token_request == slot
        scores = jnp.where(inside, scores, LOW)
        top = jnp.max(scores, axis=1, keepdims=True)
        exponent = jnp.where(inside, jnp.exp(scores - top), 0.0)
        total = jnp.maximum(jnp.sum(exponent, axis=1, keepdims=True), 1e-30)
        numer = jnp.dot(exponent.astype(BF16), vals[...], preferred_element_type=F32)
        mean = (numer * (1.0 / total)).astype(BF16)
        quarter = rows // 4
        for part in range(4):
            out[part, slot * quarter : (slot + 1) * quarter, :] = mean[
                part * quarter : (part + 1) * quarter
            ]
        level = top + jnp.log(total)
        line = jnp.sum(jnp.where(eye, level, 0.0), axis=0, keepdims=True)
        for _ in range(3):
            piece = line.astype(BF16).astype(F32)
            pieces.append(piece)
            line = line - piece
    pieces.append(jnp.zeros((16 - len(pieces), rows), F32))
    stats = jnp.concatenate(pieces, axis=0).astype(BF16)
    for part in range(4):
        out[part, 96:112, :] = stats


def attend(base, requests, queries, anchors, deltas, scales):
    number = anchors.shape[0]
    rows = STEPS * QH // KVH
    return pl.pallas_call(
        attend_kernel,
        grid_spec=pltpu.PrefetchScalarGridSpec(
            num_scalar_prefetch=1,
            grid=(KVH,),
            in_specs=[
                pl.BlockSpec((1, number), lambda h, *_: (0, 0)),
                pl.BlockSpec((SPAN, rows, HD), lambda h, *_: (0, h, 0)),
                pl.BlockSpec((number, HD), lambda h, *_: (0, h)),
                pl.BlockSpec((number, HD), lambda h, *_: (0, h + KVH)),
                pl.BlockSpec((PAGE - 1, number, HD), lambda h, *_: (0, 0, h)),
                pl.BlockSpec((PAGE - 1, number, HD), lambda h, *_: (0, 0, h + KVH)),
                pl.BlockSpec((number, 2 * KVH), lambda h, *_: (0, 0)),
            ],
            out_specs=pl.BlockSpec((4, 112, HD), lambda h, *_: (h, 0, 0)),
            scratch_shapes=[
                pltpu.VMEM((PAGE * number, HD), BF16),
                pltpu.VMEM((PAGE * number, HD), BF16),
            ],
        ),
        out_shape=jax.ShapeDtypeStruct((16, 112, HD), BF16),
        compiler_params=pltpu.CompilerParams(vmem_limit_bytes=VMEM_LIMIT),
        cost_estimate=pl.CostEstimate(
            flops=SPAN * KVH * rows * number * PAGE * HD * 4,
            bytes_accessed=5 * 2**20,
            transcendentals=SPAN * KVH * rows * number * PAGE,
        ),
        name="attend",
    )(base, requests, queries, anchors, anchors, deltas, deltas, scales)


def merge_kernel(bases, part, parts, out, level, top, total, numer):
    quarter = 32
    row = lax.broadcasted_iota(I32, (quarter, HD), 0)
    lane = lax.broadcasted_iota(I32, (quarter, HD), 1)
    mine = lane == row + quarter * part[0]
    top[...] = jnp.full(top.shape, LOW, F32)
    total[...] = jnp.zeros(total.shape, F32)
    numer[...] = jnp.zeros(numer.shape, F32)
    for sender in range(16):
        stats = parts[sender, 96:112, :].astype(F32)
        for slot in range(SPAN):
            line = stats[3 * slot : 3 * slot + 1] + (
                stats[3 * slot + 1 : 3 * slot + 2] + stats[3 * slot + 2 : 3 * slot + 3]
            )
            column = jnp.sum(jnp.where(mine, line, 0.0), axis=1, keepdims=True)
            column = jnp.broadcast_to(column, (quarter, HD))
            level[sender * SPAN + slot] = column
            request = bases[sender] + slot
            top[request] = jnp.maximum(top[request], column)
    for sender in range(16):
        for slot in range(SPAN):
            request = bases[sender] + slot
            weight = jnp.exp(level[sender * SPAN + slot] - top[request])
            mean = parts[sender, slot * quarter : (slot + 1) * quarter, :].astype(F32)
            total[request] += weight
            numer[request] += weight * mean
    for request in range(REQS):
        result = (numer[request] / total[request]).astype(BF16)
        for group in range(4):
            out[request, :, group * HD : (group + 1) * HD] = result[
                group * STEPS : (group + 1) * STEPS
            ]


def merge(bases, part, parts):
    return pl.pallas_call(
        merge_kernel,
        grid_spec=pltpu.PrefetchScalarGridSpec(
            num_scalar_prefetch=2,
            grid=(1,),
            in_specs=[pl.BlockSpec((16, 112, HD), lambda i, *_: (0, 0, 0))],
            out_specs=pl.BlockSpec((REQS, STEPS, 4 * HD), lambda i, *_: (0, 0, 0)),
            scratch_shapes=[
                pltpu.VMEM((16 * SPAN, 32, HD), F32),
                pltpu.VMEM((REQS, 32, HD), F32),
                pltpu.VMEM((REQS, 32, HD), F32),
                pltpu.VMEM((REQS, 32, HD), F32),
            ],
        ),
        out_shape=jax.ShapeDtypeStruct((REQS, STEPS, 4 * HD), BF16),
        compiler_params=pltpu.CompilerParams(vmem_limit_bytes=VMEM_LIMIT),
        name="merge",
    )(bases, part, parts)


def assemble_kernel(flags, blocks, arrived, out, sems):
    copies = []
    for sender in range(16):
        copy = pltpu.make_async_copy(
            arrived.at[pl.ds(sender * PAGE, PAGE)],
            out.at[pl.ds(blocks[sender] * PAGE, PAGE)],
            sems.at[sender],
        )
        pl.when(flags[sender] > 0)(copy.start)
        copies.append(copy)
    for sender in range(16):
        pl.when(flags[sender] > 0)(copies[sender].wait)


def assemble(flags, blocks, arrived, number):
    return pl.pallas_call(
        assemble_kernel,
        grid_spec=pltpu.PrefetchScalarGridSpec(
            num_scalar_prefetch=2,
            grid=(1,),
            in_specs=[pl.BlockSpec(memory_space=pl.ANY)],
            out_specs=pl.BlockSpec(memory_space=pl.ANY),
            scratch_shapes=[pltpu.SemaphoreType.DMA((16,))],
        ),
        out_shape=jax.ShapeDtypeStruct((number, PAGE, KVW), BF16),
        name="assemble",
    )(flags, blocks, arrived)


def local_slab(anchors, deltas, scales, queries, lengths, page_owner):
    position = lax.axis_index("pool")
    number = anchors.shape[0]
    by_token = jnp.transpose(deltas, (1, 0, 2))
    ends = jnp.cumsum(lengths)
    owners = lax.dynamic_slice_in_dim(page_owner, position * number, number, 0)
    order = jnp.arange(number, dtype=I32)
    ahead = (owners[None, :] < owners[:, None]) | (
        (owners[None, :] == owners[:, None]) & (order[None, :] < order[:, None])
    )
    place = jnp.sum(ahead.astype(I32), axis=1)
    devices = jnp.arange(16, dtype=I32)
    sent = jnp.any(owners[None, :] == devices[:, None], axis=1).astype(I32)
    slabs = decode_sorted(place, sent, jnp.cumsum(sent) - sent, anchors, by_token, scales)
    arrived = lax.all_to_all(slabs, "pool", split_axis=0, concat_axis=0, tiled=True)
    taken = jnp.any((page_owner == position).reshape(16, number), axis=1).astype(I32)
    bases = jnp.sum((devices[:, None] * number >= ends[None, :]).astype(I32), axis=1)
    bases = jnp.minimum(bases, REQS - SPAN)
    base = lax.dynamic_slice_in_dim(bases, position, 1, 0)
    pages = position * number + order
    requests = jnp.sum((pages[:, None] >= ends[None, :]).astype(I32), axis=1)[None, :]
    near = lax.dynamic_slice_in_dim(queries, base[0], SPAN, 0)
    near = near.reshape(SPAN, STEPS, QH, HD).transpose(0, 2, 1, 3).reshape(SPAN, QH * STEPS, HD)
    parts = attend(base, requests, near, anchors, by_token, scales)
    swapped = lax.all_to_all(parts, "pool", split_axis=0, concat_axis=0, tiled=True)
    attention = merge(bases, (position % 4)[None].astype(I32), swapped)
    cache = assemble(taken, jnp.cumsum(taken) - taken, arrived, number)
    return (cache, attention)


def decode_pages(anchors, deltas, scales):
    block_scale = jnp.repeat(scales, HD, axis=1)
    rebuilt = anchors[:, None, :].astype(jnp.float32) + block_scale[:, None, :] * deltas.astype(
        jnp.float32
    )
    return jnp.concatenate([anchors[:, None, :], rebuilt.astype(jnp.bfloat16)], axis=1)


def page_scores(work_pages, queries, requests):
    number = work_pages.shape[0]
    key_rows = work_pages[:, :, : KVH * HD].reshape(number, PAGE, KVH, HD)
    picked = jnp.take(queries, requests, axis=0).reshape(number, STEPS, KVH, QH // KVH, HD)
    scores = jnp.einsum(
        "nskgd,ntkd->nskgt", picked, key_rows, preferred_element_type=jnp.float32
    ) * HD ** (-0.5)
    return (scores, jnp.max(scores, axis=4))


def accumulate(scores, page_max, work_pages, requests, shift_max):
    number = work_pages.shape[0]
    rows_out = shift_max.shape[0]
    block_size = min(32, number)
    blocks = number // block_size
    value_rows = work_pages[:, :, KVH * HD :].reshape(blocks, block_size, PAGE, KVH, HD)
    score_blocks = scores.reshape((blocks, block_size) + scores.shape[1:])
    max_blocks = page_max.reshape((blocks, block_size) + page_max.shape[1:])
    request_blocks = requests.reshape(blocks, block_size)

    def block_step(running, pieces):
        totals, numerator = running
        block_scores, block_max, block_values, block_requests = pieces
        exponent = jnp.exp(block_scores - block_max[..., None])
        weights = exponent.astype(jnp.bfloat16)
        page_out = jnp.einsum(
            "nskgt,ntkd->nskgd", weights, block_values, preferred_element_type=jnp.float32
        )
        factor = jnp.exp(block_max - jnp.take(shift_max, block_requests, axis=0))
        select = (block_requests[None, :] == jnp.arange(rows_out, dtype=jnp.int32)[:, None]).astype(
            jnp.float32
        )
        spread = select[:, :, None, None, None] * factor[None]
        totals = totals + jnp.sum(spread * jnp.sum(exponent, axis=4)[None], axis=1)
        numerator = numerator + jnp.einsum(
            "rnskg,nskgd->rskgd", spread, page_out, precision=lax.Precision.HIGHEST
        )
        return ((totals, numerator), None)

    start_totals = jnp.zeros(shift_max.shape, jnp.float32)
    start_numer = jnp.zeros(shift_max.shape + (HD,), jnp.float32)
    finals, ignored = lax.scan(
        block_step,
        (start_totals, start_numer),
        (score_blocks, max_blocks, value_rows, request_blocks),
    )
    return finals


def request_of(index, request_ends):
    return jnp.sum((index[:, None] >= request_ends[None, :]).astype(jnp.int32), axis=1)


def local(anchors, deltas, scales, queries, lengths, page_owner):
    devices = lax.axis_size("pool")
    position = lax.axis_index("pool")
    number = anchors.shape[0]
    capacity = max(2, 2 * number // devices)
    pages = decode_pages(anchors, deltas, scales)
    request_ends = jnp.cumsum(lengths)
    owners = lax.dynamic_slice_in_dim(page_owner, position * number, number, 0)
    marked = (owners[:, None] == jnp.arange(devices, dtype=jnp.int32)[None, :]).astype(jnp.int32)
    ranking = jnp.sum((jnp.cumsum(marked, axis=0) - 1) * marked, axis=1)
    slot_ids = owners * capacity + ranking
    matches = slot_ids[None, :] == jnp.arange(devices * capacity, dtype=jnp.int32)[:, None]
    sources = jnp.sum(jnp.where(matches, jnp.arange(number, dtype=jnp.int32)[None, :], 0), axis=1)
    outgoing = jnp.take(pages, sources, axis=0)
    arrived = lax.all_to_all(outgoing, "pool", split_axis=0, concat_axis=0, tiled=True)
    held_pages = jnp.nonzero(page_owner == position, size=number)[0].astype(jnp.int32)
    senders = held_pages // number
    before = jnp.sum((held_pages[None, :] < (senders * number)[:, None]).astype(jnp.int32), axis=1)
    row_ids = senders * capacity + jnp.arange(number, dtype=jnp.int32) - before
    cache = jnp.take(arrived, row_ids, axis=0)
    columns = QH * HD // devices
    requests = request_of(held_pages, request_ends)
    scores, page_max = page_scores(cache, queries, requests)
    onehot = requests[None, :] == jnp.arange(REQS, dtype=jnp.int32)[:, None]
    local_max = jnp.max(jnp.where(onehot[:, :, None, None, None], page_max[None], -1e30), axis=1)
    global_max = lax.pmax(local_max.astype(jnp.bfloat16), "pool").astype(local_max.dtype)
    totals, numerator = accumulate(scores, page_max, cache, requests, global_max)
    summed, numerator = lax.psum((totals, numerator), "pool")
    whole = (numerator / summed[..., None]).reshape(REQS, STEPS, QH * HD)
    result = lax.dynamic_slice_in_dim(whole, position * columns, columns, 2)
    return (cache, result.astype(jnp.bfloat16))


def solution(mesh):
    placed = (
        P(("groups", "pool"), None),
        P(("groups", "pool"), None, None),
        P(("groups", "pool"), None),
        P("groups", None, None),
        P("groups"),
        P("groups"),
    )
    slab = mesh.shape["pool"] == 16
    return jax.shard_map(
        local_slab if slab else local,
        mesh=mesh,
        in_specs=placed,
        out_specs=(P(("groups", "pool"), None, None), P("groups", None, "pool")),
        check_vma=False,
    )
```

```python
import functools
import jax
import jax.numpy as jnp
from jax import lax
from jax.experimental import pallas as pl
from jax.experimental.pallas import tpu as pltpu
from jax.sharding import PartitionSpec as P

QH = 64
KVH = 4
HD = 128
PAGE = 16
STEPS = 8
REQS = 16
KVW = 2 * KVH * HD
SPAN = 3
LOW = -1e30
VMEM_LIMIT = 48 * 1024 * 1024
F32 = jnp.float32
BF16 = jnp.bfloat16
I32 = jnp.int32


def decode_kernel(chunk, place, flags, blocks, anchors, deltas, scales, out, rows, staged, sems):
    step = pl.program_id(0)
    for head in range(2 * KVH):
        cols = slice(head * HD, (head + 1) * HD)
        scale = jnp.broadcast_to(scales[:, head : head + 1], (chunk, HD))
        anchor = anchors[:, cols].astype(F32)
        rows[head * PAGE * chunk : head * PAGE * chunk + chunk, :] = anchor
        for token in range(1, PAGE):
            start = (head * PAGE + token) * chunk
            rows[start : start + chunk, :] = anchor + scale * deltas[token - 1, :, cols].astype(F32)
    for page in range(chunk):
        picked = [
            rows[pl.ds(head * PAGE * chunk + page, PAGE, stride=chunk), :]
            for head in range(2 * KVH)
        ]
        staged[place[step * chunk + page]] = jnp.concatenate(picked, axis=1).astype(BF16)

    @pl.when(step == pl.num_programs(0) - 1)
    def flush():
        copies = []
        for owner in range(16):
            copy = pltpu.make_async_copy(
                staged.at[pl.ds(blocks[owner] * PAGE, PAGE)],
                out.at[pl.ds(owner * PAGE, PAGE)],
                sems.at[owner],
            )
            pl.when(flags[owner] > 0)(copy.start)
            copies.append(copy)
        for owner in range(16):
            pl.when(flags[owner] > 0)(copies[owner].wait)


def decode_sorted(place, flags, blocks, anchors, deltas, scales):
    number = anchors.shape[0]
    chunk = 16
    return pl.pallas_call(
        functools.partial(decode_kernel, chunk),
        grid_spec=pltpu.PrefetchScalarGridSpec(
            num_scalar_prefetch=3,
            grid=(number // chunk,),
            in_specs=[
                pl.BlockSpec((chunk, KVW), lambda i, *_: (i, 0)),
                pl.BlockSpec((PAGE - 1, chunk, KVW), lambda i, *_: (0, i, 0)),
                pl.BlockSpec((chunk, 2 * KVH), lambda i, *_: (i, 0)),
            ],
            out_specs=pl.BlockSpec(memory_space=pl.ANY),
            scratch_shapes=[
                pltpu.VMEM((2 * KVH * PAGE * chunk, HD), F32),
                pltpu.VMEM((number, PAGE, KVW), BF16),
                pltpu.SemaphoreType.DMA((16,)),
            ],
        ),
        out_shape=jax.ShapeDtypeStruct((16 * PAGE, PAGE, KVW), BF16),
        compiler_params=pltpu.CompilerParams(vmem_limit_bytes=VMEM_LIMIT),
        name="decode_sorted",
    )(place, flags, blocks, anchors, deltas, scales)


def attend_kernel(base, requests, queries, key_anchor, val_anchor, key_delta, val_delta, scales, out, keys, vals):
    head = pl.program_id(0)
    number = key_anchor.shape[0]
    lane = lax.broadcasted_iota(I32, scales.shape, 1)
    table = scales[...]
    key_scale = jnp.sum(jnp.where(lane == head, table, 0.0), axis=1, keepdims=True)
    val_scale = jnp.sum(jnp.where(lane == head + KVH, table, 0.0), axis=1, keepdims=True)
    for anchor, delta, scale, kept in (
        (key_anchor, key_delta, key_scale, keys),
        (val_anchor, val_delta, val_scale, vals),
    ):
        first = anchor[...]
        kept[0:number, :] = first
        wide = first.astype(F32)
        for token in range(1, PAGE):
            kept[token * number : (token + 1) * number, :] = (
                wide + scale * delta[token - 1].astype(F32)
            ).astype(BF16)
    token_request = jnp.concatenate([requests[...]] * PAGE, axis=1) - base[0]
    rows = STEPS * QH // KVH
    eye = lax.broadcasted_iota(I32, (rows, rows), 0) == lax.broadcasted_iota(I32, (rows, rows), 1)
    pieces = []
    for slot in range(SPAN):
        scores = lax.dot_general(
            queries[slot], keys[...], (((1,), (1,)), ((), ())), preferred_element_type=F32
        ) * HD ** (-0.5)
        inside = token_request == slot
        scores = jnp.where(inside, scores, LOW)
        top = jnp.max(scores, axis=1, keepdims=True)
        exponent = jnp.where(inside, jnp.exp(scores - top), 0.0)
        total = jnp.maximum(jnp.sum(exponent, axis=1, keepdims=True), 1e-30)
        numer = jnp.dot(exponent.astype(BF16), vals[...], preferred_element_type=F32)
        mean = (numer * (1.0 / total)).astype(BF16)
        quarter = rows // 4
        for part in range(4):
            out[part, slot * quarter : (slot + 1) * quarter, :] = mean[
                part * quarter : (part + 1) * quarter
            ]
        level = top + jnp.log(total)
        line = jnp.sum(jnp.where(eye, level, 0.0), axis=0, keepdims=True)
        for _ in range(3):
            piece = line.astype(BF16).astype(F32)
            pieces.append(piece)
            line = line - piece
    pieces.append(jnp.zeros((16 - len(pieces), rows), F32))
    stats = jnp.concatenate(pieces, axis=0).astype(BF16)
    for part in range(4):
        out[part, 96:112, :] = stats


def attend(base, requests, queries, anchors, deltas, scales):
    number = anchors.shape[0]
    rows = STEPS * QH // KVH
    return pl.pallas_call(
        attend_kernel,
        grid_spec=pltpu.PrefetchScalarGridSpec(
            num_scalar_prefetch=1,
            grid=(KVH,),
            in_specs=[
                pl.BlockSpec((1, number), lambda h, *_: (0, 0)),
                pl.BlockSpec((SPAN, rows, HD), lambda h, *_: (0, h, 0)),
                pl.BlockSpec((number, HD), lambda h, *_: (0, h)),
                pl.BlockSpec((number, HD), lambda h, *_: (0, h + KVH)),
                pl.BlockSpec((PAGE - 1, number, HD), lambda h, *_: (0, 0, h)),
                pl.BlockSpec((PAGE - 1, number, HD), lambda h, *_: (0, 0, h + KVH)),
                pl.BlockSpec((number, 2 * KVH), lambda h, *_: (0, 0)),
            ],
            out_specs=pl.BlockSpec((4, 112, HD), lambda h, *_: (h, 0, 0)),
            scratch_shapes=[
                pltpu.VMEM((PAGE * number, HD), BF16),
                pltpu.VMEM((PAGE * number, HD), BF16),
            ],
        ),
        out_shape=jax.ShapeDtypeStruct((16, 112, HD), BF16),
        compiler_params=pltpu.CompilerParams(vmem_limit_bytes=VMEM_LIMIT),
        cost_estimate=pl.CostEstimate(
            flops=SPAN * KVH * rows * number * PAGE * HD * 4,
            bytes_accessed=5 * 2**20,
            transcendentals=SPAN * KVH * rows * number * PAGE,
        ),
        name="attend",
    )(base, requests, queries, anchors, anchors, deltas, deltas, scales)


def merge_kernel(bases, part, parts, out, level, top, total, numer):
    quarter = 32
    row = lax.broadcasted_iota(I32, (quarter, HD), 0)
    lane = lax.broadcasted_iota(I32, (quarter, HD), 1)
    mine = lane == row + quarter * part[0]
    top[...] = jnp.full(top.shape, LOW, F32)
    total[...] = jnp.zeros(total.shape, F32)
    numer[...] = jnp.zeros(numer.shape, F32)
    for sender in range(16):
        stats = parts[sender, 96:112, :].astype(F32)
        for slot in range(SPAN):
            line = stats[3 * slot : 3 * slot + 1] + (
                stats[3 * slot + 1 : 3 * slot + 2] + stats[3 * slot + 2 : 3 * slot + 3]
            )
            column = jnp.sum(jnp.where(mine, line, 0.0), axis=1, keepdims=True)
            column = jnp.broadcast_to(column, (quarter, HD))
            level[sender * SPAN + slot] = column
            request = bases[sender] + slot
            top[request] = jnp.maximum(top[request], column)
    for sender in range(16):
        for slot in range(SPAN):
            request = bases[sender] + slot
            weight = jnp.exp(level[sender * SPAN + slot] - top[request])
            mean = parts[sender, slot * quarter : (slot + 1) * quarter, :].astype(F32)
            total[request] += weight
            numer[request] += weight * mean
    for request in range(REQS):
        result = (numer[request] / total[request]).astype(BF16)
        for group in range(4):
            out[request, :, group * HD : (group + 1) * HD] = result[
                group * STEPS : (group + 1) * STEPS
            ]


def merge(bases, part, parts):
    return pl.pallas_call(
        merge_kernel,
        grid_spec=pltpu.PrefetchScalarGridSpec(
            num_scalar_prefetch=2,
            grid=(1,),
            in_specs=[pl.BlockSpec((16, 112, HD), lambda i, *_: (0, 0, 0))],
            out_specs=pl.BlockSpec((REQS, STEPS, 4 * HD), lambda i, *_: (0, 0, 0)),
            scratch_shapes=[
                pltpu.VMEM((16 * SPAN, 32, HD), F32),
                pltpu.VMEM((REQS, 32, HD), F32),
                pltpu.VMEM((REQS, 32, HD), F32),
                pltpu.VMEM((REQS, 32, HD), F32),
            ],
        ),
        out_shape=jax.ShapeDtypeStruct((REQS, STEPS, 4 * HD), BF16),
        compiler_params=pltpu.CompilerParams(vmem_limit_bytes=VMEM_LIMIT),
        name="merge",
    )(bases, part, parts)


def assemble_kernel(flags, blocks, arrived, out, staged, in_sems, out_sems):
    reads, writes = [], []
    for sender in range(16):
        rows = pl.ds(blocks[sender] * PAGE, PAGE)
        source = arrived.at[pl.ds(sender * PAGE, PAGE)]
        reads.append(pltpu.make_async_copy(source, staged.at[rows], in_sems.at[sender]))
        writes.append(pltpu.make_async_copy(staged.at[rows], out.at[rows], out_sems.at[sender]))
    for sender in range(16):
        pl.when(flags[sender] > 0)(reads[sender].start)
    for sender in range(16):

        @pl.when(flags[sender] > 0)
        def forward():
            reads[sender].wait()
            writes[sender].start()

    for sender in range(16):
        pl.when(flags[sender] > 0)(writes[sender].wait)


def assemble(flags, blocks, arrived, number):
    return pl.pallas_call(
        assemble_kernel,
        grid_spec=pltpu.PrefetchScalarGridSpec(
            num_scalar_prefetch=2,
            grid=(1,),
            in_specs=[pl.BlockSpec(memory_space=pl.ANY)],
            out_specs=pl.BlockSpec(memory_space=pl.ANY),
            scratch_shapes=[
                pltpu.VMEM((number, PAGE, KVW), BF16),
                pltpu.SemaphoreType.DMA((16,)),
                pltpu.SemaphoreType.DMA((16,)),
            ],
        ),
        out_shape=jax.ShapeDtypeStruct((number, PAGE, KVW), BF16),
        compiler_params=pltpu.CompilerParams(vmem_limit_bytes=VMEM_LIMIT),
        name="assemble",
    )(flags, blocks, arrived)


def local_slab(anchors, deltas, scales, queries, lengths, page_owner):
    position = lax.axis_index("pool")
    number = anchors.shape[0]
    by_token = jnp.transpose(deltas, (1, 0, 2))
    ends = jnp.cumsum(lengths)
    owners = lax.dynamic_slice_in_dim(page_owner, position * number, number, 0)
    order = jnp.arange(number, dtype=I32)
    ahead = (owners[None, :] < owners[:, None]) | (
        (owners[None, :] == owners[:, None]) & (order[None, :] < order[:, None])
    )
    place = jnp.sum(ahead.astype(I32), axis=1)
    devices = jnp.arange(16, dtype=I32)
    sent = jnp.any(owners[None, :] == devices[:, None], axis=1).astype(I32)
    slabs = decode_sorted(place, sent, jnp.cumsum(sent) - sent, anchors, by_token, scales)
    arrived = lax.all_to_all(slabs, "pool", split_axis=0, concat_axis=0, tiled=True)
    taken = jnp.any((page_owner == position).reshape(16, number), axis=1).astype(I32)
    bases = jnp.sum((devices[:, None] * number >= ends[None, :]).astype(I32), axis=1)
    bases = jnp.minimum(bases, REQS - SPAN)
    base = lax.dynamic_slice_in_dim(bases, position, 1, 0)
    pages = position * number + order
    requests = jnp.sum((pages[:, None] >= ends[None, :]).astype(I32), axis=1)[None, :]
    near = lax.dynamic_slice_in_dim(queries, base[0], SPAN, 0)
    near = near.reshape(SPAN, STEPS, QH, HD).transpose(0, 2, 1, 3).reshape(SPAN, QH * STEPS, HD)
    parts = attend(base, requests, near, anchors, by_token, scales)
    swapped = lax.all_to_all(parts, "pool", split_axis=0, concat_axis=0, tiled=True)
    attention = merge(bases, (position % 4)[None].astype(I32), swapped)
    cache = assemble(taken, jnp.cumsum(taken) - taken, arrived, number)
    return (cache, attention)


def decode_pages(anchors, deltas, scales):
    block_scale = jnp.repeat(scales, HD, axis=1)
    rebuilt = anchors[:, None, :].astype(jnp.float32) + block_scale[:, None, :] * deltas.astype(
        jnp.float32
    )
    return jnp.concatenate([anchors[:, None, :], rebuilt.astype(jnp.bfloat16)], axis=1)


def page_scores(work_pages, queries, requests):
    number = work_pages.shape[0]
    key_rows = work_pages[:, :, : KVH * HD].reshape(number, PAGE, KVH, HD)
    picked = jnp.take(queries, requests, axis=0).reshape(number, STEPS, KVH, QH // KVH, HD)
    scores = jnp.einsum(
        "nskgd,ntkd->nskgt", picked, key_rows, preferred_element_type=jnp.float32
    ) * HD ** (-0.5)
    return (scores, jnp.max(scores, axis=4))


def accumulate(scores, page_max, work_pages, requests, shift_max):
    number = work_pages.shape[0]
    rows_out = shift_max.shape[0]
    block_size = min(32, number)
    blocks = number // block_size
    value_rows = work_pages[:, :, KVH * HD :].reshape(blocks, block_size, PAGE, KVH, HD)
    score_blocks = scores.reshape((blocks, block_size) + scores.shape[1:])
    max_blocks = page_max.reshape((blocks, block_size) + page_max.shape[1:])
    request_blocks = requests.reshape(blocks, block_size)

    def block_step(running, pieces):
        totals, numerator = running
        block_scores, block_max, block_values, block_requests = pieces
        exponent = jnp.exp(block_scores - block_max[..., None])
        weights = exponent.astype(jnp.bfloat16)
        page_out = jnp.einsum(
            "nskgt,ntkd->nskgd", weights, block_values, preferred_element_type=jnp.float32
        )
        factor = jnp.exp(block_max - jnp.take(shift_max, block_requests, axis=0))
        select = (block_requests[None, :] == jnp.arange(rows_out, dtype=jnp.int32)[:, None]).astype(
            jnp.float32
        )
        spread = select[:, :, None, None, None] * factor[None]
        totals = totals + jnp.sum(spread * jnp.sum(exponent, axis=4)[None], axis=1)
        numerator = numerator + jnp.einsum(
            "rnskg,nskgd->rskgd", spread, page_out, precision=lax.Precision.HIGHEST
        )
        return ((totals, numerator), None)

    start_totals = jnp.zeros(shift_max.shape, jnp.float32)
    start_numer = jnp.zeros(shift_max.shape + (HD,), jnp.float32)
    finals, ignored = lax.scan(
        block_step,
        (start_totals, start_numer),
        (score_blocks, max_blocks, value_rows, request_blocks),
    )
    return finals


def request_of(index, request_ends):
    return jnp.sum((index[:, None] >= request_ends[None, :]).astype(jnp.int32), axis=1)


def local(anchors, deltas, scales, queries, lengths, page_owner):
    devices = lax.axis_size("pool")
    position = lax.axis_index("pool")
    number = anchors.shape[0]
    capacity = max(2, 2 * number // devices)
    pages = decode_pages(anchors, deltas, scales)
    request_ends = jnp.cumsum(lengths)
    owners = lax.dynamic_slice_in_dim(page_owner, position * number, number, 0)
    marked = (owners[:, None] == jnp.arange(devices, dtype=jnp.int32)[None, :]).astype(jnp.int32)
    ranking = jnp.sum((jnp.cumsum(marked, axis=0) - 1) * marked, axis=1)
    slot_ids = owners * capacity + ranking
    matches = slot_ids[None, :] == jnp.arange(devices * capacity, dtype=jnp.int32)[:, None]
    sources = jnp.sum(jnp.where(matches, jnp.arange(number, dtype=jnp.int32)[None, :], 0), axis=1)
    outgoing = jnp.take(pages, sources, axis=0)
    arrived = lax.all_to_all(outgoing, "pool", split_axis=0, concat_axis=0, tiled=True)
    held_pages = jnp.nonzero(page_owner == position, size=number)[0].astype(jnp.int32)
    senders = held_pages // number
    before = jnp.sum((held_pages[None, :] < (senders * number)[:, None]).astype(jnp.int32), axis=1)
    row_ids = senders * capacity + jnp.arange(number, dtype=jnp.int32) - before
    cache = jnp.take(arrived, row_ids, axis=0)
    columns = QH * HD // devices
    requests = request_of(held_pages, request_ends)
    scores, page_max = page_scores(cache, queries, requests)
    onehot = requests[None, :] == jnp.arange(REQS, dtype=jnp.int32)[:, None]
    local_max = jnp.max(jnp.where(onehot[:, :, None, None, None], page_max[None], -1e30), axis=1)
    global_max = lax.pmax(local_max.astype(jnp.bfloat16), "pool").astype(local_max.dtype)
    totals, numerator = accumulate(scores, page_max, cache, requests, global_max)
    summed, numerator = lax.psum((totals, numerator), "pool")
    whole = (numerator / summed[..., None]).reshape(REQS, STEPS, QH * HD)
    result = lax.dynamic_slice_in_dim(whole, position * columns, columns, 2)
    return (cache, result.astype(jnp.bfloat16))


def solution(mesh):
    placed = (
        P(("groups", "pool"), None),
        P(("groups", "pool"), None, None),
        P(("groups", "pool"), None),
        P("groups", None, None),
        P("groups"),
        P("groups"),
    )
    slab = mesh.shape["pool"] == 16
    return jax.shard_map(
        local_slab if slab else local,
        mesh=mesh,
        in_specs=placed,
        out_specs=(P(("groups", "pool"), None, None), P("groups", None, "pool")),
        check_vma=False,
    )
```

```python
import functools
import jax
import jax.numpy as jnp
from jax import lax
from jax.experimental import pallas as pl
from jax.experimental.pallas import tpu as pltpu
from jax.sharding import PartitionSpec as P

QH = 64
KVH = 4
HD = 128
PAGE = 16
STEPS = 8
REQS = 16
KVW = 2 * KVH * HD
SPAN = 3
LOW = -1e30
VMEM_LIMIT = 48 * 1024 * 1024
F32 = jnp.float32
BF16 = jnp.bfloat16
I32 = jnp.int32


def decode_kernel(chunk, place, flags, blocks, anchors, deltas, scales, out, rows, staged, sems):
    step = pl.program_id(0)
    for head in range(2 * KVH):
        cols = slice(head * HD, (head + 1) * HD)
        scale = jnp.broadcast_to(scales[:, head : head + 1], (chunk, HD))
        anchor = anchors[:, cols].astype(F32)
        rows[head * PAGE * chunk : head * PAGE * chunk + chunk, :] = anchor
        for token in range(1, PAGE):
            start = (head * PAGE + token) * chunk
            rows[start : start + chunk, :] = anchor + scale * deltas[token - 1, :, cols].astype(F32)
    for page in range(chunk):
        picked = [
            rows[pl.ds(head * PAGE * chunk + page, PAGE, stride=chunk), :]
            for head in range(2 * KVH)
        ]
        staged[place[step * chunk + page]] = jnp.concatenate(picked, axis=1).astype(BF16)

    @pl.when(step == pl.num_programs(0) - 1)
    def flush():
        copies = []
        for owner in range(16):
            copy = pltpu.make_async_copy(
                staged.at[pl.ds(blocks[owner] * PAGE, PAGE)],
                out.at[pl.ds(owner * PAGE, PAGE)],
                sems.at[owner],
            )
            pl.when(flags[owner] > 0)(copy.start)
            copies.append(copy)
        for owner in range(16):
            pl.when(flags[owner] > 0)(copies[owner].wait)


def decode_sorted(place, flags, blocks, anchors, deltas, scales):
    number = anchors.shape[0]
    chunk = 16
    return pl.pallas_call(
        functools.partial(decode_kernel, chunk),
        grid_spec=pltpu.PrefetchScalarGridSpec(
            num_scalar_prefetch=3,
            grid=(number // chunk,),
            in_specs=[
                pl.BlockSpec((chunk, KVW), lambda i, *_: (i, 0)),
                pl.BlockSpec((PAGE - 1, chunk, KVW), lambda i, *_: (0, i, 0)),
                pl.BlockSpec((chunk, 2 * KVH), lambda i, *_: (i, 0)),
            ],
            out_specs=pl.BlockSpec(memory_space=pl.ANY),
            scratch_shapes=[
                pltpu.VMEM((2 * KVH * PAGE * chunk, HD), F32),
                pltpu.VMEM((number, PAGE, KVW), BF16),
                pltpu.SemaphoreType.DMA((16,)),
            ],
        ),
        out_shape=jax.ShapeDtypeStruct((16 * PAGE, PAGE, KVW), BF16),
        compiler_params=pltpu.CompilerParams(vmem_limit_bytes=VMEM_LIMIT),
        name="decode_sorted",
    )(place, flags, blocks, anchors, deltas, scales)


def attend_kernel(base, requests, queries, key_anchor, val_anchor, key_delta, val_delta, scales, out, keys, vals):
    head = pl.program_id(0)
    number = key_anchor.shape[0]
    lane = lax.broadcasted_iota(I32, scales.shape, 1)
    table = scales[...]
    key_scale = jnp.sum(jnp.where(lane == head, table, 0.0), axis=1, keepdims=True)
    val_scale = jnp.sum(jnp.where(lane == head + KVH, table, 0.0), axis=1, keepdims=True)
    for anchor, delta, scale, kept in (
        (key_anchor, key_delta, key_scale, keys),
        (val_anchor, val_delta, val_scale, vals),
    ):
        first = anchor[...]
        kept[0:number, :] = first
        wide = first.astype(F32)
        for token in range(1, PAGE):
            kept[token * number : (token + 1) * number, :] = (
                wide + scale * delta[token - 1].astype(F32)
            ).astype(BF16)
    token_request = jnp.concatenate([requests[...]] * PAGE, axis=1) - base[0]
    rows = STEPS * QH // KVH
    eye = lax.broadcasted_iota(I32, (rows, rows), 0) == lax.broadcasted_iota(I32, (rows, rows), 1)
    pieces = []
    for slot in range(SPAN):
        scores = lax.dot_general(
            queries[slot], keys[...], (((1,), (1,)), ((), ())), preferred_element_type=F32
        ) * HD ** (-0.5)
        inside = token_request == slot
        scores = jnp.where(inside, scores, LOW)
        top = jnp.max(scores, axis=1, keepdims=True)
        exponent = jnp.where(inside, jnp.exp(scores - top), 0.0)
        total = jnp.maximum(jnp.sum(exponent, axis=1, keepdims=True), 1e-30)
        numer = jnp.dot(exponent.astype(BF16), vals[...], preferred_element_type=F32)
        mean = (numer * (1.0 / total)).astype(BF16)
        quarter = rows // 4
        for part in range(4):
            out[part, slot * quarter : (slot + 1) * quarter, :] = mean[
                part * quarter : (part + 1) * quarter
            ]
        level = top + jnp.log(total)
        line = jnp.sum(jnp.where(eye, level, 0.0), axis=0, keepdims=True)
        for _ in range(3):
            piece = line.astype(BF16).astype(F32)
            pieces.append(piece)
            line = line - piece
    pieces.append(jnp.zeros((16 - len(pieces), rows), F32))
    stats = jnp.concatenate(pieces, axis=0).astype(BF16)
    for part in range(4):
        out[part, 96:112, :] = stats


def attend(base, requests, queries, anchors, deltas, scales):
    number = anchors.shape[0]
    rows = STEPS * QH // KVH
    return pl.pallas_call(
        attend_kernel,
        grid_spec=pltpu.PrefetchScalarGridSpec(
            num_scalar_prefetch=1,
            grid=(KVH,),
            in_specs=[
                pl.BlockSpec((1, number), lambda h, *_: (0, 0)),
                pl.BlockSpec((SPAN, rows, HD), lambda h, *_: (0, h, 0)),
                pl.BlockSpec((number, HD), lambda h, *_: (0, h)),
                pl.BlockSpec((number, HD), lambda h, *_: (0, h + KVH)),
                pl.BlockSpec((PAGE - 1, number, HD), lambda h, *_: (0, 0, h)),
                pl.BlockSpec((PAGE - 1, number, HD), lambda h, *_: (0, 0, h + KVH)),
                pl.BlockSpec((number, 2 * KVH), lambda h, *_: (0, 0)),
            ],
            out_specs=pl.BlockSpec((4, 112, HD), lambda h, *_: (h, 0, 0)),
            scratch_shapes=[
                pltpu.VMEM((PAGE * number, HD), BF16),
                pltpu.VMEM((PAGE * number, HD), BF16),
            ],
        ),
        out_shape=jax.ShapeDtypeStruct((16, 112, HD), BF16),
        compiler_params=pltpu.CompilerParams(vmem_limit_bytes=VMEM_LIMIT),
        cost_estimate=pl.CostEstimate(
            flops=SPAN * KVH * rows * number * PAGE * HD * 4,
            bytes_accessed=5 * 2**20,
            transcendentals=SPAN * KVH * rows * number * PAGE,
        ),
        name="attend",
    )(base, requests, queries, anchors, anchors, deltas, deltas, scales)


def merge_kernel(bases, part, parts, out, level, top, total, numer):
    quarter = 32
    row = lax.broadcasted_iota(I32, (quarter, HD), 0)
    lane = lax.broadcasted_iota(I32, (quarter, HD), 1)
    mine = lane == row + quarter * part[0]
    top[...] = jnp.full(top.shape, LOW, F32)
    total[...] = jnp.zeros(total.shape, F32)
    numer[...] = jnp.zeros(numer.shape, F32)
    for sender in range(16):
        stats = parts[sender, 96:112, :].astype(F32)
        for slot in range(SPAN):
            line = stats[3 * slot : 3 * slot + 1] + (
                stats[3 * slot + 1 : 3 * slot + 2] + stats[3 * slot + 2 : 3 * slot + 3]
            )
            column = jnp.sum(jnp.where(mine, line, 0.0), axis=1, keepdims=True)
            column = jnp.broadcast_to(column, (quarter, HD))
            level[sender * SPAN + slot] = column
            request = bases[sender] + slot
            top[request] = jnp.maximum(top[request], column)
    for sender in range(16):
        for slot in range(SPAN):
            request = bases[sender] + slot
            weight = jnp.exp(level[sender * SPAN + slot] - top[request])
            mean = parts[sender, slot * quarter : (slot + 1) * quarter, :].astype(F32)
            total[request] += weight
            numer[request] += weight * mean
    for request in range(REQS):
        result = (numer[request] / total[request]).astype(BF16)
        for group in range(4):
            out[request, :, group * HD : (group + 1) * HD] = result[
                group * STEPS : (group + 1) * STEPS
            ]


def merge(bases, part, parts):
    return pl.pallas_call(
        merge_kernel,
        grid_spec=pltpu.PrefetchScalarGridSpec(
            num_scalar_prefetch=2,
            grid=(1,),
            in_specs=[pl.BlockSpec((16, 112, HD), lambda i, *_: (0, 0, 0))],
            out_specs=pl.BlockSpec((REQS, STEPS, 4 * HD), lambda i, *_: (0, 0, 0)),
            scratch_shapes=[
                pltpu.VMEM((16 * SPAN, 32, HD), F32),
                pltpu.VMEM((REQS, 32, HD), F32),
                pltpu.VMEM((REQS, 32, HD), F32),
                pltpu.VMEM((REQS, 32, HD), F32),
            ],
        ),
        out_shape=jax.ShapeDtypeStruct((REQS, STEPS, 4 * HD), BF16),
        compiler_params=pltpu.CompilerParams(vmem_limit_bytes=VMEM_LIMIT),
        name="merge",
    )(bases, part, parts)


def assemble_kernel(flags, blocks, arrived, out, staged, in_sems, out_sems):
    reads, writes = [], []
    for sender in range(16):
        rows = pl.ds(blocks[sender] * PAGE, PAGE)
        source = arrived.at[pl.ds(sender * PAGE, PAGE)]
        reads.append(pltpu.make_async_copy(source, staged.at[rows], in_sems.at[sender]))
        writes.append(pltpu.make_async_copy(staged.at[rows], out.at[rows], out_sems.at[sender]))
    for sender in range(16):
        pl.when(flags[sender] > 0)(reads[sender].start)
    for sender in range(16):

        @pl.when(flags[sender] > 0)
        def forward():
            reads[sender].wait()
            writes[sender].start()

    for sender in range(16):
        pl.when(flags[sender] > 0)(writes[sender].wait)


def assemble(flags, blocks, arrived, number):
    return pl.pallas_call(
        assemble_kernel,
        grid_spec=pltpu.PrefetchScalarGridSpec(
            num_scalar_prefetch=2,
            grid=(1,),
            in_specs=[pl.BlockSpec(memory_space=pl.ANY)],
            out_specs=pl.BlockSpec(memory_space=pl.ANY),
            scratch_shapes=[
                pltpu.VMEM((number, PAGE, KVW), BF16),
                pltpu.SemaphoreType.DMA((16,)),
                pltpu.SemaphoreType.DMA((16,)),
            ],
        ),
        out_shape=jax.ShapeDtypeStruct((number, PAGE, KVW), BF16),
        compiler_params=pltpu.CompilerParams(vmem_limit_bytes=VMEM_LIMIT),
        name="assemble",
    )(flags, blocks, arrived)


ROUNDS = 9
LIMIT = 12
UNIT = 2
LAG = 2
HALF = PAGE // 2
FAR = 1e6


def plan_kernel(place, owners, out):
    chip = place[0]
    row = lax.broadcasted_iota(I32, (16, 128), 0)
    lanes = lax.broadcasted_iota(I32, (16, 128), 1)
    sender_of = lanes >> 3
    turn = (lanes & 7).astype(F32)
    table = owners[...]
    running = jnp.zeros((16, 1), F32)
    sends = []
    targets = jnp.zeros((16, 128), F32)
    for owner in range(16):
        flag = jnp.max(jnp.where(table == owner, 1.0, 0.0), axis=1, keepdims=True)
        targets += jnp.where(turn == running, flag * owner, 0.0)
        sends.append(flag)
        running = running + flag
    dest = jnp.sum(jnp.where(row == sender_of, targets, 0.0), axis=0, keepdims=True)
    hits = jnp.zeros((16, 128), F32)
    for owner in range(16):
        hits += sends[owner] * jnp.where(dest == owner, 1.0, 0.0)
    rank = jnp.sum(jnp.where(row < sender_of, hits, 0.0), axis=0, keepdims=True).astype(I32)
    dest = dest.astype(I32)
    lane = lax.broadcasted_iota(I32, (1, 128), 1)
    sender = lane >> 3
    from_z, from_x = sender >> 2, (sender >> 1) & 1
    to_z, to_x = dest >> 2, (dest >> 1) & 1
    crosses = (from_z >> 1) != (to_z >> 1)
    below = jnp.where(
        lax.broadcasted_iota(I32, (128, 128), 0) < lax.broadcasted_iota(I32, (128, 128), 1), 1.0, 0.0
    )
    line = from_x
    for side in range(2):
        leaving = crosses & ((from_z >> 1) == side)
        free = jnp.where(leaving & (from_x != to_x), 1.0, 0.0)
        fixed = jnp.where(leaving & (from_x == to_x), 1.0, 0.0)
        tilt = jnp.sum(fixed * (2 * from_x - 1).astype(F32), axis=1, keepdims=True)
        count = jnp.sum(free, axis=1, keepdims=True)
        share = jnp.clip(jnp.floor((tilt + count) * 0.5), 0.0, count)
        step = share / jnp.maximum(count, 1.0)
        index = jnp.dot(jnp.broadcast_to(free, (8, 128)), below, preferred_element_type=F32)[0:1]
        first = jnp.floor((index + 1.0) * step + 1e-3) > jnp.floor(index * step + 1e-3)
        line = jnp.where(free > 0.0, jnp.where(first, 0, 1), line)
    chips = lax.broadcasted_iota(I32, (8, 128), 0)
    mine = lax.broadcasted_iota(I32, (8, 1), 0) == chip

    def round_step(time, carry):
        at_z, at_x, ready, code, steps, needed = carry
        waits = crosses & ((at_z >> 1) == (from_z >> 1))
        turns = ((at_z == to_z) & (at_x != to_x)) | (waits & (line != at_x))
        along = jnp.logical_not(turns) & (at_z != to_z)
        left = jnp.abs(to_z - at_z) + jnp.where(at_x != to_x, 1, 0)
        key = ((8 - left) * 128 + lane).astype(F32)
        here = (at_z * 2 + at_x == chips) & (ready <= time)
        heading = jnp.where(turns, 2, jnp.where(along, jnp.where(to_z > at_z, 0, 1), 3))
        moved = jnp.zeros((1, 128), F32)
        landed = jnp.zeros((1, 128), F32)
        value = (code + 1).astype(F32)
        for port in range(3):
            keys = jnp.where(here & (heading == port), key, FAR)
            for unit in range(UNIT):
                least = jnp.min(keys, axis=1, keepdims=True)
                chosen = jnp.where((keys == least) & (keys < FAR), 1.0, 0.0)
                source = jnp.sum(chosen * value, axis=1, keepdims=True)
                source = jnp.sum(jnp.where(mine, source, 0.0), axis=0, keepdims=True)
                slot = 3 * UNIT * time + UNIT * port + unit
                steps = steps + jnp.where(lane == slot, source, 0.0)
                taken = jnp.sum(chosen, axis=0, keepdims=True)
                moved = moved + taken * (port + 1)
                landed = landed + taken * (slot + 16).astype(F32)
                keys = jnp.where(chosen > 0.0, FAR, keys)
        went = moved.astype(I32)
        at_z = at_z + jnp.where(went == 1, 1, 0) - jnp.where(went == 2, 1, 0)
        at_x = jnp.where(went == 3, 1 - at_x, at_x)
        ready = jnp.where(went > 0, time + LAG, ready)
        code = jnp.where(went > 0, landed.astype(I32), code)
        any_move = jnp.max(moved, axis=1, keepdims=True)
        needed = jnp.where(any_move > 0.0, (time + 1).astype(F32), needed)
        return at_z, at_x, ready, code, steps, needed

    start = (
        from_z,
        from_x,
        jnp.zeros((1, 128), I32),
        (sender & 1) * 8 + (lane & 7),
        jnp.zeros((1, 128), F32),
        jnp.zeros((1, 1), F32),
    )
    at_z, at_x, ready, code, steps, needed = lax.fori_loop(0, LIMIT, round_step, start)
    undone = jnp.where((at_z == to_z) & (at_x == to_x), 0.0, 1.0)
    undone = jnp.max(undone, axis=1, keepdims=True)
    needed = jnp.where(undone > 0.0, float(LIMIT + 1), needed)
    arrives = (dest >> 1) == chip
    slots = (dest & 1) * 8 + rank
    final = jnp.sum(
        jnp.where((row == slots) & arrives, (code + 1).astype(F32), 0.0), axis=1, keepdims=True
    )
    final = jnp.sum(jnp.where(row == lanes, final, 0.0), axis=0, keepdims=True)
    out[0:1, :] = steps.astype(I32)
    out[1:2, :] = final.astype(I32)
    out[2:3, :] = jnp.broadcast_to(needed, (1, 128)).astype(I32)
    out[3:8, :] = jnp.zeros((5, 128), I32)


def make_plan(place, page_owner):
    return pl.pallas_call(
        plan_kernel,
        grid_spec=pltpu.PrefetchScalarGridSpec(
            num_scalar_prefetch=1,
            grid=(1,),
            in_specs=[pl.BlockSpec((16, 128), lambda i, *_: (0, 0))],
            out_specs=pl.BlockSpec((8, 128), lambda i, *_: (0, 0)),
        ),
        out_shape=jax.ShapeDtypeStruct((8, 128), I32),
        name="make_plan",
    )(place, page_owner.reshape(16, 128))


def halves_kernel(chunk, order, place, anchors, deltas, scales, keep, give, rows, staged, sems):
    step = pl.program_id(0)
    for head in range(2 * KVH):
        cols = slice(head * HD, (head + 1) * HD)
        scale = jnp.broadcast_to(scales[:, head : head + 1], (chunk, HD))
        anchor = anchors[:, cols].astype(F32)
        rows[head * PAGE * chunk : head * PAGE * chunk + chunk, :] = anchor
        for token in range(1, PAGE):
            start = (head * PAGE + token) * chunk
            rows[start : start + chunk, :] = anchor + scale * deltas[token - 1, :, cols].astype(F32)
    core = place[1]
    for page in range(chunk):
        picked = [
            rows[pl.ds(head * PAGE * chunk + page, PAGE, stride=chunk), :]
            for head in range(2 * KVH)
        ]
        rank = order[step * chunk + page]
        half = (rank >> 3) & 1
        slot = (half ^ core) * 64 + (rank >> 4) * HALF + (rank & 7)
        staged[slot] = jnp.concatenate(picked, axis=1).astype(BF16)

    @pl.when(step == pl.num_programs(0) - 1)
    def flush():
        copies = [
            pltpu.make_async_copy(staged.at[pl.ds(64, 64)], give, sems.at[0]),
            pltpu.make_async_copy(staged.at[pl.ds(0, 64)], keep, sems.at[1]),
        ]
        for copy in copies:
            copy.start()
        for copy in copies:
            copy.wait()


def decode_halves(order, place, anchors, deltas, scales):
    number = anchors.shape[0]
    chunk = 16
    half = jax.ShapeDtypeStruct((number // 2, PAGE, KVW), BF16)
    return pl.pallas_call(
        functools.partial(halves_kernel, chunk),
        grid_spec=pltpu.PrefetchScalarGridSpec(
            num_scalar_prefetch=2,
            grid=(number // chunk,),
            in_specs=[
                pl.BlockSpec((chunk, KVW), lambda i, *_: (i, 0)),
                pl.BlockSpec((PAGE - 1, chunk, KVW), lambda i, *_: (0, i, 0)),
                pl.BlockSpec((chunk, 2 * KVH), lambda i, *_: (i, 0)),
            ],
            out_specs=[pl.BlockSpec(memory_space=pl.ANY)] * 2,
            scratch_shapes=[
                pltpu.VMEM((2 * KVH * PAGE * chunk, HD), F32),
                pltpu.VMEM((number, PAGE, KVW), BF16),
                pltpu.SemaphoreType.DMA((2,)),
            ],
        ),
        out_shape=(half, half),
        compiler_params=pltpu.CompilerParams(vmem_limit_bytes=VMEM_LIMIT),
        name="decode_halves",
    )(order, place, anchors, deltas, scales)


def fetch(code, core, own, landed, ports, target, sem):
    value = code - 1
    keep, got = own

    @pl.when((value >= 0) & (value < 16))
    def from_own():
        rows = pl.ds((value & 7) * HALF, HALF)

        @pl.when((value >> 3) == core)
        def kept():
            pltpu.make_async_copy(keep.at[rows], target, sem).start()

        @pl.when((value >> 3) != core)
        def gotten():
            pltpu.make_async_copy(got.at[rows], target, sem).start()

    for time, arrivals in enumerate(landed):
        offset = value - 16 - 3 * UNIT * time

        @pl.when((offset >= 0) & (offset < 3 * UNIT))
        def from_round():
            rows = pl.ds((offset % UNIT) * HALF, HALF)
            for port in ports:

                @pl.when((offset >= UNIT * port) & (offset < UNIT * (port + 1)))
                def from_port():
                    pltpu.make_async_copy(arrivals[port].at[rows], target, sem).start()


def settle(code, own, target, sem):
    @pl.when(code > 0)
    def wait():
        pltpu.make_async_copy(own[0].at[pl.ds(0, HALF)], target, sem).wait()


def unpack(refs):
    own, rest = refs[:2], refs[2:]
    return own, [rest[3 * i : 3 * i + 3] for i in range(len(rest) // 3)]


def pick_kernel(time, count, plan, place, *refs):
    own, landed = unpack(refs[: 2 + 3 * count])
    outs, sems = refs[2 + 3 * count : 5 + 3 * count], refs[-1]
    for phase in range(2):
        for port in range(3):
            ports = (0, 1) if port == 2 else (port, 2)
            for unit in range(UNIT):
                code = plan[0, 3 * UNIT * time + UNIT * port + unit]
                target = outs[port].at[pl.ds(unit * HALF, HALF)]
                sem = sems.at[UNIT * port + unit]
                if phase == 0:
                    fetch(code, place[1], own, landed, ports, target, sem)
                else:
                    settle(code, own, target, sem)


def pick(time, plan, place, own, landed):
    sources = list(own) + [array for arrivals in landed for array in arrivals]
    piece = jax.ShapeDtypeStruct((UNIT * HALF, PAGE, KVW), BF16)
    return pl.pallas_call(
        functools.partial(pick_kernel, time, len(landed)),
        grid_spec=pltpu.PrefetchScalarGridSpec(
            num_scalar_prefetch=2,
            grid=(1,),
            in_specs=[pl.BlockSpec(memory_space=pl.ANY)] * len(sources),
            out_specs=[pl.BlockSpec(piece.shape, lambda i, *_: (0, 0, 0))] * 3,
            scratch_shapes=[pltpu.SemaphoreType.DMA((3 * UNIT,))],
        ),
        out_shape=(piece,) * 3,
        compiler_params=pltpu.CompilerParams(vmem_limit_bytes=VMEM_LIMIT),
        name=f"pick_{time}",
    )(plan, place, *sources)


def gather_kernel(mode, count, plan, place, *refs):
    own, landed = unpack(refs[: 2 + 3 * count])
    out, staged, in_sems, out_sems = refs[2 + 3 * count :]
    core = place[1]
    half = core if mode == "own" else 1 - core
    codes = [plan[1, half * 8 + slot] for slot in range(8)]
    targets = [staged.at[pl.ds(slot * HALF, HALF)] for slot in range(8)]
    for slot in range(8):
        fetch(codes[slot], core, own, landed, (0, 1, 2), targets[slot], in_sems.at[slot])
    writes = []
    for slot in range(8):
        start = slot * PAGE + core * HALF if mode == "own" else slot * HALF
        writes.append(
            pltpu.make_async_copy(targets[slot], out.at[pl.ds(start, HALF)], out_sems.at[slot])
        )
        settle(codes[slot], own, targets[slot], in_sems.at[slot])
        writes[slot].start()
    for write in writes:
        write.wait()


def gather(mode, plan, place, own, landed):
    sources = list(own) + [array for arrivals in landed for array in arrivals]
    pages = 8 * PAGE if mode == "own" else 8 * HALF
    return pl.pallas_call(
        functools.partial(gather_kernel, mode, len(landed)),
        grid_spec=pltpu.PrefetchScalarGridSpec(
            num_scalar_prefetch=2,
            grid=(1,),
            in_specs=[pl.BlockSpec(memory_space=pl.ANY)] * len(sources),
            out_specs=pl.BlockSpec(memory_space=pl.ANY),
            scratch_shapes=[
                pltpu.VMEM((8 * HALF, PAGE, KVW), BF16),
                pltpu.SemaphoreType.DMA((8,)),
                pltpu.SemaphoreType.DMA((8,)),
            ],
        ),
        out_shape=jax.ShapeDtypeStruct((pages, PAGE, KVW), BF16),
        compiler_params=pltpu.CompilerParams(vmem_limit_bytes=VMEM_LIMIT),
        name=f"gather_{mode}",
    )(plan, place, *sources)


def fill_kernel(place, cache, other, out, staged, in_sems, out_sems):
    half = 1 - place[1]
    reads, writes = [], []
    for slot in range(8):
        rows = pl.ds(slot * HALF, HALF)
        reads.append(pltpu.make_async_copy(other.at[rows], staged.at[rows], in_sems.at[slot]))
        writes.append(
            pltpu.make_async_copy(
                staged.at[rows], out.at[pl.ds(slot * PAGE + half * HALF, HALF)], out_sems.at[slot]
            )
        )
    for read in reads:
        read.start()
    for read, write in zip(reads, writes):
        read.wait()
        write.start()
    for write in writes:
        write.wait()


def fill(place, cache, other):
    return pl.pallas_call(
        fill_kernel,
        grid_spec=pltpu.PrefetchScalarGridSpec(
            num_scalar_prefetch=1,
            grid=(1,),
            in_specs=[pl.BlockSpec(memory_space=pl.ANY)] * 2,
            out_specs=pl.BlockSpec(memory_space=pl.ANY),
            scratch_shapes=[
                pltpu.VMEM((8 * HALF, PAGE, KVW), BF16),
                pltpu.SemaphoreType.DMA((8,)),
                pltpu.SemaphoreType.DMA((8,)),
            ],
        ),
        out_shape=jax.ShapeDtypeStruct(cache.shape, cache.dtype),
        input_output_aliases={1: 0},
        compiler_params=pltpu.CompilerParams(vmem_limit_bytes=VMEM_LIMIT),
        name="fill",
    )(place, cache, other)


UP = tuple((i, i + 4) for i in range(12))
DOWN = tuple((i + 4, i) for i in range(12))
ACROSS = tuple((i, i ^ 2) for i in range(16))
TWIN = tuple((i, i ^ 1) for i in range(16))


def play(time, plan, place, own, landed):
    parts = pick(time, plan, place, own, landed[: max(0, time - LAG + 1)])
    return [lax.ppermute(part, "pool", pairs) for part, pairs in zip(parts, (UP, DOWN, ACROSS))]


def finish(plan, place, own, landed):
    other = lax.ppermute(gather("give", plan, place, own, landed), "pool", TWIN)
    return fill(place, gather("own", plan, place, own, landed), other)


def local_lanes(anchors, deltas, scales, queries, lengths, page_owner):
    position = lax.axis_index("pool")
    number = anchors.shape[0]
    by_token = jnp.transpose(deltas, (1, 0, 2))
    place = jnp.stack([position >> 1, position & 1]).astype(I32)
    owners = lax.dynamic_slice_in_dim(page_owner, position * number, number, 0)
    index = jnp.arange(number, dtype=I32)
    ahead = (owners[None, :] < owners[:, None]) | (
        (owners[None, :] == owners[:, None]) & (index[None, :] < index[:, None])
    )
    order = jnp.sum(ahead.astype(I32), axis=1)
    keep, give = decode_halves(order, place, anchors, by_token, scales)
    got = lax.ppermute(give, "pool", TWIN)
    plan = make_plan(place, page_owner)
    own = (keep, got)
    devices = jnp.arange(16, dtype=I32)
    ends = jnp.cumsum(lengths)
    landed = []
    for time in range(ROUNDS):
        landed.append(play(time, plan, place, own, landed))
    bases = jnp.sum((devices[:, None] * number >= ends[None, :]).astype(I32), axis=1)
    bases = jnp.minimum(bases, REQS - SPAN)
    base = lax.dynamic_slice_in_dim(bases, position, 1, 0)
    pages = position * number + index
    requests = jnp.sum((pages[:, None] >= ends[None, :]).astype(I32), axis=1)[None, :]
    near = lax.dynamic_slice_in_dim(queries, base[0], SPAN, 0)
    near = near.reshape(SPAN, STEPS, QH, HD).transpose(0, 2, 1, 3).reshape(SPAN, QH * STEPS, HD)
    parts = attend(base, requests, near, anchors, by_token, scales)
    swapped = lax.all_to_all(parts, "pool", split_axis=0, concat_axis=0, tiled=True)
    attention = merge(bases, (position % 4)[None].astype(I32), swapped)

    def in_time(landed):
        return finish(plan, place, own, landed)

    def late(landed):
        landed = list(landed)
        for time in range(ROUNDS, LIMIT):
            landed.append(play(time, plan, place, own, landed))
        return finish(plan, place, own, landed)

    def padded(landed):
        sent = jnp.any(owners[None, :] == devices[:, None], axis=1).astype(I32)
        slabs = decode_sorted(order, sent, jnp.cumsum(sent) - sent, anchors, by_token, scales)
        arrived = lax.all_to_all(slabs, "pool", split_axis=0, concat_axis=0, tiled=True)
        taken = jnp.any((page_owner == position).reshape(16, number), axis=1).astype(I32)
        return assemble(taken, jnp.cumsum(taken) - taken, arrived, number)

    needed = plan[2, 0]
    branch = (needed > ROUNDS).astype(I32) + (needed > LIMIT).astype(I32)
    cache = lax.switch(branch, (in_time, late, padded), landed)
    return (cache, attention)


def decode_pages(anchors, deltas, scales):
    block_scale = jnp.repeat(scales, HD, axis=1)
    rebuilt = anchors[:, None, :].astype(jnp.float32) + block_scale[:, None, :] * deltas.astype(
        jnp.float32
    )
    return jnp.concatenate([anchors[:, None, :], rebuilt.astype(jnp.bfloat16)], axis=1)


def page_scores(work_pages, queries, requests):
    number = work_pages.shape[0]
    key_rows = work_pages[:, :, : KVH * HD].reshape(number, PAGE, KVH, HD)
    picked = jnp.take(queries, requests, axis=0).reshape(number, STEPS, KVH, QH // KVH, HD)
    scores = jnp.einsum(
        "nskgd,ntkd->nskgt", picked, key_rows, preferred_element_type=jnp.float32
    ) * HD ** (-0.5)
    return (scores, jnp.max(scores, axis=4))


def accumulate(scores, page_max, work_pages, requests, shift_max):
    number = work_pages.shape[0]
    rows_out = shift_max.shape[0]
    block_size = min(32, number)
    blocks = number // block_size
    value_rows = work_pages[:, :, KVH * HD :].reshape(blocks, block_size, PAGE, KVH, HD)
    score_blocks = scores.reshape((blocks, block_size) + scores.shape[1:])
    max_blocks = page_max.reshape((blocks, block_size) + page_max.shape[1:])
    request_blocks = requests.reshape(blocks, block_size)

    def block_step(running, pieces):
        totals, numerator = running
        block_scores, block_max, block_values, block_requests = pieces
        exponent = jnp.exp(block_scores - block_max[..., None])
        weights = exponent.astype(jnp.bfloat16)
        page_out = jnp.einsum(
            "nskgt,ntkd->nskgd", weights, block_values, preferred_element_type=jnp.float32
        )
        factor = jnp.exp(block_max - jnp.take(shift_max, block_requests, axis=0))
        select = (block_requests[None, :] == jnp.arange(rows_out, dtype=jnp.int32)[:, None]).astype(
            jnp.float32
        )
        spread = select[:, :, None, None, None] * factor[None]
        totals = totals + jnp.sum(spread * jnp.sum(exponent, axis=4)[None], axis=1)
        numerator = numerator + jnp.einsum(
            "rnskg,nskgd->rskgd", spread, page_out, precision=lax.Precision.HIGHEST
        )
        return ((totals, numerator), None)

    start_totals = jnp.zeros(shift_max.shape, jnp.float32)
    start_numer = jnp.zeros(shift_max.shape + (HD,), jnp.float32)
    finals, ignored = lax.scan(
        block_step,
        (start_totals, start_numer),
        (score_blocks, max_blocks, value_rows, request_blocks),
    )
    return finals


def request_of(index, request_ends):
    return jnp.sum((index[:, None] >= request_ends[None, :]).astype(jnp.int32), axis=1)


def local(anchors, deltas, scales, queries, lengths, page_owner):
    devices = lax.axis_size("pool")
    position = lax.axis_index("pool")
    number = anchors.shape[0]
    capacity = max(2, 2 * number // devices)
    pages = decode_pages(anchors, deltas, scales)
    request_ends = jnp.cumsum(lengths)
    owners = lax.dynamic_slice_in_dim(page_owner, position * number, number, 0)
    marked = (owners[:, None] == jnp.arange(devices, dtype=jnp.int32)[None, :]).astype(jnp.int32)
    ranking = jnp.sum((jnp.cumsum(marked, axis=0) - 1) * marked, axis=1)
    slot_ids = owners * capacity + ranking
    matches = slot_ids[None, :] == jnp.arange(devices * capacity, dtype=jnp.int32)[:, None]
    sources = jnp.sum(jnp.where(matches, jnp.arange(number, dtype=jnp.int32)[None, :], 0), axis=1)
    outgoing = jnp.take(pages, sources, axis=0)
    arrived = lax.all_to_all(outgoing, "pool", split_axis=0, concat_axis=0, tiled=True)
    held_pages = jnp.nonzero(page_owner == position, size=number)[0].astype(jnp.int32)
    senders = held_pages // number
    before = jnp.sum((held_pages[None, :] < (senders * number)[:, None]).astype(jnp.int32), axis=1)
    row_ids = senders * capacity + jnp.arange(number, dtype=jnp.int32) - before
    cache = jnp.take(arrived, row_ids, axis=0)
    columns = QH * HD // devices
    requests = request_of(held_pages, request_ends)
    scores, page_max = page_scores(cache, queries, requests)
    onehot = requests[None, :] == jnp.arange(REQS, dtype=jnp.int32)[:, None]
    local_max = jnp.max(jnp.where(onehot[:, :, None, None, None], page_max[None], -1e30), axis=1)
    global_max = lax.pmax(local_max.astype(jnp.bfloat16), "pool").astype(local_max.dtype)
    totals, numerator = accumulate(scores, page_max, cache, requests, global_max)
    summed, numerator = lax.psum((totals, numerator), "pool")
    whole = (numerator / summed[..., None]).reshape(REQS, STEPS, QH * HD)
    result = lax.dynamic_slice_in_dim(whole, position * columns, columns, 2)
    return (cache, result.astype(jnp.bfloat16))


def solution(mesh):
    placed = (
        P(("groups", "pool"), None),
        P(("groups", "pool"), None, None),
        P(("groups", "pool"), None),
        P("groups", None, None),
        P("groups"),
        P("groups"),
    )
    lanes = mesh.shape["pool"] == 16
    return jax.shard_map(
        local_lanes if lanes else local,
        mesh=mesh,
        in_specs=placed,
        out_specs=(P(("groups", "pool"), None, None), P("groups", None, "pool")),
        check_vma=False,
    )
```

```python
import functools
import jax
import jax.numpy as jnp
from jax import lax
from jax.experimental import pallas as pl
from jax.experimental.pallas import tpu as pltpu
from jax.sharding import PartitionSpec as P

QH = 64
KVH = 4
HD = 128
PAGE = 16
STEPS = 8
REQS = 16
KVW = 2 * KVH * HD
SPAN = 3
LOW = -1e30
VMEM_LIMIT = 48 * 1024 * 1024
F32 = jnp.float32
BF16 = jnp.bfloat16
I32 = jnp.int32


def decode_kernel(chunk, place, flags, blocks, anchors, deltas, scales, out, rows, staged, sems):
    step = pl.program_id(0)
    for head in range(2 * KVH):
        cols = slice(head * HD, (head + 1) * HD)
        scale = jnp.broadcast_to(scales[:, head : head + 1], (chunk, HD))
        anchor = anchors[:, cols].astype(F32)
        rows[head * PAGE * chunk : head * PAGE * chunk + chunk, :] = anchor
        for token in range(1, PAGE):
            start = (head * PAGE + token) * chunk
            rows[start : start + chunk, :] = anchor + scale * deltas[token - 1, :, cols].astype(F32)
    for page in range(chunk):
        picked = [
            rows[pl.ds(head * PAGE * chunk + page, PAGE, stride=chunk), :]
            for head in range(2 * KVH)
        ]
        staged[place[step * chunk + page]] = jnp.concatenate(picked, axis=1).astype(BF16)

    @pl.when(step == pl.num_programs(0) - 1)
    def flush():
        copies = []
        for owner in range(16):
            copy = pltpu.make_async_copy(
                staged.at[pl.ds(blocks[owner] * PAGE, PAGE)],
                out.at[pl.ds(owner * PAGE, PAGE)],
                sems.at[owner],
            )
            pl.when(flags[owner] > 0)(copy.start)
            copies.append(copy)
        for owner in range(16):
            pl.when(flags[owner] > 0)(copies[owner].wait)


def decode_sorted(place, flags, blocks, anchors, deltas, scales):
    number = anchors.shape[0]
    chunk = 16
    return pl.pallas_call(
        functools.partial(decode_kernel, chunk),
        grid_spec=pltpu.PrefetchScalarGridSpec(
            num_scalar_prefetch=3,
            grid=(number // chunk,),
            in_specs=[
                pl.BlockSpec((chunk, KVW), lambda i, *_: (i, 0)),
                pl.BlockSpec((PAGE - 1, chunk, KVW), lambda i, *_: (0, i, 0)),
                pl.BlockSpec((chunk, 2 * KVH), lambda i, *_: (i, 0)),
            ],
            out_specs=pl.BlockSpec(memory_space=pl.ANY),
            scratch_shapes=[
                pltpu.VMEM((2 * KVH * PAGE * chunk, HD), F32),
                pltpu.VMEM((number, PAGE, KVW), BF16),
                pltpu.SemaphoreType.DMA((16,)),
            ],
        ),
        out_shape=jax.ShapeDtypeStruct((16 * PAGE, PAGE, KVW), BF16),
        compiler_params=pltpu.CompilerParams(vmem_limit_bytes=VMEM_LIMIT),
        name="decode_sorted",
    )(place, flags, blocks, anchors, deltas, scales)


def attend_kernel(plan, requests, first, second, third, key_anchor, val_anchor, key_delta, val_delta, scales, out, keys, vals):
    head = pl.program_id(0)
    number = key_anchor.shape[0]
    lane = lax.broadcasted_iota(I32, scales.shape, 1)
    table = scales[...]
    key_scale = jnp.sum(jnp.where(lane == head, table, 0.0), axis=1, keepdims=True)
    val_scale = jnp.sum(jnp.where(lane == head + KVH, table, 0.0), axis=1, keepdims=True)
    for anchor, delta, scale, kept in (
        (key_anchor, key_delta, key_scale, keys),
        (val_anchor, val_delta, val_scale, vals),
    ):
        kept[0:number, :] = anchor[...]
        wide = anchor[...].astype(F32)
        for token in range(1, PAGE):
            kept[token * number : (token + 1) * number, :] = (
                wide + scale * delta[token - 1].astype(F32)
            ).astype(BF16)
    token_request = jnp.concatenate([requests[4:5, :]] * PAGE, axis=1) - plan[5, 0]
    rows = STEPS * QH // KVH
    eye = lax.broadcasted_iota(I32, (rows, rows), 0) == lax.broadcasted_iota(I32, (rows, rows), 1)
    pieces = []
    for slot, queries in enumerate((first, second, third)):
        wide = queries[0].astype(F32)
        picked = jnp.concatenate(
            [wide[:, group * HD : (group + 1) * HD] for group in range(QH // KVH)], axis=0
        ).astype(BF16)
        scores = lax.dot_general(
            picked, keys[...], (((1,), (1,)), ((), ())), preferred_element_type=F32
        ) * HD ** (-0.5)
        inside = token_request == slot
        scores = jnp.where(inside, scores, LOW)
        top = jnp.max(scores, axis=1, keepdims=True)
        exponent = jnp.where(inside, jnp.exp(scores - top), 0.0)
        total = jnp.maximum(jnp.sum(exponent, axis=1, keepdims=True), 1e-30)
        numer = jnp.dot(exponent.astype(BF16), vals[...], preferred_element_type=F32)
        mean = (numer * (1.0 / total)).astype(BF16)
        quarter = rows // 4
        for part in range(4):
            out[part, slot * quarter : (slot + 1) * quarter, :] = mean[
                part * quarter : (part + 1) * quarter
            ]
        level = top + jnp.log(total)
        line = jnp.sum(jnp.where(eye, level, 0.0), axis=0, keepdims=True)
        for _ in range(3):
            piece = line.astype(BF16).astype(F32)
            pieces.append(piece)
            line = line - piece
    pieces.append(jnp.zeros((16 - len(pieces), rows), F32))
    stats = jnp.concatenate(pieces, axis=0).astype(BF16)
    for part in range(4):
        out[part, 96:112, :] = stats


def attend(plan, queries, anchors, deltas, scales):
    number = anchors.shape[0]
    rows = STEPS * QH // KVH
    return pl.pallas_call(
        attend_kernel,
        grid_spec=pltpu.PrefetchScalarGridSpec(
            num_scalar_prefetch=1,
            grid=(KVH,),
            in_specs=[
                pl.BlockSpec((8, number), lambda h, *_: (0, 0)),
                *[
                    pl.BlockSpec((1, STEPS, rows * HD // STEPS), lambda h, p, k=k: (p[5, 0] + k, 0, h))
                    for k in range(SPAN)
                ],
                pl.BlockSpec((number, HD), lambda h, *_: (0, h)),
                pl.BlockSpec((number, HD), lambda h, *_: (0, h + KVH)),
                pl.BlockSpec((PAGE - 1, number, HD), lambda h, *_: (0, 0, h)),
                pl.BlockSpec((PAGE - 1, number, HD), lambda h, *_: (0, 0, h + KVH)),
                pl.BlockSpec((number, 2 * KVH), lambda h, *_: (0, 0)),
            ],
            out_specs=pl.BlockSpec((4, 112, HD), lambda h, *_: (h, 0, 0)),
            scratch_shapes=[
                pltpu.VMEM((PAGE * number, HD), BF16),
                pltpu.VMEM((PAGE * number, HD), BF16),
            ],
        ),
        out_shape=jax.ShapeDtypeStruct((16, 112, HD), BF16),
        compiler_params=pltpu.CompilerParams(vmem_limit_bytes=VMEM_LIMIT),
        cost_estimate=pl.CostEstimate(
            flops=SPAN * KVH * rows * number * PAGE * HD * 4,
            bytes_accessed=5 * 2**20,
            transcendentals=SPAN * KVH * rows * number * PAGE,
        ),
        name="attend",
    )(plan, plan, queries, queries, queries, anchors, anchors, deltas, deltas, scales)


def merge_kernel(plan, place, parts, out, level, top, total, numer):
    quarter = 32
    row = lax.broadcasted_iota(I32, (quarter, HD), 0)
    lane = lax.broadcasted_iota(I32, (quarter, HD), 1)
    mine = lane == row + quarter * ((place[0] & 1) * 2 + place[1])
    top[...] = jnp.full(top.shape, LOW, F32)
    total[...] = jnp.zeros(total.shape, F32)
    numer[...] = jnp.zeros(numer.shape, F32)
    for sender in range(16):
        stats = parts[sender, 96:112, :].astype(F32)
        for slot in range(SPAN):
            line = stats[3 * slot : 3 * slot + 1] + (
                stats[3 * slot + 1 : 3 * slot + 2] + stats[3 * slot + 2 : 3 * slot + 3]
            )
            column = jnp.sum(jnp.where(mine, line, 0.0), axis=1, keepdims=True)
            column = jnp.broadcast_to(column, (quarter, HD))
            level[sender * SPAN + slot] = column
            request = plan[3, sender] + slot
            top[request] = jnp.maximum(top[request], column)
    for sender in range(16):
        for slot in range(SPAN):
            request = plan[3, sender] + slot
            weight = jnp.exp(level[sender * SPAN + slot] - top[request])
            mean = parts[sender, slot * quarter : (slot + 1) * quarter, :].astype(F32)
            total[request] += weight
            numer[request] += weight * mean
    for request in range(REQS):
        result = (numer[request] / total[request]).astype(BF16)
        for group in range(4):
            out[request, :, group * HD : (group + 1) * HD] = result[
                group * STEPS : (group + 1) * STEPS
            ]


def merge(plan, place, parts):
    return pl.pallas_call(
        merge_kernel,
        grid_spec=pltpu.PrefetchScalarGridSpec(
            num_scalar_prefetch=2,
            grid=(1,),
            in_specs=[pl.BlockSpec((16, 112, HD), lambda i, *_: (0, 0, 0))],
            out_specs=pl.BlockSpec((REQS, STEPS, 4 * HD), lambda i, *_: (0, 0, 0)),
            scratch_shapes=[
                pltpu.VMEM((16 * SPAN, 32, HD), F32),
                pltpu.VMEM((REQS, 32, HD), F32),
                pltpu.VMEM((REQS, 32, HD), F32),
                pltpu.VMEM((REQS, 32, HD), F32),
            ],
        ),
        out_shape=jax.ShapeDtypeStruct((REQS, STEPS, 4 * HD), BF16),
        compiler_params=pltpu.CompilerParams(vmem_limit_bytes=VMEM_LIMIT),
        name="merge",
    )(plan, place, parts)


def assemble_kernel(flags, blocks, arrived, out, staged, in_sems, out_sems):
    reads, writes = [], []
    for sender in range(16):
        rows = pl.ds(blocks[sender] * PAGE, PAGE)
        source = arrived.at[pl.ds(sender * PAGE, PAGE)]
        reads.append(pltpu.make_async_copy(source, staged.at[rows], in_sems.at[sender]))
        writes.append(pltpu.make_async_copy(staged.at[rows], out.at[rows], out_sems.at[sender]))
    for sender in range(16):
        pl.when(flags[sender] > 0)(reads[sender].start)
    for sender in range(16):

        @pl.when(flags[sender] > 0)
        def forward():
            reads[sender].wait()
            writes[sender].start()

    for sender in range(16):
        pl.when(flags[sender] > 0)(writes[sender].wait)


def assemble(flags, blocks, arrived, number):
    return pl.pallas_call(
        assemble_kernel,
        grid_spec=pltpu.PrefetchScalarGridSpec(
            num_scalar_prefetch=2,
            grid=(1,),
            in_specs=[pl.BlockSpec(memory_space=pl.ANY)],
            out_specs=pl.BlockSpec(memory_space=pl.ANY),
            scratch_shapes=[
                pltpu.VMEM((number, PAGE, KVW), BF16),
                pltpu.SemaphoreType.DMA((16,)),
                pltpu.SemaphoreType.DMA((16,)),
            ],
        ),
        out_shape=jax.ShapeDtypeStruct((number, PAGE, KVW), BF16),
        compiler_params=pltpu.CompilerParams(vmem_limit_bytes=VMEM_LIMIT),
        name="assemble",
    )(flags, blocks, arrived)


ROUNDS = 9
LIMIT = 12
UNIT = 2
LAG = 2
HALF = PAGE // 2
FAR = 1e6


def plan_kernel(place, lengths, owners, out):
    chip = place[0]
    row = lax.broadcasted_iota(I32, (16, 128), 0)
    lanes = lax.broadcasted_iota(I32, (16, 128), 1)
    sender_of = lanes >> 3
    turn = (lanes & 7).astype(F32)
    table = owners[...]
    running = jnp.zeros((16, 1), F32)
    sends = []
    targets = jnp.zeros((16, 128), F32)
    for owner in range(16):
        flag = jnp.max(jnp.where(table == owner, 1.0, 0.0), axis=1, keepdims=True)
        targets += jnp.where(turn == running, flag * owner, 0.0)
        sends.append(flag)
        running = running + flag
    dest = jnp.sum(jnp.where(row == sender_of, targets, 0.0), axis=0, keepdims=True)
    hits = jnp.zeros((16, 128), F32)
    for owner in range(16):
        hits += sends[owner] * jnp.where(dest == owner, 1.0, 0.0)
    rank = jnp.sum(jnp.where(row < sender_of, hits, 0.0), axis=0, keepdims=True).astype(I32)
    dest = dest.astype(I32)
    lane = lax.broadcasted_iota(I32, (1, 128), 1)
    sender = lane >> 3
    from_z, from_x = sender >> 2, (sender >> 1) & 1
    to_z, to_x = dest >> 2, (dest >> 1) & 1
    crosses = (from_z >> 1) != (to_z >> 1)
    below = jnp.where(
        lax.broadcasted_iota(I32, (128, 128), 0) < lax.broadcasted_iota(I32, (128, 128), 1), 1.0, 0.0
    )
    line = from_x
    for side in range(2):
        leaving = crosses & ((from_z >> 1) == side)
        free = jnp.where(leaving & (from_x != to_x), 1.0, 0.0)
        fixed = jnp.where(leaving & (from_x == to_x), 1.0, 0.0)
        tilt = jnp.sum(fixed * (2 * from_x - 1).astype(F32), axis=1, keepdims=True)
        count = jnp.sum(free, axis=1, keepdims=True)
        share = jnp.clip(jnp.floor((tilt + count) * 0.5), 0.0, count)
        step = share / jnp.maximum(count, 1.0)
        index = jnp.dot(jnp.broadcast_to(free, (8, 128)), below, preferred_element_type=F32)[0:1]
        first = jnp.floor((index + 1.0) * step + 1e-3) > jnp.floor(index * step + 1e-3)
        line = jnp.where(free > 0.0, jnp.where(first, 0, 1), line)
    chips = lax.broadcasted_iota(I32, (8, 128), 0)
    mine = lax.broadcasted_iota(I32, (8, 1), 0) == chip

    def round_step(time, carry):
        at_z, at_x, ready, code, steps, needed = carry
        waits = crosses & ((at_z >> 1) == (from_z >> 1))
        turns = ((at_z == to_z) & (at_x != to_x)) | (waits & (line != at_x))
        along = jnp.logical_not(turns) & (at_z != to_z)
        left = jnp.abs(to_z - at_z) + jnp.where(at_x != to_x, 1, 0)
        key = ((8 - left) * 128 + lane).astype(F32)
        here = (at_z * 2 + at_x == chips) & (ready <= time)
        heading = jnp.where(turns, 2, jnp.where(along, jnp.where(to_z > at_z, 0, 1), 3))
        moved = jnp.zeros((1, 128), F32)
        landed = jnp.zeros((1, 128), F32)
        value = (code + 1).astype(F32)
        for port in range(3):
            keys = jnp.where(here & (heading == port), key, FAR)
            for unit in range(UNIT):
                least = jnp.min(keys, axis=1, keepdims=True)
                chosen = jnp.where((keys == least) & (keys < FAR), 1.0, 0.0)
                source = jnp.sum(chosen * value, axis=1, keepdims=True)
                source = jnp.sum(jnp.where(mine, source, 0.0), axis=0, keepdims=True)
                slot = 3 * UNIT * time + UNIT * port + unit
                steps = steps + jnp.where(lane == slot, source, 0.0)
                taken = jnp.sum(chosen, axis=0, keepdims=True)
                moved = moved + taken * (port + 1)
                landed = landed + taken * (slot + 16).astype(F32)
                keys = jnp.where(chosen > 0.0, FAR, keys)
        went = moved.astype(I32)
        at_z = at_z + jnp.where(went == 1, 1, 0) - jnp.where(went == 2, 1, 0)
        at_x = jnp.where(went == 3, 1 - at_x, at_x)
        ready = jnp.where(went > 0, time + LAG, ready)
        code = jnp.where(went > 0, landed.astype(I32), code)
        any_move = jnp.max(moved, axis=1, keepdims=True)
        needed = jnp.where(any_move > 0.0, (time + 1).astype(F32), needed)
        return at_z, at_x, ready, code, steps, needed

    start = (
        from_z,
        from_x,
        jnp.zeros((1, 128), I32),
        (sender & 1) * 8 + (lane & 7),
        jnp.zeros((1, 128), F32),
        jnp.zeros((1, 1), F32),
    )
    at_z, at_x, ready, code, steps, needed = lax.fori_loop(0, LIMIT, round_step, start)
    undone = jnp.where((at_z == to_z) & (at_x == to_x), 0.0, 1.0)
    undone = jnp.max(undone, axis=1, keepdims=True)
    needed = jnp.where(undone > 0.0, float(LIMIT + 1), needed)
    arrives = (dest >> 1) == chip
    slots = (dest & 1) * 8 + rank
    final = jnp.sum(
        jnp.where((row == slots) & arrives, (code + 1).astype(F32), 0.0), axis=1, keepdims=True
    )
    final = jnp.sum(jnp.where(row == lanes, final, 0.0), axis=0, keepdims=True)
    out[0:1, :] = steps.astype(I32)
    out[1:2, :] = final.astype(I32)
    out[2:3, :] = jnp.broadcast_to(needed, (1, 128)).astype(I32)
    page = (2 * chip + place[1]) * 128 + lane
    requests = jnp.zeros((1, 128), I32)
    bases = jnp.zeros((1, 128), I32)
    end = 0
    for request in range(REQS):
        end = end + lengths[request]
        requests = requests + jnp.where(page >= end, 1, 0)
        bases = bases + jnp.where(lane * 128 >= end, 1, 0)
    bases = jnp.minimum(bases, REQS - SPAN)
    base = jnp.sum(jnp.where(lane == 2 * chip + place[1], bases, 0).astype(F32), axis=1, keepdims=True)
    out[3:4, :] = bases
    out[4:5, :] = requests
    out[5:6, :] = jnp.broadcast_to(base, (1, 128)).astype(I32)
    out[6:8, :] = jnp.zeros((2, 128), I32)


def make_plan(place, lengths, page_owner):
    return pl.pallas_call(
        plan_kernel,
        grid_spec=pltpu.PrefetchScalarGridSpec(
            num_scalar_prefetch=2,
            grid=(1,),
            in_specs=[pl.BlockSpec((16, 128), lambda i, *_: (0, 0))],
            out_specs=pl.BlockSpec((8, 128), lambda i, *_: (0, 0)),
        ),
        out_shape=jax.ShapeDtypeStruct((8, 128), I32),
        name="make_plan",
    )(place, lengths, page_owner.reshape(16, 128))


def halves_kernel(order, place, anchors, deltas, scales, keep, give, swap, rows, staged, sems):
    step = pl.program_id(0)
    count = PAGE * PAGE

    @pl.when(step == 0)
    def build():
        row = lax.broadcasted_iota(I32, (count, count), 0)
        lane = lax.broadcasted_iota(I32, (count, count), 1)
        swap[...] = jnp.where(lane == (row & 15) * PAGE + (row >> 4), 1.0, 0.0).astype(BF16)

    core = place[1]
    for part in range(anchors.shape[0] // PAGE):
        pages = slice(part * PAGE, (part + 1) * PAGE)
        for head in range(2 * KVH):
            cols = slice(head * HD, (head + 1) * HD)
            scale = jnp.broadcast_to(scales[pages, head : head + 1], (PAGE, HD))
            first = anchors[pages, cols]
            anchor = first.astype(F32)
            rows[0:PAGE, cols] = first
            for token in range(1, PAGE):
                rebuilt = anchor + scale * deltas[token - 1, pages, cols].astype(F32)
                rows[token * PAGE : (token + 1) * PAGE, cols] = rebuilt.astype(BF16)
        turned = jnp.dot(swap[...], rows[...], preferred_element_type=F32).astype(BF16)
        for page in range(PAGE):
            rank = order[step * anchors.shape[0] + part * PAGE + page]
            half = (rank >> 3) & 1
            slot = (half ^ core) * 64 + (rank >> 4) * HALF + (rank & 7)
            staged[slot] = turned[page * PAGE : (page + 1) * PAGE]

    @pl.when(step == pl.num_programs(0) - 1)
    def flush():
        copies = [
            pltpu.make_async_copy(staged.at[pl.ds(64, 64)], give, sems.at[0]),
            pltpu.make_async_copy(staged.at[pl.ds(0, 64)], keep, sems.at[1]),
        ]
        for copy in copies:
            copy.start()
        for copy in copies:
            copy.wait()


def decode_halves(order, place, anchors, deltas, scales):
    number = anchors.shape[0]
    chunk = 2 * PAGE
    half = jax.ShapeDtypeStruct((number // 2, PAGE, KVW), BF16)
    return pl.pallas_call(
        halves_kernel,
        grid_spec=pltpu.PrefetchScalarGridSpec(
            num_scalar_prefetch=2,
            grid=(number // chunk,),
            in_specs=[
                pl.BlockSpec((chunk, KVW), lambda i, *_: (i, 0)),
                pl.BlockSpec((PAGE - 1, chunk, KVW), lambda i, *_: (0, i, 0)),
                pl.BlockSpec((chunk, 2 * KVH), lambda i, *_: (i, 0)),
            ],
            out_specs=[pl.BlockSpec(memory_space=pl.ANY)] * 2,
            scratch_shapes=[
                pltpu.VMEM((PAGE * PAGE, PAGE * PAGE), BF16),
                pltpu.VMEM((PAGE * PAGE, KVW), BF16),
                pltpu.VMEM((number, PAGE, KVW), BF16),
                pltpu.SemaphoreType.DMA((2,)),
            ],
        ),
        out_shape=(half, half),
        compiler_params=pltpu.CompilerParams(vmem_limit_bytes=VMEM_LIMIT),
        name="decode_halves",
    )(order, place, anchors, deltas, scales)


def fetch(code, core, own, landed, ports, target, sem):
    value = code - 1
    keep, got = own

    @pl.when((value >= 0) & (value < 16))
    def from_own():
        rows = pl.ds((value & 7) * HALF, HALF)

        @pl.when((value >> 3) == core)
        def kept():
            pltpu.make_async_copy(keep.at[rows], target, sem).start()

        @pl.when((value >> 3) != core)
        def gotten():
            pltpu.make_async_copy(got.at[rows], target, sem).start()

    for time, arrivals in enumerate(landed):
        offset = value - 16 - 3 * UNIT * time

        @pl.when((offset >= 0) & (offset < 3 * UNIT))
        def from_round():
            rows = pl.ds((offset % UNIT) * HALF, HALF)
            for port in ports:

                @pl.when((offset >= UNIT * port) & (offset < UNIT * (port + 1)))
                def from_port():
                    pltpu.make_async_copy(arrivals[port].at[rows], target, sem).start()


def settle(code, own, target, sem):
    @pl.when(code > 0)
    def wait():
        pltpu.make_async_copy(own[0].at[pl.ds(0, HALF)], target, sem).wait()


def unpack(refs):
    own, rest = refs[:2], refs[2:]
    return own, [rest[3 * i : 3 * i + 3] for i in range(len(rest) // 3)]


def pick_kernel(time, count, plan, place, *refs):
    own, landed = unpack(refs[: 2 + 3 * count])
    outs, sems = refs[-4:-1], refs[-1]
    for phase in range(2):
        for port in range(3):
            ports = (0, 1) if port == 2 else (port, 2)
            for unit in range(UNIT):
                code = plan[0, 3 * UNIT * time + UNIT * port + unit]
                target = outs[port].at[pl.ds(unit * HALF, HALF)]
                sem = sems.at[UNIT * port + unit]
                if phase == 0:
                    fetch(code, place[1], own, landed, ports, target, sem)
                else:
                    settle(code, own, target, sem)


def pick(time, plan, place, own, landed, after):
    landed = landed[: max(0, time - LAG + 1)]
    sources = list(own) + [array for arrivals in landed for array in arrivals] + [after]
    piece = jax.ShapeDtypeStruct((UNIT * HALF, PAGE, KVW), BF16)
    return pl.pallas_call(
        functools.partial(pick_kernel, time, len(landed)),
        grid_spec=pltpu.PrefetchScalarGridSpec(
            num_scalar_prefetch=2,
            grid=(1,),
            in_specs=[pl.BlockSpec(memory_space=pl.ANY)] * len(sources),
            out_specs=[pl.BlockSpec(piece.shape, lambda i, *_: (0, 0, 0))] * 3,
            scratch_shapes=[pltpu.SemaphoreType.DMA((3 * UNIT,))],
        ),
        out_shape=(piece,) * 3,
        compiler_params=pltpu.CompilerParams(vmem_limit_bytes=VMEM_LIMIT),
        name=f"pick_{time}",
    )(plan, place, *sources)


def give_kernel(count, plan, place, *refs):
    own, landed = unpack(refs[: 2 + 3 * count])
    out, sems = refs[2 + 3 * count :]
    core = place[1]
    codes = [plan[1, (1 - core) * 8 + slot] for slot in range(8)]
    targets = [out.at[pl.ds(slot * HALF, HALF)] for slot in range(8)]
    for slot in range(8):
        fetch(codes[slot], core, own, landed, (0, 1, 2), targets[slot], sems.at[slot])
    for slot in range(8):
        settle(codes[slot], own, targets[slot], sems.at[slot])


def gather_give(plan, place, own, landed):
    sources = list(own) + [array for arrivals in landed for array in arrivals]
    shape = (8 * HALF, PAGE, KVW)
    return pl.pallas_call(
        functools.partial(give_kernel, len(landed)),
        grid_spec=pltpu.PrefetchScalarGridSpec(
            num_scalar_prefetch=2,
            grid=(1,),
            in_specs=[pl.BlockSpec(memory_space=pl.ANY)] * len(sources),
            out_specs=pl.BlockSpec(shape, lambda i, *_: (0, 0, 0)),
            scratch_shapes=[pltpu.SemaphoreType.DMA((8,))],
        ),
        out_shape=jax.ShapeDtypeStruct(shape, BF16),
        compiler_params=pltpu.CompilerParams(vmem_limit_bytes=VMEM_LIMIT),
        name="gather_give",
    )(plan, place, *sources)


def own_kernel(count, plan, place, *refs):
    own, landed = unpack(refs[: 2 + 3 * count])
    out, staged, in_sems, out_sems = refs[2 + 3 * count :]
    core = place[1]
    codes = [plan[1, core * 8 + slot] for slot in range(8)]
    targets = [staged.at[pl.ds(slot * HALF, HALF)] for slot in range(8)]
    for slot in range(8):
        fetch(codes[slot], core, own, landed, (0, 1, 2), targets[slot], in_sems.at[slot])
    writes = []
    for slot in range(8):
        start = slot * PAGE + core * HALF
        writes.append(
            pltpu.make_async_copy(targets[slot], out.at[pl.ds(start, HALF)], out_sems.at[slot])
        )
        settle(codes[slot], own, targets[slot], in_sems.at[slot])
        writes[slot].start()
    for write in writes:
        write.wait()


def gather_own(plan, place, own, landed):
    sources = list(own) + [array for arrivals in landed for array in arrivals]
    return pl.pallas_call(
        functools.partial(own_kernel, len(landed)),
        grid_spec=pltpu.PrefetchScalarGridSpec(
            num_scalar_prefetch=2,
            grid=(1,),
            in_specs=[pl.BlockSpec(memory_space=pl.ANY)] * len(sources),
            out_specs=pl.BlockSpec(memory_space=pl.ANY),
            scratch_shapes=[
                pltpu.VMEM((8 * HALF, PAGE, KVW), BF16),
                pltpu.SemaphoreType.DMA((8,)),
                pltpu.SemaphoreType.DMA((8,)),
            ],
        ),
        out_shape=jax.ShapeDtypeStruct((8 * PAGE, PAGE, KVW), BF16),
        compiler_params=pltpu.CompilerParams(vmem_limit_bytes=VMEM_LIMIT),
        name="gather_own",
    )(plan, place, *sources)


def fill_kernel(place, cache, other, out, staged, in_sems, out_sems):
    half = 1 - place[1]
    reads, writes = [], []
    for slot in range(8):
        rows = pl.ds(slot * HALF, HALF)
        reads.append(pltpu.make_async_copy(other.at[rows], staged.at[rows], in_sems.at[slot]))
        writes.append(
            pltpu.make_async_copy(
                staged.at[rows], out.at[pl.ds(slot * PAGE + half * HALF, HALF)], out_sems.at[slot]
            )
        )
    for read in reads:
        read.start()
    for read, write in zip(reads, writes):
        read.wait()
        write.start()
    for write in writes:
        write.wait()


def fill(place, cache, other):
    return pl.pallas_call(
        fill_kernel,
        grid_spec=pltpu.PrefetchScalarGridSpec(
            num_scalar_prefetch=1,
            grid=(1,),
            in_specs=[pl.BlockSpec(memory_space=pl.ANY)] * 2,
            out_specs=pl.BlockSpec(memory_space=pl.ANY),
            scratch_shapes=[
                pltpu.VMEM((8 * HALF, PAGE, KVW), BF16),
                pltpu.SemaphoreType.DMA((8,)),
                pltpu.SemaphoreType.DMA((8,)),
            ],
        ),
        out_shape=jax.ShapeDtypeStruct(cache.shape, cache.dtype),
        input_output_aliases={1: 0},
        compiler_params=pltpu.CompilerParams(vmem_limit_bytes=VMEM_LIMIT),
        name="fill",
    )(place, cache, other)


UP = tuple((i, i + 4) for i in range(12))
DOWN = tuple((i + 4, i) for i in range(12))
ACROSS = tuple((i, i ^ 2) for i in range(16))
TWIN = tuple((i, i ^ 1) for i in range(16))


def ship(parts):
    return [lax.ppermute(part, "pool", pairs) for part, pairs in zip(parts, (UP, DOWN, ACROSS))]


def finish(plan, place, own, landed):
    other = lax.ppermute(gather_give(plan, place, own, landed), "pool", TWIN)
    return fill(place, gather_own(plan, place, own, landed), other)


def local_lanes(anchors, deltas, scales, queries, lengths, page_owner):
    position = lax.axis_index("pool")
    number = anchors.shape[0]
    by_token = jnp.transpose(deltas, (1, 0, 2))
    place = jnp.stack([position >> 1, position & 1]).astype(I32)
    owners = lax.dynamic_slice_in_dim(page_owner, position * number, number, 0)
    index = jnp.arange(number, dtype=I32)
    ahead = (owners[None, :] < owners[:, None]) | (
        (owners[None, :] == owners[:, None]) & (index[None, :] < index[:, None])
    )
    order = jnp.sum(ahead.astype(I32), axis=1)
    keep, give = decode_halves(order, place, anchors, by_token, scales)
    got = lax.ppermute(give, "pool", TWIN)
    plan = make_plan(place, lengths, page_owner)
    own = (keep, got)
    landed = []
    after = plan
    for time in range(ROUNDS):
        parts = pick(time, plan, place, own, landed, after)
        landed.append(ship(parts))
        after = parts[2]
        if time == 1:
            seen, _ = lax.optimization_barrier((plan, after))
            after = partial = attend(seen, queries, anchors, by_token, scales)
    partial, _ = lax.optimization_barrier((partial, landed[ROUNDS - 2][0]))
    swapped = lax.all_to_all(partial, "pool", split_axis=0, concat_axis=0, tiled=True)
    attention = merge(plan, place, swapped)

    def in_time(landed):
        return finish(plan, place, own, landed)

    def late(landed):
        landed, last = list(landed), plan
        for time in range(ROUNDS, LIMIT):
            parts = pick(time, plan, place, own, landed, last)
            landed.append(ship(parts))
            last = parts[2]
        return finish(plan, place, own, landed)

    def padded(landed):
        devices = jnp.arange(16, dtype=I32)
        sent = jnp.any(owners[None, :] == devices[:, None], axis=1).astype(I32)
        slabs = decode_sorted(order, sent, jnp.cumsum(sent) - sent, anchors, by_token, scales)
        arrived = lax.all_to_all(slabs, "pool", split_axis=0, concat_axis=0, tiled=True)
        taken = jnp.any((page_owner == position).reshape(16, number), axis=1).astype(I32)
        return assemble(taken, jnp.cumsum(taken) - taken, arrived, number)

    needed = plan[2, 0]
    branch = (needed > ROUNDS).astype(I32) + (needed > LIMIT).astype(I32)
    cache = lax.switch(branch, (in_time, late, padded), landed)
    return (cache, attention)


def decode_pages(anchors, deltas, scales):
    block_scale = jnp.repeat(scales, HD, axis=1)
    rebuilt = anchors[:, None, :].astype(jnp.float32) + block_scale[:, None, :] * deltas.astype(
        jnp.float32
    )
    return jnp.concatenate([anchors[:, None, :], rebuilt.astype(jnp.bfloat16)], axis=1)


def page_scores(work_pages, queries, requests):
    number = work_pages.shape[0]
    key_rows = work_pages[:, :, : KVH * HD].reshape(number, PAGE, KVH, HD)
    picked = jnp.take(queries, requests, axis=0).reshape(number, STEPS, KVH, QH // KVH, HD)
    scores = jnp.einsum(
        "nskgd,ntkd->nskgt", picked, key_rows, preferred_element_type=jnp.float32
    ) * HD ** (-0.5)
    return (scores, jnp.max(scores, axis=4))


def accumulate(scores, page_max, work_pages, requests, shift_max):
    number = work_pages.shape[0]
    rows_out = shift_max.shape[0]
    block_size = min(32, number)
    blocks = number // block_size
    value_rows = work_pages[:, :, KVH * HD :].reshape(blocks, block_size, PAGE, KVH, HD)
    score_blocks = scores.reshape((blocks, block_size) + scores.shape[1:])
    max_blocks = page_max.reshape((blocks, block_size) + page_max.shape[1:])
    request_blocks = requests.reshape(blocks, block_size)

    def block_step(running, pieces):
        totals, numerator = running
        block_scores, block_max, block_values, block_requests = pieces
        exponent = jnp.exp(block_scores - block_max[..., None])
        weights = exponent.astype(jnp.bfloat16)
        page_out = jnp.einsum(
            "nskgt,ntkd->nskgd", weights, block_values, preferred_element_type=jnp.float32
        )
        factor = jnp.exp(block_max - jnp.take(shift_max, block_requests, axis=0))
        select = (block_requests[None, :] == jnp.arange(rows_out, dtype=jnp.int32)[:, None]).astype(
            jnp.float32
        )
        spread = select[:, :, None, None, None] * factor[None]
        totals = totals + jnp.sum(spread * jnp.sum(exponent, axis=4)[None], axis=1)
        numerator = numerator + jnp.einsum(
            "rnskg,nskgd->rskgd", spread, page_out, precision=lax.Precision.HIGHEST
        )
        return ((totals, numerator), None)

    start_totals = jnp.zeros(shift_max.shape, jnp.float32)
    start_numer = jnp.zeros(shift_max.shape + (HD,), jnp.float32)
    finals, ignored = lax.scan(
        block_step,
        (start_totals, start_numer),
        (score_blocks, max_blocks, value_rows, request_blocks),
    )
    return finals


def request_of(index, request_ends):
    return jnp.sum((index[:, None] >= request_ends[None, :]).astype(jnp.int32), axis=1)


def local(anchors, deltas, scales, queries, lengths, page_owner):
    devices = lax.axis_size("pool")
    position = lax.axis_index("pool")
    number = anchors.shape[0]
    capacity = max(2, 2 * number // devices)
    pages = decode_pages(anchors, deltas, scales)
    request_ends = jnp.cumsum(lengths)
    owners = lax.dynamic_slice_in_dim(page_owner, position * number, number, 0)
    marked = (owners[:, None] == jnp.arange(devices, dtype=jnp.int32)[None, :]).astype(jnp.int32)
    ranking = jnp.sum((jnp.cumsum(marked, axis=0) - 1) * marked, axis=1)
    slot_ids = owners * capacity + ranking
    matches = slot_ids[None, :] == jnp.arange(devices * capacity, dtype=jnp.int32)[:, None]
    sources = jnp.sum(jnp.where(matches, jnp.arange(number, dtype=jnp.int32)[None, :], 0), axis=1)
    outgoing = jnp.take(pages, sources, axis=0)
    arrived = lax.all_to_all(outgoing, "pool", split_axis=0, concat_axis=0, tiled=True)
    held_pages = jnp.nonzero(page_owner == position, size=number)[0].astype(jnp.int32)
    senders = held_pages // number
    before = jnp.sum((held_pages[None, :] < (senders * number)[:, None]).astype(jnp.int32), axis=1)
    row_ids = senders * capacity + jnp.arange(number, dtype=jnp.int32) - before
    cache = jnp.take(arrived, row_ids, axis=0)
    columns = QH * HD // devices
    requests = request_of(held_pages, request_ends)
    scores, page_max = page_scores(cache, queries, requests)
    onehot = requests[None, :] == jnp.arange(REQS, dtype=jnp.int32)[:, None]
    local_max = jnp.max(jnp.where(onehot[:, :, None, None, None], page_max[None], -1e30), axis=1)
    global_max = lax.pmax(local_max.astype(jnp.bfloat16), "pool").astype(local_max.dtype)
    totals, numerator = accumulate(scores, page_max, cache, requests, global_max)
    summed, numerator = lax.psum((totals, numerator), "pool")
    whole = (numerator / summed[..., None]).reshape(REQS, STEPS, QH * HD)
    result = lax.dynamic_slice_in_dim(whole, position * columns, columns, 2)
    return (cache, result.astype(jnp.bfloat16))


def solution(mesh):
    placed = (
        P(("groups", "pool"), None),
        P(("groups", "pool"), None, None),
        P(("groups", "pool"), None),
        P("groups", None, None),
        P("groups"),
        P("groups"),
    )
    lanes = mesh.shape["pool"] == 16
    return jax.shard_map(
        local_lanes if lanes else local,
        mesh=mesh,
        in_specs=placed,
        out_specs=(P(("groups", "pool"), None, None), P("groups", None, "pool")),
        check_vma=False,
    )
```

```python
import functools
import jax
import jax.numpy as jnp
from jax import lax
from jax.experimental import pallas as pl
from jax.experimental.pallas import tpu as pltpu
from jax.sharding import PartitionSpec as P

QH = 64
KVH = 4
HD = 128
PAGE = 16
STEPS = 8
REQS = 16
KVW = 2 * KVH * HD
SPAN = 3
LOW = -1e30
VMEM_LIMIT = 48 * 1024 * 1024
F32 = jnp.float32
BF16 = jnp.bfloat16
I32 = jnp.int32


def decode_kernel(chunk, place, flags, blocks, anchors, deltas, scales, out, rows, staged, sems):
    step = pl.program_id(0)
    for head in range(2 * KVH):
        cols = slice(head * HD, (head + 1) * HD)
        scale = jnp.broadcast_to(scales[:, head : head + 1], (chunk, HD))
        anchor = anchors[:, cols].astype(F32)
        rows[head * PAGE * chunk : head * PAGE * chunk + chunk, :] = anchor
        for token in range(1, PAGE):
            start = (head * PAGE + token) * chunk
            rows[start : start + chunk, :] = anchor + scale * deltas[token - 1, :, cols].astype(F32)
    for page in range(chunk):
        picked = [
            rows[pl.ds(head * PAGE * chunk + page, PAGE, stride=chunk), :]
            for head in range(2 * KVH)
        ]
        staged[place[step * chunk + page]] = jnp.concatenate(picked, axis=1).astype(BF16)

    @pl.when(step == pl.num_programs(0) - 1)
    def flush():
        copies = []
        for owner in range(16):
            copy = pltpu.make_async_copy(
                staged.at[pl.ds(blocks[owner] * PAGE, PAGE)],
                out.at[pl.ds(owner * PAGE, PAGE)],
                sems.at[owner],
            )
            pl.when(flags[owner] > 0)(copy.start)
            copies.append(copy)
        for owner in range(16):
            pl.when(flags[owner] > 0)(copies[owner].wait)


def decode_sorted(place, flags, blocks, anchors, deltas, scales):
    number = anchors.shape[0]
    chunk = 16
    return pl.pallas_call(
        functools.partial(decode_kernel, chunk),
        grid_spec=pltpu.PrefetchScalarGridSpec(
            num_scalar_prefetch=3,
            grid=(number // chunk,),
            in_specs=[
                pl.BlockSpec((chunk, KVW), lambda i, *_: (i, 0)),
                pl.BlockSpec((PAGE - 1, chunk, KVW), lambda i, *_: (0, i, 0)),
                pl.BlockSpec((chunk, 2 * KVH), lambda i, *_: (i, 0)),
            ],
            out_specs=pl.BlockSpec(memory_space=pl.ANY),
            scratch_shapes=[
                pltpu.VMEM((2 * KVH * PAGE * chunk, HD), F32),
                pltpu.VMEM((number, PAGE, KVW), BF16),
                pltpu.SemaphoreType.DMA((16,)),
            ],
        ),
        out_shape=jax.ShapeDtypeStruct((16 * PAGE, PAGE, KVW), BF16),
        compiler_params=pltpu.CompilerParams(vmem_limit_bytes=VMEM_LIMIT),
        name="decode_sorted",
    )(place, flags, blocks, anchors, deltas, scales)


def attend_kernel(head, plan, requests, first, second, third, key_anchor, val_anchor, key_delta, val_delta, scales, after, out, keys, vals):
    number = key_anchor.shape[0]
    columns = jnp.transpose(scales[...])
    key_scale = columns[:, head : head + 1]
    val_scale = columns[:, head + KVH : head + KVH + 1]
    for anchor, delta, scale, kept in (
        (key_anchor, key_delta, key_scale, keys),
        (val_anchor, val_delta, val_scale, vals),
    ):
        kept[0:number, :] = anchor[...]
        wide = anchor[...].astype(F32)
        for token in range(1, PAGE):
            kept[token * number : (token + 1) * number, :] = (
                wide + scale * delta[token - 1].astype(F32)
            ).astype(BF16)
    token_request = jnp.concatenate([requests[4:5, :]] * PAGE, axis=1) - plan[5, 0]
    rows = STEPS * QH // KVH
    eye = lax.broadcasted_iota(I32, (rows, rows), 0) == lax.broadcasted_iota(I32, (rows, rows), 1)
    pieces = []
    for slot, queries in enumerate((first, second, third)):
        wide = queries[0].astype(F32)
        picked = jnp.concatenate(
            [wide[:, group * HD : (group + 1) * HD] for group in range(QH // KVH)], axis=0
        ).astype(BF16)
        scores = lax.dot_general(
            picked, keys[...], (((1,), (1,)), ((), ())), preferred_element_type=F32
        ) * HD ** (-0.5)
        inside = token_request == slot
        scores = jnp.where(inside, scores, LOW)
        top = jnp.max(scores, axis=1, keepdims=True)
        exponent = jnp.where(inside, jnp.exp(scores - top), 0.0)
        total = jnp.maximum(jnp.sum(exponent, axis=1, keepdims=True), 1e-30)
        numer = jnp.dot(exponent.astype(BF16), vals[...], preferred_element_type=F32)
        mean = (numer * (1.0 / total)).astype(BF16)
        quarter = rows // 4
        for part in range(4):
            out[part, slot * quarter : (slot + 1) * quarter, :] = mean[
                part * quarter : (part + 1) * quarter
            ]
        level = top + jnp.log(total)
        line = jnp.sum(jnp.where(eye, level, 0.0), axis=0, keepdims=True)
        for _ in range(3):
            piece = line.astype(BF16).astype(F32)
            pieces.append(piece)
            line = line - piece
    pieces.append(jnp.zeros((16 - len(pieces), rows), F32))
    stats = jnp.concatenate(pieces, axis=0).astype(BF16)
    for part in range(4):
        out[part, 96:112, :] = stats


def attend(head, plan, queries, anchors, deltas, scales, after):
    number = anchors.shape[0]
    rows = STEPS * QH // KVH
    return pl.pallas_call(
        functools.partial(attend_kernel, head),
        grid_spec=pltpu.PrefetchScalarGridSpec(
            num_scalar_prefetch=1,
            grid=(1,),
            in_specs=[
                pl.BlockSpec((8, number), lambda i, *_: (0, 0)),
                *[
                    pl.BlockSpec((1, STEPS, rows * HD // STEPS), lambda i, p, k=k: (p[5, 0] + k, 0, head))
                    for k in range(SPAN)
                ],
                pl.BlockSpec((number, HD), lambda i, *_: (0, head)),
                pl.BlockSpec((number, HD), lambda i, *_: (0, head + KVH)),
                pl.BlockSpec((PAGE - 1, number, HD), lambda i, *_: (0, 0, head)),
                pl.BlockSpec((PAGE - 1, number, HD), lambda i, *_: (0, 0, head + KVH)),
                pl.BlockSpec((2 * KVH, number), lambda i, *_: (0, 0)),
                pl.BlockSpec(memory_space=pl.ANY),
            ],
            out_specs=pl.BlockSpec((4, 112, HD), lambda i, *_: (head, 0, 0)),
            scratch_shapes=[
                pltpu.VMEM((PAGE * number, HD), BF16),
                pltpu.VMEM((PAGE * number, HD), BF16),
            ],
        ),
        out_shape=jax.ShapeDtypeStruct((16, 112, HD), BF16),
        input_output_aliases={} if head == 0 else {10: 0},
        compiler_params=pltpu.CompilerParams(vmem_limit_bytes=VMEM_LIMIT),
        name=f"attend_{head}",
    )(plan, plan, queries, queries, queries, anchors, anchors, deltas, deltas, scales, after)


def merge_kernel(plan, place, parts, out, level, top, total, numer):
    quarter = 32
    row = lax.broadcasted_iota(I32, (quarter, HD), 0)
    lane = lax.broadcasted_iota(I32, (quarter, HD), 1)
    mine = lane == row + quarter * ((place[0] & 1) * 2 + place[1])
    top[...] = jnp.full(top.shape, LOW, F32)
    total[...] = jnp.zeros(total.shape, F32)
    numer[...] = jnp.zeros(numer.shape, F32)
    for sender in range(16):
        stats = parts[sender, 96:112, :].astype(F32)
        for slot in range(SPAN):
            line = stats[3 * slot : 3 * slot + 1] + (
                stats[3 * slot + 1 : 3 * slot + 2] + stats[3 * slot + 2 : 3 * slot + 3]
            )
            column = jnp.sum(jnp.where(mine, line, 0.0), axis=1, keepdims=True)
            column = jnp.broadcast_to(column, (quarter, HD))
            level[sender * SPAN + slot] = column
            request = plan[3, sender] + slot
            top[request] = jnp.maximum(top[request], column)
    for sender in range(16):
        for slot in range(SPAN):
            request = plan[3, sender] + slot
            weight = jnp.exp(level[sender * SPAN + slot] - top[request])
            mean = parts[sender, slot * quarter : (slot + 1) * quarter, :].astype(F32)
            total[request] += weight
            numer[request] += weight * mean
    for request in range(REQS):
        result = (numer[request] / total[request]).astype(BF16)
        for group in range(4):
            out[request, :, group * HD : (group + 1) * HD] = result[
                group * STEPS : (group + 1) * STEPS
            ]


def merge(plan, place, parts):
    return pl.pallas_call(
        merge_kernel,
        grid_spec=pltpu.PrefetchScalarGridSpec(
            num_scalar_prefetch=2,
            grid=(1,),
            in_specs=[pl.BlockSpec((16, 112, HD), lambda i, *_: (0, 0, 0))],
            out_specs=pl.BlockSpec((REQS, STEPS, 4 * HD), lambda i, *_: (0, 0, 0)),
            scratch_shapes=[
                pltpu.VMEM((16 * SPAN, 32, HD), F32),
                pltpu.VMEM((REQS, 32, HD), F32),
                pltpu.VMEM((REQS, 32, HD), F32),
                pltpu.VMEM((REQS, 32, HD), F32),
            ],
        ),
        out_shape=jax.ShapeDtypeStruct((REQS, STEPS, 4 * HD), BF16),
        compiler_params=pltpu.CompilerParams(vmem_limit_bytes=VMEM_LIMIT),
        name="merge",
    )(plan, place, parts)


def assemble_kernel(flags, blocks, arrived, out, staged, in_sems, out_sems):
    reads, writes = [], []
    for sender in range(16):
        rows = pl.ds(blocks[sender] * PAGE, PAGE)
        source = arrived.at[pl.ds(sender * PAGE, PAGE)]
        reads.append(pltpu.make_async_copy(source, staged.at[rows], in_sems.at[sender]))
        writes.append(pltpu.make_async_copy(staged.at[rows], out.at[rows], out_sems.at[sender]))
    for sender in range(16):
        pl.when(flags[sender] > 0)(reads[sender].start)
    for sender in range(16):

        @pl.when(flags[sender] > 0)
        def forward():
            reads[sender].wait()
            writes[sender].start()

    for sender in range(16):
        pl.when(flags[sender] > 0)(writes[sender].wait)


def assemble(flags, blocks, arrived, number):
    return pl.pallas_call(
        assemble_kernel,
        grid_spec=pltpu.PrefetchScalarGridSpec(
            num_scalar_prefetch=2,
            grid=(1,),
            in_specs=[pl.BlockSpec(memory_space=pl.ANY)],
            out_specs=pl.BlockSpec(memory_space=pl.ANY),
            scratch_shapes=[
                pltpu.VMEM((number, PAGE, KVW), BF16),
                pltpu.SemaphoreType.DMA((16,)),
                pltpu.SemaphoreType.DMA((16,)),
            ],
        ),
        out_shape=jax.ShapeDtypeStruct((number, PAGE, KVW), BF16),
        compiler_params=pltpu.CompilerParams(vmem_limit_bytes=VMEM_LIMIT),
        name="assemble",
    )(flags, blocks, arrived)


ROUNDS = 9
LIMIT = 12
UNIT = 2
LAG = 2
HALF = PAGE // 2
FAR = 1e6


def plan_kernel(place, lengths, owners, out):
    chip = place[0]
    row = lax.broadcasted_iota(I32, (16, 128), 0)
    lanes = lax.broadcasted_iota(I32, (16, 128), 1)
    sender_of = lanes >> 3
    turn = (lanes & 7).astype(F32)
    table = owners[...]
    running = jnp.zeros((16, 1), F32)
    sends = []
    targets = jnp.zeros((16, 128), F32)
    for owner in range(16):
        flag = jnp.max(jnp.where(table == owner, 1.0, 0.0), axis=1, keepdims=True)
        targets += jnp.where(turn == running, flag * owner, 0.0)
        sends.append(flag)
        running = running + flag
    dest = jnp.sum(jnp.where(row == sender_of, targets, 0.0), axis=0, keepdims=True)
    hits = jnp.zeros((16, 128), F32)
    for owner in range(16):
        hits += sends[owner] * jnp.where(dest == owner, 1.0, 0.0)
    rank = jnp.sum(jnp.where(row < sender_of, hits, 0.0), axis=0, keepdims=True).astype(I32)
    dest = dest.astype(I32)
    lane = lax.broadcasted_iota(I32, (1, 128), 1)
    sender = lane >> 3
    from_z, from_x = sender >> 2, (sender >> 1) & 1
    to_z, to_x = dest >> 2, (dest >> 1) & 1
    crosses = (from_z >> 1) != (to_z >> 1)
    below = jnp.where(
        lax.broadcasted_iota(I32, (128, 128), 0) < lax.broadcasted_iota(I32, (128, 128), 1), 1.0, 0.0
    )
    line = from_x
    for side in range(2):
        leaving = crosses & ((from_z >> 1) == side)
        free = jnp.where(leaving & (from_x != to_x), 1.0, 0.0)
        fixed = jnp.where(leaving & (from_x == to_x), 1.0, 0.0)
        tilt = jnp.sum(fixed * (2 * from_x - 1).astype(F32), axis=1, keepdims=True)
        count = jnp.sum(free, axis=1, keepdims=True)
        share = jnp.clip(jnp.floor((tilt + count) * 0.5), 0.0, count)
        step = share / jnp.maximum(count, 1.0)
        index = jnp.dot(jnp.broadcast_to(free, (8, 128)), below, preferred_element_type=F32)[0:1]
        first = jnp.floor((index + 1.0) * step + 1e-3) > jnp.floor(index * step + 1e-3)
        line = jnp.where(free > 0.0, jnp.where(first, 0, 1), line)
    chips = lax.broadcasted_iota(I32, (8, 128), 0)
    mine = lax.broadcasted_iota(I32, (8, 1), 0) == chip

    def round_step(time, carry):
        at_z, at_x, ready, code, steps, needed = carry
        waits = crosses & ((at_z >> 1) == (from_z >> 1))
        turns = ((at_z == to_z) & (at_x != to_x)) | (waits & (line != at_x))
        along = jnp.logical_not(turns) & (at_z != to_z)
        left = jnp.abs(to_z - at_z) + jnp.where(at_x != to_x, 1, 0)
        key = ((8 - left) * 128 + lane).astype(F32)
        here = (at_z * 2 + at_x == chips) & (ready <= time)
        heading = jnp.where(turns, 2, jnp.where(along, jnp.where(to_z > at_z, 0, 1), 3))
        moved = jnp.zeros((1, 128), F32)
        landed = jnp.zeros((1, 128), F32)
        value = (code + 1).astype(F32)
        for port in range(3):
            keys = jnp.where(here & (heading == port), key, FAR)
            for unit in range(UNIT):
                least = jnp.min(keys, axis=1, keepdims=True)
                chosen = jnp.where((keys == least) & (keys < FAR), 1.0, 0.0)
                source = jnp.sum(chosen * value, axis=1, keepdims=True)
                source = jnp.sum(jnp.where(mine, source, 0.0), axis=0, keepdims=True)
                slot = 3 * UNIT * time + UNIT * port + unit
                steps = steps + jnp.where(lane == slot, source, 0.0)
                taken = jnp.sum(chosen, axis=0, keepdims=True)
                moved = moved + taken * (port + 1)
                landed = landed + taken * (slot + 16).astype(F32)
                keys = jnp.where(chosen > 0.0, FAR, keys)
        went = moved.astype(I32)
        at_z = at_z + jnp.where(went == 1, 1, 0) - jnp.where(went == 2, 1, 0)
        at_x = jnp.where(went == 3, 1 - at_x, at_x)
        ready = jnp.where(went > 0, time + LAG, ready)
        code = jnp.where(went > 0, landed.astype(I32), code)
        any_move = jnp.max(moved, axis=1, keepdims=True)
        needed = jnp.where(any_move > 0.0, (time + 1).astype(F32), needed)
        return at_z, at_x, ready, code, steps, needed

    start = (
        from_z,
        from_x,
        jnp.zeros((1, 128), I32),
        (sender & 1) * 8 + (lane & 7),
        jnp.zeros((1, 128), F32),
        jnp.zeros((1, 1), F32),
    )
    at_z, at_x, ready, code, steps, needed = lax.fori_loop(0, LIMIT, round_step, start)
    undone = jnp.where((at_z == to_z) & (at_x == to_x), 0.0, 1.0)
    undone = jnp.max(undone, axis=1, keepdims=True)
    needed = jnp.where(undone > 0.0, float(LIMIT + 1), needed)
    arrives = (dest >> 1) == chip
    slots = (dest & 1) * 8 + rank
    final = jnp.sum(
        jnp.where((row == slots) & arrives, (code + 1).astype(F32), 0.0), axis=1, keepdims=True
    )
    final = jnp.sum(jnp.where(row == lanes, final, 0.0), axis=0, keepdims=True)
    out[0:1, :] = steps.astype(I32)
    out[1:2, :] = final.astype(I32)
    out[2:3, :] = jnp.broadcast_to(needed, (1, 128)).astype(I32)
    page = (2 * chip + place[1]) * 128 + lane
    requests = jnp.zeros((1, 128), I32)
    bases = jnp.zeros((1, 128), I32)
    end = 0
    for request in range(REQS):
        end = end + lengths[request]
        requests = requests + jnp.where(page >= end, 1, 0)
        bases = bases + jnp.where(lane * 128 >= end, 1, 0)
    bases = jnp.minimum(bases, REQS - SPAN)
    base = jnp.sum(jnp.where(lane == 2 * chip + place[1], bases, 0).astype(F32), axis=1, keepdims=True)
    out[3:4, :] = bases
    out[4:5, :] = requests
    out[5:6, :] = jnp.broadcast_to(base, (1, 128)).astype(I32)
    out[6:8, :] = jnp.zeros((2, 128), I32)


def make_plan(place, lengths, page_owner):
    return pl.pallas_call(
        plan_kernel,
        grid_spec=pltpu.PrefetchScalarGridSpec(
            num_scalar_prefetch=2,
            grid=(1,),
            in_specs=[pl.BlockSpec((16, 128), lambda i, *_: (0, 0))],
            out_specs=pl.BlockSpec((8, 128), lambda i, *_: (0, 0)),
        ),
        out_shape=jax.ShapeDtypeStruct((8, 128), I32),
        name="make_plan",
    )(place, lengths, page_owner.reshape(16, 128))


def halves_kernel(place, owners, anchors, deltas, scales, keep, give, swap, columns, ranks, order, rows, staged, sems):
    step = pl.program_id(0)
    count = PAGE * PAGE

    @pl.when(step == 0)
    def build():
        row = lax.broadcasted_iota(I32, (count, count), 0)
        lane = lax.broadcasted_iota(I32, (count, count), 1)
        swap[...] = jnp.where(lane == (row & 15) * PAGE + (row >> 4), 1.0, 0.0).astype(BF16)
        columns[...] = jnp.transpose(scales[...])
        number = owners.shape[1]
        row = lax.broadcasted_iota(I32, (number, number), 0)
        lane = lax.broadcasted_iota(I32, (number, number), 1)
        across = owners[pl.ds(2 * place[0] + place[1], 1), :].astype(F32)
        down = jnp.sum(jnp.where(row == lane, across, 0.0), axis=1, keepdims=True)
        ahead = (down < across) | ((down == across) & (row < lane))
        ranks[...] = jnp.sum(jnp.where(ahead, 1.0, 0.0), axis=0, keepdims=True).astype(I32)
        pltpu.make_async_copy(ranks, order, sems.at[2]).start()

    core = place[1]
    for part in range(anchors.shape[0] // PAGE):
        pages = slice(part * PAGE, (part + 1) * PAGE)
        for head in range(2 * KVH):
            cols = slice(head * HD, (head + 1) * HD)
            start = pl.multiple_of(step * anchors.shape[0] + part * PAGE, PAGE)
            scale = jnp.broadcast_to(columns[pl.ds(start, PAGE), head : head + 1], (PAGE, HD))
            first = anchors[pages, cols]
            anchor = first.astype(F32)
            rows[0:PAGE, cols] = first
            for token in range(1, PAGE):
                rebuilt = anchor + scale * deltas[token - 1, pages, cols].astype(F32)
                rows[token * PAGE : (token + 1) * PAGE, cols] = rebuilt.astype(BF16)
        turned = jnp.dot(swap[...], rows[...], preferred_element_type=F32).astype(BF16)
        if part == 0:

            @pl.when(step == 0)
            def ordered():
                pltpu.make_async_copy(ranks, order, sems.at[2]).wait()

        for page in range(PAGE):
            rank = order[0, step * anchors.shape[0] + part * PAGE + page]
            half = (rank >> 3) & 1
            slot = (half ^ core) * 64 + (rank >> 4) * HALF + (rank & 7)
            staged[slot] = turned[page * PAGE : (page + 1) * PAGE]

    @pl.when(step == pl.num_programs(0) - 1)
    def flush():
        copies = [
            pltpu.make_async_copy(staged.at[pl.ds(64, 64)], give, sems.at[0]),
            pltpu.make_async_copy(staged.at[pl.ds(0, 64)], keep, sems.at[1]),
        ]
        for copy in copies:
            copy.start()
        for copy in copies:
            copy.wait()


def decode_halves(place, page_owner, anchors, deltas, scales):
    number = anchors.shape[0]
    chunk = 2 * PAGE
    half = jax.ShapeDtypeStruct((number // 2, PAGE, KVW), BF16)
    return pl.pallas_call(
        halves_kernel,
        grid_spec=pltpu.PrefetchScalarGridSpec(
            num_scalar_prefetch=1,
            grid=(number // chunk,),
            in_specs=[
                pl.BlockSpec((16, number), lambda i, *_: (0, 0)),
                pl.BlockSpec((chunk, KVW), lambda i, *_: (i, 0)),
                pl.BlockSpec((PAGE - 1, chunk, KVW), lambda i, *_: (0, i, 0)),
                pl.BlockSpec((2 * KVH, number), lambda i, *_: (0, 0)),
            ],
            out_specs=[pl.BlockSpec(memory_space=pl.ANY)] * 2,
            scratch_shapes=[
                pltpu.VMEM((PAGE * PAGE, PAGE * PAGE), BF16),
                pltpu.VMEM((number, 2 * KVH), F32),
                pltpu.VMEM((1, number), I32),
                pltpu.SMEM((1, number), I32),
                pltpu.VMEM((PAGE * PAGE, KVW), BF16),
                pltpu.VMEM((number, PAGE, KVW), BF16),
                pltpu.SemaphoreType.DMA((3,)),
            ],
        ),
        out_shape=(half, half),
        compiler_params=pltpu.CompilerParams(vmem_limit_bytes=VMEM_LIMIT),
        name="decode_halves",
    )(place, page_owner.reshape(16, number), anchors, deltas, scales)


def fetch(code, core, own, landed, ports, target, sem):
    value = code - 1
    keep, got = own

    @pl.when((value >= 0) & (value < 16))
    def from_own():
        rows = pl.ds((value & 7) * HALF, HALF)

        @pl.when((value >> 3) == core)
        def kept():
            pltpu.make_async_copy(keep.at[rows], target, sem).start()

        @pl.when((value >> 3) != core)
        def gotten():
            pltpu.make_async_copy(got.at[rows], target, sem).start()

    for time, arrivals in enumerate(landed):
        offset = value - 16 - 3 * UNIT * time

        @pl.when((offset >= 0) & (offset < 3 * UNIT))
        def from_round():
            rows = pl.ds((offset % UNIT) * HALF, HALF)
            for port in ports:

                @pl.when((offset >= UNIT * port) & (offset < UNIT * (port + 1)))
                def from_port():
                    pltpu.make_async_copy(arrivals[port].at[rows], target, sem).start()


def settle(code, own, target, sem):
    @pl.when(code > 0)
    def wait():
        pltpu.make_async_copy(own[0].at[pl.ds(0, HALF)], target, sem).wait()


def unpack(refs):
    own, rest = refs[:2], refs[2:]
    return own, [rest[3 * i : 3 * i + 3] for i in range(len(rest) // 3)]


def pick_kernel(time, count, plan, place, *refs):
    own, landed = unpack(refs[: 2 + 3 * count])
    outs, sems = refs[-4:-1], refs[-1]
    for phase in range(2):
        for port in range(3):
            ports = (0, 1) if port == 2 else (port, 2)
            for unit in range(UNIT):
                code = plan[0, 3 * UNIT * time + UNIT * port + unit]
                target = outs[port].at[pl.ds(unit * HALF, HALF)]
                sem = sems.at[UNIT * port + unit]
                if phase == 0:
                    fetch(code, place[1], own, landed, ports, target, sem)
                else:
                    settle(code, own, target, sem)


def pick(time, plan, place, own, landed, after):
    landed = landed[: max(0, time - LAG + 1)]
    sources = list(own) + [array for arrivals in landed for array in arrivals] + [after]
    piece = jax.ShapeDtypeStruct((UNIT * HALF, PAGE, KVW), BF16)
    return pl.pallas_call(
        functools.partial(pick_kernel, time, len(landed)),
        grid_spec=pltpu.PrefetchScalarGridSpec(
            num_scalar_prefetch=2,
            grid=(1,),
            in_specs=[pl.BlockSpec(memory_space=pl.ANY)] * len(sources),
            out_specs=[pl.BlockSpec(piece.shape, lambda i, *_: (0, 0, 0))] * 3,
            scratch_shapes=[pltpu.SemaphoreType.DMA((3 * UNIT,))],
        ),
        out_shape=(piece,) * 3,
        compiler_params=pltpu.CompilerParams(vmem_limit_bytes=VMEM_LIMIT),
        name=f"pick_{time}",
    )(plan, place, *sources)


def give_kernel(count, plan, place, *refs):
    own, landed = unpack(refs[: 2 + 3 * count])
    out, sems = refs[2 + 3 * count :]
    core = place[1]
    codes = [plan[1, (1 - core) * 8 + slot] for slot in range(8)]
    targets = [out.at[pl.ds(slot * HALF, HALF)] for slot in range(8)]
    for slot in range(8):
        fetch(codes[slot], core, own, landed, (0, 1, 2), targets[slot], sems.at[slot])
    for slot in range(8):
        settle(codes[slot], own, targets[slot], sems.at[slot])


def gather_give(plan, place, own, landed):
    sources = list(own) + [array for arrivals in landed for array in arrivals]
    shape = (8 * HALF, PAGE, KVW)
    return pl.pallas_call(
        functools.partial(give_kernel, len(landed)),
        grid_spec=pltpu.PrefetchScalarGridSpec(
            num_scalar_prefetch=2,
            grid=(1,),
            in_specs=[pl.BlockSpec(memory_space=pl.ANY)] * len(sources),
            out_specs=pl.BlockSpec(shape, lambda i, *_: (0, 0, 0)),
            scratch_shapes=[pltpu.SemaphoreType.DMA((8,))],
        ),
        out_shape=jax.ShapeDtypeStruct(shape, BF16),
        compiler_params=pltpu.CompilerParams(vmem_limit_bytes=VMEM_LIMIT),
        name="gather_give",
    )(plan, place, *sources)


def own_kernel(count, plan, place, *refs):
    own, landed = unpack(refs[: 2 + 3 * count])
    out, staged, in_sems, out_sems = refs[2 + 3 * count :]
    core = place[1]
    codes = [plan[1, core * 8 + slot] for slot in range(8)]
    targets = [staged.at[pl.ds(slot * HALF, HALF)] for slot in range(8)]
    for slot in range(8):
        fetch(codes[slot], core, own, landed, (0, 1, 2), targets[slot], in_sems.at[slot])
    writes = []
    for slot in range(8):
        start = slot * PAGE + core * HALF
        writes.append(
            pltpu.make_async_copy(targets[slot], out.at[pl.ds(start, HALF)], out_sems.at[slot])
        )
        settle(codes[slot], own, targets[slot], in_sems.at[slot])
        writes[slot].start()
    for write in writes:
        write.wait()


def gather_own(plan, place, own, landed):
    sources = list(own) + [array for arrivals in landed for array in arrivals]
    return pl.pallas_call(
        functools.partial(own_kernel, len(landed)),
        grid_spec=pltpu.PrefetchScalarGridSpec(
            num_scalar_prefetch=2,
            grid=(1,),
            in_specs=[pl.BlockSpec(memory_space=pl.ANY)] * len(sources),
            out_specs=pl.BlockSpec(memory_space=pl.ANY),
            scratch_shapes=[
                pltpu.VMEM((8 * HALF, PAGE, KVW), BF16),
                pltpu.SemaphoreType.DMA((8,)),
                pltpu.SemaphoreType.DMA((8,)),
            ],
        ),
        out_shape=jax.ShapeDtypeStruct((8 * PAGE, PAGE, KVW), BF16),
        compiler_params=pltpu.CompilerParams(vmem_limit_bytes=VMEM_LIMIT),
        name="gather_own",
    )(plan, place, *sources)


def fill_kernel(place, cache, other, out, staged, in_sems, out_sems):
    half = 1 - place[1]
    reads, writes = [], []
    for slot in range(8):
        rows = pl.ds(slot * HALF, HALF)
        reads.append(pltpu.make_async_copy(other.at[rows], staged.at[rows], in_sems.at[slot]))
        writes.append(
            pltpu.make_async_copy(
                staged.at[rows], out.at[pl.ds(slot * PAGE + half * HALF, HALF)], out_sems.at[slot]
            )
        )
    for read in reads:
        read.start()
    for read, write in zip(reads, writes):
        read.wait()
        write.start()
    for write in writes:
        write.wait()


def fill(place, cache, other):
    return pl.pallas_call(
        fill_kernel,
        grid_spec=pltpu.PrefetchScalarGridSpec(
            num_scalar_prefetch=1,
            grid=(1,),
            in_specs=[pl.BlockSpec(memory_space=pl.ANY)] * 2,
            out_specs=pl.BlockSpec(memory_space=pl.ANY),
            scratch_shapes=[
                pltpu.VMEM((8 * HALF, PAGE, KVW), BF16),
                pltpu.SemaphoreType.DMA((8,)),
                pltpu.SemaphoreType.DMA((8,)),
            ],
        ),
        out_shape=jax.ShapeDtypeStruct(cache.shape, cache.dtype),
        input_output_aliases={1: 0},
        compiler_params=pltpu.CompilerParams(vmem_limit_bytes=VMEM_LIMIT),
        name="fill",
    )(place, cache, other)


UP = tuple((i, i + 4) for i in range(12))
DOWN = tuple((i + 4, i) for i in range(12))
ACROSS = tuple((i, i ^ 2) for i in range(16))
TWIN = tuple((i, i ^ 1) for i in range(16))


def ship(parts):
    return [lax.ppermute(part, "pool", pairs) for part, pairs in zip(parts, (UP, DOWN, ACROSS))]


def finish(plan, place, own, landed):
    other = lax.ppermute(gather_give(plan, place, own, landed), "pool", TWIN)
    return fill(place, gather_own(plan, place, own, landed), other)


def local_lanes(anchors, deltas, scales, queries, lengths, page_owner):
    position = lax.axis_index("pool")
    number = anchors.shape[0]
    by_token = jnp.transpose(deltas, (1, 0, 2))
    place = jnp.stack([position >> 1, position & 1]).astype(I32)
    lines = jnp.transpose(scales)
    keep, give = decode_halves(place, page_owner, anchors, by_token, lines)
    got = lax.ppermute(give, "pool", TWIN)
    plan = make_plan(place, lengths, page_owner)
    own = (keep, got)
    landed = []
    after = partial = plan
    for time in range(ROUNDS):
        parts = pick(time, plan, place, own, landed, after)
        landed.append(ship(parts))
        after = parts[2]
        if 1 <= time <= KVH:
            seen, _ = lax.optimization_barrier((plan, after))
            after = partial = attend(time - 1, seen, queries, anchors, by_token, lines, partial)
    swapped = lax.all_to_all(partial, "pool", split_axis=0, concat_axis=0, tiled=True)
    attention = merge(plan, place, swapped)
    plan, attention = lax.optimization_barrier((plan, attention))

    def in_time(landed):
        return finish(plan, place, own, landed)

    def late(landed):
        landed, last = list(landed), plan
        for time in range(ROUNDS, LIMIT):
            parts = pick(time, plan, place, own, landed, last)
            landed.append(ship(parts))
            last = parts[2]
        return finish(plan, place, own, landed)

    def padded(landed):
        owners = lax.dynamic_slice_in_dim(page_owner, position * number, number, 0)
        index = jnp.arange(number, dtype=I32)
        ahead = (owners[None, :] < owners[:, None]) | (
            (owners[None, :] == owners[:, None]) & (index[None, :] < index[:, None])
        )
        order = jnp.sum(ahead.astype(I32), axis=1)
        devices = jnp.arange(16, dtype=I32)
        sent = jnp.any(owners[None, :] == devices[:, None], axis=1).astype(I32)
        slabs = decode_sorted(order, sent, jnp.cumsum(sent) - sent, anchors, by_token, scales)
        arrived = lax.all_to_all(slabs, "pool", split_axis=0, concat_axis=0, tiled=True)
        taken = jnp.any((page_owner == position).reshape(16, number), axis=1).astype(I32)
        return assemble(taken, jnp.cumsum(taken) - taken, arrived, number)

    needed = plan[2, 0]
    branch = (needed > ROUNDS).astype(I32) + (needed > LIMIT).astype(I32)
    cache = lax.switch(branch, (in_time, late, padded), landed)
    return (cache, attention)


def decode_pages(anchors, deltas, scales):
    block_scale = jnp.repeat(scales, HD, axis=1)
    rebuilt = anchors[:, None, :].astype(jnp.float32) + block_scale[:, None, :] * deltas.astype(
        jnp.float32
    )
    return jnp.concatenate([anchors[:, None, :], rebuilt.astype(jnp.bfloat16)], axis=1)


def page_scores(work_pages, queries, requests):
    number = work_pages.shape[0]
    key_rows = work_pages[:, :, : KVH * HD].reshape(number, PAGE, KVH, HD)
    picked = jnp.take(queries, requests, axis=0).reshape(number, STEPS, KVH, QH // KVH, HD)
    scores = jnp.einsum(
        "nskgd,ntkd->nskgt", picked, key_rows, preferred_element_type=jnp.float32
    ) * HD ** (-0.5)
    return (scores, jnp.max(scores, axis=4))


def accumulate(scores, page_max, work_pages, requests, shift_max):
    number = work_pages.shape[0]
    rows_out = shift_max.shape[0]
    block_size = min(32, number)
    blocks = number // block_size
    value_rows = work_pages[:, :, KVH * HD :].reshape(blocks, block_size, PAGE, KVH, HD)
    score_blocks = scores.reshape((blocks, block_size) + scores.shape[1:])
    max_blocks = page_max.reshape((blocks, block_size) + page_max.shape[1:])
    request_blocks = requests.reshape(blocks, block_size)

    def block_step(running, pieces):
        totals, numerator = running
        block_scores, block_max, block_values, block_requests = pieces
        exponent = jnp.exp(block_scores - block_max[..., None])
        weights = exponent.astype(jnp.bfloat16)
        page_out = jnp.einsum(
            "nskgt,ntkd->nskgd", weights, block_values, preferred_element_type=jnp.float32
        )
        factor = jnp.exp(block_max - jnp.take(shift_max, block_requests, axis=0))
        select = (block_requests[None, :] == jnp.arange(rows_out, dtype=jnp.int32)[:, None]).astype(
            jnp.float32
        )
        spread = select[:, :, None, None, None] * factor[None]
        totals = totals + jnp.sum(spread * jnp.sum(exponent, axis=4)[None], axis=1)
        numerator = numerator + jnp.einsum(
            "rnskg,nskgd->rskgd", spread, page_out, precision=lax.Precision.HIGHEST
        )
        return ((totals, numerator), None)

    start_totals = jnp.zeros(shift_max.shape, jnp.float32)
    start_numer = jnp.zeros(shift_max.shape + (HD,), jnp.float32)
    finals, ignored = lax.scan(
        block_step,
        (start_totals, start_numer),
        (score_blocks, max_blocks, value_rows, request_blocks),
    )
    return finals


def request_of(index, request_ends):
    return jnp.sum((index[:, None] >= request_ends[None, :]).astype(jnp.int32), axis=1)


def local(anchors, deltas, scales, queries, lengths, page_owner):
    devices = lax.axis_size("pool")
    position = lax.axis_index("pool")
    number = anchors.shape[0]
    capacity = max(2, 2 * number // devices)
    pages = decode_pages(anchors, deltas, scales)
    request_ends = jnp.cumsum(lengths)
    owners = lax.dynamic_slice_in_dim(page_owner, position * number, number, 0)
    marked = (owners[:, None] == jnp.arange(devices, dtype=jnp.int32)[None, :]).astype(jnp.int32)
    ranking = jnp.sum((jnp.cumsum(marked, axis=0) - 1) * marked, axis=1)
    slot_ids = owners * capacity + ranking
    matches = slot_ids[None, :] == jnp.arange(devices * capacity, dtype=jnp.int32)[:, None]
    sources = jnp.sum(jnp.where(matches, jnp.arange(number, dtype=jnp.int32)[None, :], 0), axis=1)
    outgoing = jnp.take(pages, sources, axis=0)
    arrived = lax.all_to_all(outgoing, "pool", split_axis=0, concat_axis=0, tiled=True)
    held_pages = jnp.nonzero(page_owner == position, size=number)[0].astype(jnp.int32)
    senders = held_pages // number
    before = jnp.sum((held_pages[None, :] < (senders * number)[:, None]).astype(jnp.int32), axis=1)
    row_ids = senders * capacity + jnp.arange(number, dtype=jnp.int32) - before
    cache = jnp.take(arrived, row_ids, axis=0)
    columns = QH * HD // devices
    requests = request_of(held_pages, request_ends)
    scores, page_max = page_scores(cache, queries, requests)
    onehot = requests[None, :] == jnp.arange(REQS, dtype=jnp.int32)[:, None]
    local_max = jnp.max(jnp.where(onehot[:, :, None, None, None], page_max[None], -1e30), axis=1)
    global_max = lax.pmax(local_max.astype(jnp.bfloat16), "pool").astype(local_max.dtype)
    totals, numerator = accumulate(scores, page_max, cache, requests, global_max)
    summed, numerator = lax.psum((totals, numerator), "pool")
    whole = (numerator / summed[..., None]).reshape(REQS, STEPS, QH * HD)
    result = lax.dynamic_slice_in_dim(whole, position * columns, columns, 2)
    return (cache, result.astype(jnp.bfloat16))


def solution(mesh):
    placed = (
        P(("groups", "pool"), None),
        P(("groups", "pool"), None, None),
        P(("groups", "pool"), None),
        P("groups", None, None),
        P("groups"),
        P("groups"),
    )
    lanes = mesh.shape["pool"] == 16
    return jax.shard_map(
        local_lanes if lanes else local,
        mesh=mesh,
        in_specs=placed,
        out_specs=(P(("groups", "pool"), None, None), P("groups", None, "pool")),
        check_vma=False,
    )
```

```python
import functools
import jax
import jax.numpy as jnp
from jax import lax
from jax.experimental import pallas as pl
from jax.experimental.pallas import tpu as pltpu
from jax.sharding import PartitionSpec as P

QH = 64
KVH = 4
HD = 128
PAGE = 16
STEPS = 8
REQS = 16
KVW = 2 * KVH * HD
SPAN = 3
LOW = -1e30
VMEM_LIMIT = 48 * 1024 * 1024
F32 = jnp.float32
BF16 = jnp.bfloat16
I32 = jnp.int32


def decode_kernel(chunk, place, flags, blocks, anchors, deltas, scales, out, rows, staged, sems):
    step = pl.program_id(0)
    for head in range(2 * KVH):
        cols = slice(head * HD, (head + 1) * HD)
        scale = jnp.broadcast_to(scales[:, head : head + 1], (chunk, HD))
        anchor = anchors[:, cols].astype(F32)
        rows[head * PAGE * chunk : head * PAGE * chunk + chunk, :] = anchor
        for token in range(1, PAGE):
            start = (head * PAGE + token) * chunk
            rows[start : start + chunk, :] = anchor + scale * deltas[token - 1, :, cols].astype(F32)
    for page in range(chunk):
        picked = [
            rows[pl.ds(head * PAGE * chunk + page, PAGE, stride=chunk), :]
            for head in range(2 * KVH)
        ]
        staged[place[step * chunk + page]] = jnp.concatenate(picked, axis=1).astype(BF16)

    @pl.when(step == pl.num_programs(0) - 1)
    def flush():
        copies = []
        for owner in range(16):
            copy = pltpu.make_async_copy(
                staged.at[pl.ds(blocks[owner] * PAGE, PAGE)],
                out.at[pl.ds(owner * PAGE, PAGE)],
                sems.at[owner],
            )
            pl.when(flags[owner] > 0)(copy.start)
            copies.append(copy)
        for owner in range(16):
            pl.when(flags[owner] > 0)(copies[owner].wait)


def decode_sorted(place, flags, blocks, anchors, deltas, scales):
    number = anchors.shape[0]
    chunk = 16
    return pl.pallas_call(
        functools.partial(decode_kernel, chunk),
        grid_spec=pltpu.PrefetchScalarGridSpec(
            num_scalar_prefetch=3,
            grid=(number // chunk,),
            in_specs=[
                pl.BlockSpec((chunk, KVW), lambda i, *_: (i, 0)),
                pl.BlockSpec((PAGE - 1, chunk, KVW), lambda i, *_: (0, i, 0)),
                pl.BlockSpec((chunk, 2 * KVH), lambda i, *_: (i, 0)),
            ],
            out_specs=pl.BlockSpec(memory_space=pl.ANY),
            scratch_shapes=[
                pltpu.VMEM((2 * KVH * PAGE * chunk, HD), F32),
                pltpu.VMEM((number, PAGE, KVW), BF16),
                pltpu.SemaphoreType.DMA((16,)),
            ],
        ),
        out_shape=jax.ShapeDtypeStruct((16 * PAGE, PAGE, KVW), BF16),
        compiler_params=pltpu.CompilerParams(vmem_limit_bytes=VMEM_LIMIT),
        name="decode_sorted",
    )(place, flags, blocks, anchors, deltas, scales)


def attend_kernel(plan, requests, first, second, third, key_anchor, val_anchor, key_delta, val_delta, scales, after, out, keys, vals):
    head = pl.program_id(0)
    number = key_anchor.shape[0]
    table = jnp.transpose(scales[...])
    lane = lax.broadcasted_iota(I32, table.shape, 1)
    key_scale = jnp.sum(jnp.where(lane == head, table, 0.0), axis=1, keepdims=True)
    val_scale = jnp.sum(jnp.where(lane == head + KVH, table, 0.0), axis=1, keepdims=True)
    for anchor, delta, scale, kept in (
        (key_anchor, key_delta, key_scale, keys),
        (val_anchor, val_delta, val_scale, vals),
    ):
        kept[0:number, :] = anchor[...]
        wide = anchor[...].astype(F32)
        for token in range(1, PAGE):
            kept[token * number : (token + 1) * number, :] = (
                wide + scale * delta[token - 1].astype(F32)
            ).astype(BF16)
    token_request = jnp.concatenate([requests[4:5, :]] * PAGE, axis=1) - plan[5, 0]
    rows = STEPS * QH // KVH
    eye = lax.broadcasted_iota(I32, (rows, rows), 0) == lax.broadcasted_iota(I32, (rows, rows), 1)
    pieces = []
    for slot, queries in enumerate((first, second, third)):
        wide = queries[0].astype(F32)
        picked = jnp.concatenate(
            [wide[:, group * HD : (group + 1) * HD] for group in range(QH // KVH)], axis=0
        ).astype(BF16)
        scores = lax.dot_general(
            picked, keys[...], (((1,), (1,)), ((), ())), preferred_element_type=F32
        ) * HD ** (-0.5)
        inside = token_request == slot
        scores = jnp.where(inside, scores, LOW)
        top = jnp.max(scores, axis=1, keepdims=True)
        exponent = jnp.where(inside, jnp.exp(scores - top), 0.0)
        total = jnp.maximum(jnp.sum(exponent, axis=1, keepdims=True), 1e-30)
        numer = jnp.dot(exponent.astype(BF16), vals[...], preferred_element_type=F32)
        mean = (numer * (1.0 / total)).astype(BF16)
        quarter = rows // 4
        for part in range(4):
            out[part, slot * quarter : (slot + 1) * quarter, :] = mean[
                part * quarter : (part + 1) * quarter
            ]
        level = top + jnp.log(total)
        line = jnp.sum(jnp.where(eye, level, 0.0), axis=0, keepdims=True)
        for _ in range(3):
            piece = line.astype(BF16).astype(F32)
            pieces.append(piece)
            line = line - piece
    pieces.append(jnp.zeros((16 - len(pieces), rows), F32))
    stats = jnp.concatenate(pieces, axis=0).astype(BF16)
    for part in range(4):
        out[part, 96:112, :] = stats


def attend(plan, queries, anchors, deltas, scales, after):
    number = anchors.shape[0]
    rows = STEPS * QH // KVH
    return pl.pallas_call(
        attend_kernel,
        grid_spec=pltpu.PrefetchScalarGridSpec(
            num_scalar_prefetch=1,
            grid=(KVH,),
            in_specs=[
                pl.BlockSpec((8, number), lambda h, *_: (0, 0)),
                *[
                    pl.BlockSpec((1, STEPS, rows * HD // STEPS), lambda h, p, k=k: (p[5, 0] + k, 0, h))
                    for k in range(SPAN)
                ],
                pl.BlockSpec((number, HD), lambda h, *_: (0, h)),
                pl.BlockSpec((number, HD), lambda h, *_: (0, h + KVH)),
                pl.BlockSpec((PAGE - 1, number, HD), lambda h, *_: (0, 0, h)),
                pl.BlockSpec((PAGE - 1, number, HD), lambda h, *_: (0, 0, h + KVH)),
                pl.BlockSpec((2 * KVH, number), lambda h, *_: (0, 0)),
                pl.BlockSpec(memory_space=pl.ANY),
            ],
            out_specs=pl.BlockSpec((4, 112, HD), lambda h, *_: (h, 0, 0)),
            scratch_shapes=[
                pltpu.VMEM((PAGE * number, HD), BF16),
                pltpu.VMEM((PAGE * number, HD), BF16),
            ],
        ),
        out_shape=jax.ShapeDtypeStruct((16, 112, HD), BF16),
        compiler_params=pltpu.CompilerParams(vmem_limit_bytes=VMEM_LIMIT),
        name="attend",
    )(plan, plan, queries, queries, queries, anchors, anchors, deltas, deltas, scales, after)


def merge_kernel(plan, place, parts, out, level, top, total, numer):
    quarter = 32
    row = lax.broadcasted_iota(I32, (quarter, HD), 0)
    lane = lax.broadcasted_iota(I32, (quarter, HD), 1)
    mine = lane == row + quarter * ((place[0] & 1) * 2 + place[1])
    top[...] = jnp.full(top.shape, LOW, F32)
    total[...] = jnp.zeros(total.shape, F32)
    numer[...] = jnp.zeros(numer.shape, F32)
    for sender in range(16):
        stats = parts[sender, 96:112, :].astype(F32)
        for slot in range(SPAN):
            line = stats[3 * slot : 3 * slot + 1] + (
                stats[3 * slot + 1 : 3 * slot + 2] + stats[3 * slot + 2 : 3 * slot + 3]
            )
            column = jnp.sum(jnp.where(mine, line, 0.0), axis=1, keepdims=True)
            column = jnp.broadcast_to(column, (quarter, HD))
            level[sender * SPAN + slot] = column
            request = plan[3, sender] + slot
            top[request] = jnp.maximum(top[request], column)
    for sender in range(16):
        for slot in range(SPAN):
            request = plan[3, sender] + slot
            weight = jnp.exp(level[sender * SPAN + slot] - top[request])
            mean = parts[sender, slot * quarter : (slot + 1) * quarter, :].astype(F32)
            total[request] += weight
            numer[request] += weight * mean
    for request in range(REQS):
        result = (numer[request] / total[request]).astype(BF16)
        for group in range(4):
            out[request, :, group * HD : (group + 1) * HD] = result[
                group * STEPS : (group + 1) * STEPS
            ]


def merge(plan, place, parts):
    return pl.pallas_call(
        merge_kernel,
        grid_spec=pltpu.PrefetchScalarGridSpec(
            num_scalar_prefetch=2,
            grid=(1,),
            in_specs=[pl.BlockSpec((16, 112, HD), lambda i, *_: (0, 0, 0))],
            out_specs=pl.BlockSpec((REQS, STEPS, 4 * HD), lambda i, *_: (0, 0, 0)),
            scratch_shapes=[
                pltpu.VMEM((16 * SPAN, 32, HD), F32),
                pltpu.VMEM((REQS, 32, HD), F32),
                pltpu.VMEM((REQS, 32, HD), F32),
                pltpu.VMEM((REQS, 32, HD), F32),
            ],
        ),
        out_shape=jax.ShapeDtypeStruct((REQS, STEPS, 4 * HD), BF16),
        compiler_params=pltpu.CompilerParams(vmem_limit_bytes=VMEM_LIMIT),
        name="merge",
    )(plan, place, parts)


def assemble_kernel(flags, blocks, arrived, out, staged, in_sems, out_sems):
    reads, writes = [], []
    for sender in range(16):
        rows = pl.ds(blocks[sender] * PAGE, PAGE)
        source = arrived.at[pl.ds(sender * PAGE, PAGE)]
        reads.append(pltpu.make_async_copy(source, staged.at[rows], in_sems.at[sender]))
        writes.append(pltpu.make_async_copy(staged.at[rows], out.at[rows], out_sems.at[sender]))
    for sender in range(16):
        pl.when(flags[sender] > 0)(reads[sender].start)
    for sender in range(16):

        @pl.when(flags[sender] > 0)
        def forward():
            reads[sender].wait()
            writes[sender].start()

    for sender in range(16):
        pl.when(flags[sender] > 0)(writes[sender].wait)


def assemble(flags, blocks, arrived, number):
    return pl.pallas_call(
        assemble_kernel,
        grid_spec=pltpu.PrefetchScalarGridSpec(
            num_scalar_prefetch=2,
            grid=(1,),
            in_specs=[pl.BlockSpec(memory_space=pl.ANY)],
            out_specs=pl.BlockSpec(memory_space=pl.ANY),
            scratch_shapes=[
                pltpu.VMEM((number, PAGE, KVW), BF16),
                pltpu.SemaphoreType.DMA((16,)),
                pltpu.SemaphoreType.DMA((16,)),
            ],
        ),
        out_shape=jax.ShapeDtypeStruct((number, PAGE, KVW), BF16),
        compiler_params=pltpu.CompilerParams(vmem_limit_bytes=VMEM_LIMIT),
        name="assemble",
    )(flags, blocks, arrived)


ROUNDS = 9
LIMIT = 12
UNIT = 2
LAG = 2
SIDE_LAG = 3
SLOTS = 7
HALF = PAGE // 2
FAR = 1e6


def units_of(port, time):
    if port < 2:
        return UNIT
    if time >= 8:
        return 2
    return 3 if time in (0, 2, 4, 6, 7) else 0


def plan_kernel(place, lengths, owners, out):
    chip = place[0]
    row = lax.broadcasted_iota(I32, (16, 128), 0)
    lanes = lax.broadcasted_iota(I32, (16, 128), 1)
    sender_of = lanes >> 3
    turn = (lanes & 7).astype(F32)
    table = owners[...]
    running = jnp.zeros((16, 1), F32)
    sends = []
    targets = jnp.zeros((16, 128), F32)
    for owner in range(16):
        flag = jnp.max(jnp.where(table == owner, 1.0, 0.0), axis=1, keepdims=True)
        targets += jnp.where(turn == running, flag * owner, 0.0)
        sends.append(flag)
        running = running + flag
    dest = jnp.sum(jnp.where(row == sender_of, targets, 0.0), axis=0, keepdims=True)
    hits = jnp.zeros((16, 128), F32)
    for owner in range(16):
        hits += sends[owner] * jnp.where(dest == owner, 1.0, 0.0)
    rank = jnp.sum(jnp.where(row < sender_of, hits, 0.0), axis=0, keepdims=True).astype(I32)
    dest = dest.astype(I32)
    lane = lax.broadcasted_iota(I32, (1, 128), 1)
    sender = lane >> 3
    from_z, from_x = sender >> 2, (sender >> 1) & 1
    to_z, to_x = dest >> 2, (dest >> 1) & 1
    crosses = (from_z >> 1) != (to_z >> 1)
    below = jnp.where(
        lax.broadcasted_iota(I32, (128, 128), 0) < lax.broadcasted_iota(I32, (128, 128), 1), 1.0, 0.0
    )
    line = from_x
    for side in range(2):
        leaving = crosses & ((from_z >> 1) == side)
        free = jnp.where(leaving & (from_x != to_x), 1.0, 0.0)
        fixed = jnp.where(leaving & (from_x == to_x), 1.0, 0.0)
        tilt = jnp.sum(fixed * (2 * from_x - 1).astype(F32), axis=1, keepdims=True)
        count = jnp.sum(free, axis=1, keepdims=True)
        share = jnp.clip(jnp.floor((tilt + count) * 0.5), 0.0, count)
        step = share / jnp.maximum(count, 1.0)
        index = jnp.dot(jnp.broadcast_to(free, (8, 128)), below, preferred_element_type=F32)[0:1]
        first = jnp.floor((index + 1.0) * step + 1e-3) > jnp.floor(index * step + 1e-3)
        line = jnp.where(free > 0.0, jnp.where(first, 0, 1), line)
    chips = lax.broadcasted_iota(I32, (8, 128), 0)
    mine = lax.broadcasted_iota(I32, (8, 1), 0) == chip

    def round_step(time, carry):
        at_z, at_x, ready, code, steps, needed = carry
        waits = crosses & ((at_z >> 1) == (from_z >> 1))
        turns = ((at_z == to_z) & (at_x != to_x)) | (waits & (line != at_x))
        along = jnp.logical_not(turns) & (at_z != to_z)
        left = jnp.abs(to_z - at_z) + jnp.where(at_x != to_x, 1, 0)
        key = ((8 - left) * 128 + lane).astype(F32)
        here = (at_z * 2 + at_x == chips) & (ready <= time)
        heading = jnp.where(turns, 2, jnp.where(along, jnp.where(to_z > at_z, 0, 1), 3))
        moved = jnp.zeros((1, 128), F32)
        landed = jnp.zeros((1, 128), F32)
        value = (code + 1).astype(F32)
        side = sum(jnp.where(time == t, units_of(2, t), 0) for t in range(LIMIT))
        for port in range(3):
            keys = jnp.where(here & (heading == port), key, FAR)
            for unit in range(UNIT if port < 2 else 3):
                if port == 2:
                    keys = jnp.where(unit < side, keys, FAR)
                least = jnp.min(keys, axis=1, keepdims=True)
                chosen = jnp.where((keys == least) & (keys < FAR), 1.0, 0.0)
                source = jnp.sum(chosen * value, axis=1, keepdims=True)
                source = jnp.sum(jnp.where(mine, source, 0.0), axis=0, keepdims=True)
                slot = SLOTS * time + UNIT * port + unit
                steps = steps + jnp.where(lane == slot, source, 0.0)
                taken = jnp.sum(chosen, axis=0, keepdims=True)
                moved = moved + taken * (port + 1)
                landed = landed + taken * (slot + 16).astype(F32)
                keys = jnp.where(chosen > 0.0, FAR, keys)
        went = moved.astype(I32)
        at_z = at_z + jnp.where(went == 1, 1, 0) - jnp.where(went == 2, 1, 0)
        at_x = jnp.where(went == 3, 1 - at_x, at_x)
        ready = jnp.where(went > 0, time + jnp.where(went == 3, SIDE_LAG, LAG), ready)
        code = jnp.where(went > 0, landed.astype(I32), code)
        any_move = jnp.max(moved, axis=1, keepdims=True)
        needed = jnp.where(any_move > 0.0, (time + 1).astype(F32), needed)
        return at_z, at_x, ready, code, steps, needed

    start = (
        from_z,
        from_x,
        jnp.zeros((1, 128), I32),
        (sender & 1) * 8 + (lane & 7),
        jnp.zeros((1, 128), F32),
        jnp.zeros((1, 1), F32),
    )
    at_z, at_x, ready, code, steps, needed = lax.fori_loop(0, LIMIT, round_step, start)
    undone = jnp.where((at_z == to_z) & (at_x == to_x), 0.0, 1.0)
    undone = jnp.max(undone, axis=1, keepdims=True)
    needed = jnp.where(undone > 0.0, float(LIMIT + 1), needed)
    arrives = (dest >> 1) == chip
    slots = (dest & 1) * 8 + rank
    final = jnp.sum(
        jnp.where((row == slots) & arrives, (code + 1).astype(F32), 0.0), axis=1, keepdims=True
    )
    final = jnp.sum(jnp.where(row == lanes, final, 0.0), axis=0, keepdims=True)
    out[0:1, :] = steps.astype(I32)
    out[1:2, :] = final.astype(I32)
    out[2:3, :] = jnp.broadcast_to(needed, (1, 128)).astype(I32)
    page = (2 * chip + place[1]) * 128 + lane
    requests = jnp.zeros((1, 128), I32)
    bases = jnp.zeros((1, 128), I32)
    end = 0
    for request in range(REQS):
        end = end + lengths[request]
        requests = requests + jnp.where(page >= end, 1, 0)
        bases = bases + jnp.where(lane * 128 >= end, 1, 0)
    bases = jnp.minimum(bases, REQS - SPAN)
    base = jnp.sum(jnp.where(lane == 2 * chip + place[1], bases, 0).astype(F32), axis=1, keepdims=True)
    out[3:4, :] = bases
    out[4:5, :] = requests
    out[5:6, :] = jnp.broadcast_to(base, (1, 128)).astype(I32)
    out[6:8, :] = jnp.zeros((2, 128), I32)


def make_plan(place, lengths, page_owner):
    return pl.pallas_call(
        plan_kernel,
        grid_spec=pltpu.PrefetchScalarGridSpec(
            num_scalar_prefetch=2,
            grid=(1,),
            in_specs=[pl.BlockSpec((16, 128), lambda i, *_: (0, 0))],
            out_specs=pl.BlockSpec((8, 128), lambda i, *_: (0, 0)),
        ),
        out_shape=jax.ShapeDtypeStruct((8, 128), I32),
        name="make_plan",
    )(place, lengths, page_owner.reshape(16, 128))


def halves_kernel(place, owners, anchors, deltas, scales, keep, give, swap, columns, ranks, order, rows, staged, sems):
    step = pl.program_id(0)
    count = PAGE * PAGE

    @pl.when(step == 0)
    def build():
        row = lax.broadcasted_iota(I32, (count, count), 0)
        lane = lax.broadcasted_iota(I32, (count, count), 1)
        swap[...] = jnp.where(lane == (row & 15) * PAGE + (row >> 4), 1.0, 0.0).astype(BF16)
        columns[...] = jnp.transpose(scales[...])
        number = owners.shape[1]
        row = lax.broadcasted_iota(I32, (number, number), 0)
        lane = lax.broadcasted_iota(I32, (number, number), 1)
        across = owners[pl.ds(2 * place[0] + place[1], 1), :].astype(F32)
        down = jnp.sum(jnp.where(row == lane, across, 0.0), axis=1, keepdims=True)
        ahead = (down < across) | ((down == across) & (row < lane))
        ranks[...] = jnp.sum(jnp.where(ahead, 1.0, 0.0), axis=0, keepdims=True).astype(I32)
        pltpu.make_async_copy(ranks, order, sems.at[2]).start()

    core = place[1]
    for part in range(anchors.shape[0] // PAGE):
        pages = slice(part * PAGE, (part + 1) * PAGE)
        for head in range(2 * KVH):
            cols = slice(head * HD, (head + 1) * HD)
            start = pl.multiple_of(step * anchors.shape[0] + part * PAGE, PAGE)
            scale = jnp.broadcast_to(columns[pl.ds(start, PAGE), head : head + 1], (PAGE, HD))
            first = anchors[pages, cols]
            anchor = first.astype(F32)
            rows[0:PAGE, cols] = first
            for token in range(1, PAGE):
                rebuilt = anchor + scale * deltas[token - 1, pages, cols].astype(F32)
                rows[token * PAGE : (token + 1) * PAGE, cols] = rebuilt.astype(BF16)
        turned = jnp.dot(swap[...], rows[...], preferred_element_type=F32).astype(BF16)
        if part == 0:

            @pl.when(step == 0)
            def ordered():
                pltpu.make_async_copy(ranks, order, sems.at[2]).wait()

        for page in range(PAGE):
            rank = order[0, step * anchors.shape[0] + part * PAGE + page]
            half = (rank >> 3) & 1
            slot = (half ^ core) * 64 + (rank >> 4) * HALF + (rank & 7)
            staged[slot] = turned[page * PAGE : (page + 1) * PAGE]

    @pl.when(step == pl.num_programs(0) - 1)
    def flush():
        copies = [
            pltpu.make_async_copy(staged.at[pl.ds(64, 64)], give, sems.at[0]),
            pltpu.make_async_copy(staged.at[pl.ds(0, 64)], keep, sems.at[1]),
        ]
        for copy in copies:
            copy.start()
        for copy in copies:
            copy.wait()


def decode_halves(place, page_owner, anchors, deltas, scales):
    number = anchors.shape[0]
    chunk = 2 * PAGE
    half = jax.ShapeDtypeStruct((number // 2, PAGE, KVW), BF16)
    return pl.pallas_call(
        halves_kernel,
        grid_spec=pltpu.PrefetchScalarGridSpec(
            num_scalar_prefetch=1,
            grid=(number // chunk,),
            in_specs=[
                pl.BlockSpec((16, number), lambda i, *_: (0, 0)),
                pl.BlockSpec((chunk, KVW), lambda i, *_: (i, 0)),
                pl.BlockSpec((PAGE - 1, chunk, KVW), lambda i, *_: (0, i, 0)),
                pl.BlockSpec((2 * KVH, number), lambda i, *_: (0, 0)),
            ],
            out_specs=[pl.BlockSpec(memory_space=pl.ANY)] * 2,
            scratch_shapes=[
                pltpu.VMEM((PAGE * PAGE, PAGE * PAGE), BF16),
                pltpu.VMEM((number, 2 * KVH), F32),
                pltpu.VMEM((1, number), I32),
                pltpu.SMEM((1, number), I32),
                pltpu.VMEM((PAGE * PAGE, KVW), BF16),
                pltpu.VMEM((number, PAGE, KVW), BF16),
                pltpu.SemaphoreType.DMA((3,)),
            ],
        ),
        out_shape=(half, half),
        compiler_params=pltpu.CompilerParams(vmem_limit_bytes=VMEM_LIMIT),
        name="decode_halves",
    )(place, page_owner.reshape(16, number), anchors, deltas, scales)


def fetch(code, core, own, landed, ports, target, sem):
    value = code - 1
    keep, got = own

    @pl.when((value >= 0) & (value < 16))
    def from_own():
        rows = pl.ds((value & 7) * HALF, HALF)

        @pl.when((value >> 3) == core)
        def kept():
            pltpu.make_async_copy(keep.at[rows], target, sem).start()

        @pl.when((value >> 3) != core)
        def gotten():
            pltpu.make_async_copy(got.at[rows], target, sem).start()

    for time, port, arrivals in landed:
        if port in ports:
            offset = value - 16 - SLOTS * time - UNIT * port

            @pl.when((offset >= 0) & (offset < units_of(port, time)))
            def from_round():
                rows = pl.ds(offset * HALF, HALF)
                pltpu.make_async_copy(arrivals.at[rows], target, sem).start()


def settle(code, own, target, sem):
    @pl.when(code > 0)
    def wait():
        pltpu.make_async_copy(own[0].at[pl.ds(0, HALF)], target, sem).wait()


def pick_kernel(time, tags, plan, place, *refs):
    own, landed = refs[:2], [tag + (ref,) for tag, ref in zip(tags, refs[2:])]
    used = [port for port in range(3) if units_of(port, time)]
    outs, sems = refs[-1 - len(used) : -1], refs[-1]
    for phase in range(2):
        for port, out in zip(used, outs):
            ports = (0, 1) if port == 2 else (port, 2)
            for unit in range(units_of(port, time)):
                code = plan[0, SLOTS * time + UNIT * port + unit]
                target = out.at[pl.ds(unit * HALF, HALF)]
                sem = sems.at[UNIT * port + unit]
                if phase == 0:
                    fetch(code, place[1], own, landed, ports, target, sem)
                else:
                    settle(code, own, target, sem)


def pick(time, plan, place, own, landed, after):
    landed = [item for item in landed if item[0] + (SIDE_LAG if item[1] == 2 else LAG) <= time]
    sources = list(own) + [item[2] for item in landed] + [after]
    pieces = [
        jax.ShapeDtypeStruct((units_of(port, time) * HALF, PAGE, KVW), BF16)
        for port in range(3)
        if units_of(port, time)
    ]
    return pl.pallas_call(
        functools.partial(pick_kernel, time, [item[:2] for item in landed]),
        grid_spec=pltpu.PrefetchScalarGridSpec(
            num_scalar_prefetch=2,
            grid=(1,),
            in_specs=[pl.BlockSpec(memory_space=pl.ANY)] * len(sources),
            out_specs=[pl.BlockSpec(piece.shape, lambda i, *_: (0, 0, 0)) for piece in pieces],
            scratch_shapes=[pltpu.SemaphoreType.DMA((SLOTS,))],
        ),
        out_shape=pieces,
        compiler_params=pltpu.CompilerParams(vmem_limit_bytes=VMEM_LIMIT),
        name=f"pick_{time}",
    )(plan, place, *sources)


def give_kernel(tags, plan, place, *refs):
    own, landed = refs[:2], [tag + (ref,) for tag, ref in zip(tags, refs[2:])]
    out, sems = refs[-2:]
    core = place[1]
    codes = [plan[1, (1 - core) * 8 + slot] for slot in range(8)]
    targets = [out.at[pl.ds(slot * HALF, HALF)] for slot in range(8)]
    for slot in range(8):
        fetch(codes[slot], core, own, landed, (0, 1, 2), targets[slot], sems.at[slot])
    for slot in range(8):
        settle(codes[slot], own, targets[slot], sems.at[slot])


def gather_give(plan, place, own, landed, after):
    sources = list(own) + [item[2] for item in landed] + [after]
    shape = (8 * HALF, PAGE, KVW)
    return pl.pallas_call(
        functools.partial(give_kernel, [item[:2] for item in landed]),
        grid_spec=pltpu.PrefetchScalarGridSpec(
            num_scalar_prefetch=2,
            grid=(1,),
            in_specs=[pl.BlockSpec(memory_space=pl.ANY)] * len(sources),
            out_specs=pl.BlockSpec(shape, lambda i, *_: (0, 0, 0)),
            scratch_shapes=[pltpu.SemaphoreType.DMA((8,))],
        ),
        out_shape=jax.ShapeDtypeStruct(shape, BF16),
        compiler_params=pltpu.CompilerParams(vmem_limit_bytes=VMEM_LIMIT),
        name="gather_give",
    )(plan, place, *sources)


def own_kernel(tags, plan, place, *refs):
    own, landed = refs[:2], [tag + (ref,) for tag, ref in zip(tags, refs[2:])]
    out, staged, in_sems, out_sems = refs[-4:]
    core = place[1]
    codes = [plan[1, core * 8 + slot] for slot in range(8)]
    targets = [staged.at[pl.ds(slot * HALF, HALF)] for slot in range(8)]
    for slot in range(8):
        fetch(codes[slot], core, own, landed, (0, 1, 2), targets[slot], in_sems.at[slot])
    writes = []
    for slot in range(8):
        start = slot * PAGE + core * HALF
        writes.append(
            pltpu.make_async_copy(targets[slot], out.at[pl.ds(start, HALF)], out_sems.at[slot])
        )
        settle(codes[slot], own, targets[slot], in_sems.at[slot])
        writes[slot].start()
    for write in writes:
        write.wait()


def gather_own(plan, place, own, landed):
    sources = list(own) + [item[2] for item in landed]
    return pl.pallas_call(
        functools.partial(own_kernel, [item[:2] for item in landed]),
        grid_spec=pltpu.PrefetchScalarGridSpec(
            num_scalar_prefetch=2,
            grid=(1,),
            in_specs=[pl.BlockSpec(memory_space=pl.ANY)] * len(sources),
            out_specs=pl.BlockSpec(memory_space=pl.ANY),
            scratch_shapes=[
                pltpu.VMEM((8 * HALF, PAGE, KVW), BF16),
                pltpu.SemaphoreType.DMA((8,)),
                pltpu.SemaphoreType.DMA((8,)),
            ],
        ),
        out_shape=jax.ShapeDtypeStruct((8 * PAGE, PAGE, KVW), BF16),
        compiler_params=pltpu.CompilerParams(vmem_limit_bytes=VMEM_LIMIT),
        name="gather_own",
    )(plan, place, *sources)


def fill_kernel(place, cache, other, out, staged, in_sems, out_sems):
    half = 1 - place[1]
    reads, writes = [], []
    for slot in range(8):
        rows = pl.ds(slot * HALF, HALF)
        reads.append(pltpu.make_async_copy(other.at[rows], staged.at[rows], in_sems.at[slot]))
        writes.append(
            pltpu.make_async_copy(
                staged.at[rows], out.at[pl.ds(slot * PAGE + half * HALF, HALF)], out_sems.at[slot]
            )
        )
    for read in reads:
        read.start()
    for read, write in zip(reads, writes):
        read.wait()
        write.start()
    for write in writes:
        write.wait()


def fill(place, cache, other):
    return pl.pallas_call(
        fill_kernel,
        grid_spec=pltpu.PrefetchScalarGridSpec(
            num_scalar_prefetch=1,
            grid=(1,),
            in_specs=[pl.BlockSpec(memory_space=pl.ANY)] * 2,
            out_specs=pl.BlockSpec(memory_space=pl.ANY),
            scratch_shapes=[
                pltpu.VMEM((8 * HALF, PAGE, KVW), BF16),
                pltpu.SemaphoreType.DMA((8,)),
                pltpu.SemaphoreType.DMA((8,)),
            ],
        ),
        out_shape=jax.ShapeDtypeStruct(cache.shape, cache.dtype),
        input_output_aliases={1: 0},
        compiler_params=pltpu.CompilerParams(vmem_limit_bytes=VMEM_LIMIT),
        name="fill",
    )(place, cache, other)


UP = tuple((i, i + 4) for i in range(12))
DOWN = tuple((i + 4, i) for i in range(12))
ACROSS = tuple((i, i ^ 2) for i in range(16))
TWIN = tuple((i, i ^ 1) for i in range(16))


def ship(time, parts):
    used = [port for port in range(3) if units_of(port, time)]
    hops = (UP, DOWN, ACROSS)
    return [(time, port, lax.ppermute(part, "pool", hops[port])) for port, part in zip(used, parts)]


def finish(plan, place, own, landed, after):
    other = lax.ppermute(gather_give(plan, place, own, landed, after), "pool", TWIN)
    return fill(place, gather_own(plan, place, own, landed), other)


def local_lanes(anchors, deltas, scales, queries, lengths, page_owner):
    position = lax.axis_index("pool")
    number = anchors.shape[0]
    by_token = jnp.transpose(deltas, (1, 0, 2))
    place = jnp.stack([position >> 1, position & 1]).astype(I32)
    lines = jnp.transpose(scales)
    keep, give = decode_halves(place, page_owner, anchors, by_token, lines)
    got = lax.ppermute(give, "pool", TWIN)
    plan = make_plan(place, lengths, page_owner)
    own = (keep, got)
    landed = []
    after = plan
    for time in range(ROUNDS):
        parts = pick(time, plan, place, own, landed, after)
        landed += ship(time, parts)
        after = parts[0]
    partial = attend(plan, queries, anchors, by_token, lines, after)
    swapped = lax.all_to_all(partial, "pool", split_axis=0, concat_axis=0, tiled=True)
    attention = merge(plan, place, swapped)
    cache = finish(plan, place, own, landed, partial)

    def in_time(cache):
        return cache

    def late(cache):
        more, last = list(landed), plan
        for time in range(ROUNDS, LIMIT):
            parts = pick(time, plan, place, own, more, last)
            more += ship(time, parts)
            last = parts[0]
        return finish(plan, place, own, more, last)

    def padded(cache):
        owners = lax.dynamic_slice_in_dim(page_owner, position * number, number, 0)
        index = jnp.arange(number, dtype=I32)
        ahead = (owners[None, :] < owners[:, None]) | (
            (owners[None, :] == owners[:, None]) & (index[None, :] < index[:, None])
        )
        order = jnp.sum(ahead.astype(I32), axis=1)
        devices = jnp.arange(16, dtype=I32)
        sent = jnp.any(owners[None, :] == devices[:, None], axis=1).astype(I32)
        slabs = decode_sorted(order, sent, jnp.cumsum(sent) - sent, anchors, by_token, scales)
        arrived = lax.all_to_all(slabs, "pool", split_axis=0, concat_axis=0, tiled=True)
        taken = jnp.any((page_owner == position).reshape(16, number), axis=1).astype(I32)
        return assemble(taken, jnp.cumsum(taken) - taken, arrived, number)

    needed = plan[2, 0]
    branch = (needed > ROUNDS).astype(I32) + (needed > LIMIT).astype(I32)
    branch, attention = lax.optimization_barrier((branch, attention))
    cache = lax.switch(branch, (in_time, late, padded), cache)
    return (cache, attention)


def decode_pages(anchors, deltas, scales):
    block_scale = jnp.repeat(scales, HD, axis=1)
    rebuilt = anchors[:, None, :].astype(jnp.float32) + block_scale[:, None, :] * deltas.astype(
        jnp.float32
    )
    return jnp.concatenate([anchors[:, None, :], rebuilt.astype(jnp.bfloat16)], axis=1)


def page_scores(work_pages, queries, requests):
    number = work_pages.shape[0]
    key_rows = work_pages[:, :, : KVH * HD].reshape(number, PAGE, KVH, HD)
    picked = jnp.take(queries, requests, axis=0).reshape(number, STEPS, KVH, QH // KVH, HD)
    scores = jnp.einsum(
        "nskgd,ntkd->nskgt", picked, key_rows, preferred_element_type=jnp.float32
    ) * HD ** (-0.5)
    return (scores, jnp.max(scores, axis=4))


def accumulate(scores, page_max, work_pages, requests, shift_max):
    number = work_pages.shape[0]
    rows_out = shift_max.shape[0]
    block_size = min(32, number)
    blocks = number // block_size
    value_rows = work_pages[:, :, KVH * HD :].reshape(blocks, block_size, PAGE, KVH, HD)
    score_blocks = scores.reshape((blocks, block_size) + scores.shape[1:])
    max_blocks = page_max.reshape((blocks, block_size) + page_max.shape[1:])
    request_blocks = requests.reshape(blocks, block_size)

    def block_step(running, pieces):
        totals, numerator = running
        block_scores, block_max, block_values, block_requests = pieces
        exponent = jnp.exp(block_scores - block_max[..., None])
        weights = exponent.astype(jnp.bfloat16)
        page_out = jnp.einsum(
            "nskgt,ntkd->nskgd", weights, block_values, preferred_element_type=jnp.float32
        )
        factor = jnp.exp(block_max - jnp.take(shift_max, block_requests, axis=0))
        select = (block_requests[None, :] == jnp.arange(rows_out, dtype=jnp.int32)[:, None]).astype(
            jnp.float32
        )
        spread = select[:, :, None, None, None] * factor[None]
        totals = totals + jnp.sum(spread * jnp.sum(exponent, axis=4)[None], axis=1)
        numerator = numerator + jnp.einsum(
            "rnskg,nskgd->rskgd", spread, page_out, precision=lax.Precision.HIGHEST
        )
        return ((totals, numerator), None)

    start_totals = jnp.zeros(shift_max.shape, jnp.float32)
    start_numer = jnp.zeros(shift_max.shape + (HD,), jnp.float32)
    finals, ignored = lax.scan(
        block_step,
        (start_totals, start_numer),
        (score_blocks, max_blocks, value_rows, request_blocks),
    )
    return finals


def request_of(index, request_ends):
    return jnp.sum((index[:, None] >= request_ends[None, :]).astype(jnp.int32), axis=1)


def local(anchors, deltas, scales, queries, lengths, page_owner):
    devices = lax.axis_size("pool")
    position = lax.axis_index("pool")
    number = anchors.shape[0]
    capacity = max(2, 2 * number // devices)
    pages = decode_pages(anchors, deltas, scales)
    request_ends = jnp.cumsum(lengths)
    owners = lax.dynamic_slice_in_dim(page_owner, position * number, number, 0)
    marked = (owners[:, None] == jnp.arange(devices, dtype=jnp.int32)[None, :]).astype(jnp.int32)
    ranking = jnp.sum((jnp.cumsum(marked, axis=0) - 1) * marked, axis=1)
    slot_ids = owners * capacity + ranking
    matches = slot_ids[None, :] == jnp.arange(devices * capacity, dtype=jnp.int32)[:, None]
    sources = jnp.sum(jnp.where(matches, jnp.arange(number, dtype=jnp.int32)[None, :], 0), axis=1)
    outgoing = jnp.take(pages, sources, axis=0)
    arrived = lax.all_to_all(outgoing, "pool", split_axis=0, concat_axis=0, tiled=True)
    held_pages = jnp.nonzero(page_owner == position, size=number)[0].astype(jnp.int32)
    senders = held_pages // number
    before = jnp.sum((held_pages[None, :] < (senders * number)[:, None]).astype(jnp.int32), axis=1)
    row_ids = senders * capacity + jnp.arange(number, dtype=jnp.int32) - before
    cache = jnp.take(arrived, row_ids, axis=0)
    columns = QH * HD // devices
    requests = request_of(held_pages, request_ends)
    scores, page_max = page_scores(cache, queries, requests)
    onehot = requests[None, :] == jnp.arange(REQS, dtype=jnp.int32)[:, None]
    local_max = jnp.max(jnp.where(onehot[:, :, None, None, None], page_max[None], -1e30), axis=1)
    global_max = lax.pmax(local_max.astype(jnp.bfloat16), "pool").astype(local_max.dtype)
    totals, numerator = accumulate(scores, page_max, cache, requests, global_max)
    summed, numerator = lax.psum((totals, numerator), "pool")
    whole = (numerator / summed[..., None]).reshape(REQS, STEPS, QH * HD)
    result = lax.dynamic_slice_in_dim(whole, position * columns, columns, 2)
    return (cache, result.astype(jnp.bfloat16))


def solution(mesh):
    placed = (
        P(("groups", "pool"), None),
        P(("groups", "pool"), None, None),
        P(("groups", "pool"), None),
        P("groups", None, None),
        P("groups"),
        P("groups"),
    )
    lanes = mesh.shape["pool"] == 16
    return jax.shard_map(
        local_lanes if lanes else local,
        mesh=mesh,
        in_specs=placed,
        out_specs=(P(("groups", "pool"), None, None), P("groups", None, "pool")),
        check_vma=False,
    )
```

```python
import functools
import jax
import jax.numpy as jnp
from jax import lax
from jax.experimental import pallas as pl
from jax.experimental.pallas import tpu as pltpu
from jax.sharding import PartitionSpec as P

QH = 64
KVH = 4
HD = 128
PAGE = 16
STEPS = 8
REQS = 16
KVW = 2 * KVH * HD
SPAN = 3
LOW = -1e30
VMEM_LIMIT = 48 * 1024 * 1024
F32 = jnp.float32
BF16 = jnp.bfloat16
I32 = jnp.int32


def decode_kernel(chunk, place, flags, blocks, anchors, deltas, scales, out, rows, staged, sems):
    step = pl.program_id(0)
    for head in range(2 * KVH):
        cols = slice(head * HD, (head + 1) * HD)
        scale = jnp.broadcast_to(scales[:, head : head + 1], (chunk, HD))
        anchor = anchors[:, cols].astype(F32)
        rows[head * PAGE * chunk : head * PAGE * chunk + chunk, :] = anchor
        for token in range(1, PAGE):
            start = (head * PAGE + token) * chunk
            rows[start : start + chunk, :] = anchor + scale * deltas[token - 1, :, cols].astype(F32)
    for page in range(chunk):
        picked = [
            rows[pl.ds(head * PAGE * chunk + page, PAGE, stride=chunk), :]
            for head in range(2 * KVH)
        ]
        staged[place[step * chunk + page]] = jnp.concatenate(picked, axis=1).astype(BF16)

    @pl.when(step == pl.num_programs(0) - 1)
    def flush():
        copies = []
        for owner in range(16):
            copy = pltpu.make_async_copy(
                staged.at[pl.ds(blocks[owner] * PAGE, PAGE)],
                out.at[pl.ds(owner * PAGE, PAGE)],
                sems.at[owner],
            )
            pl.when(flags[owner] > 0)(copy.start)
            copies.append(copy)
        for owner in range(16):
            pl.when(flags[owner] > 0)(copies[owner].wait)


def decode_sorted(place, flags, blocks, anchors, deltas, scales):
    number = anchors.shape[0]
    chunk = 16
    return pl.pallas_call(
        functools.partial(decode_kernel, chunk),
        grid_spec=pltpu.PrefetchScalarGridSpec(
            num_scalar_prefetch=3,
            grid=(number // chunk,),
            in_specs=[
                pl.BlockSpec((chunk, KVW), lambda i, *_: (i, 0)),
                pl.BlockSpec((PAGE - 1, chunk, KVW), lambda i, *_: (0, i, 0)),
                pl.BlockSpec((chunk, 2 * KVH), lambda i, *_: (i, 0)),
            ],
            out_specs=pl.BlockSpec(memory_space=pl.ANY),
            scratch_shapes=[
                pltpu.VMEM((2 * KVH * PAGE * chunk, HD), F32),
                pltpu.VMEM((number, PAGE, KVW), BF16),
                pltpu.SemaphoreType.DMA((16,)),
            ],
        ),
        out_shape=jax.ShapeDtypeStruct((16 * PAGE, PAGE, KVW), BF16),
        compiler_params=pltpu.CompilerParams(vmem_limit_bytes=VMEM_LIMIT),
        name="decode_sorted",
    )(place, flags, blocks, anchors, deltas, scales)


def attend_kernel(head, plan, requests, first, second, third, key_anchor, val_anchor, key_delta, val_delta, scales, after, out, keys, vals):
    number = key_anchor.shape[0]
    columns = jnp.transpose(scales[...])
    key_scale = columns[:, head : head + 1]
    val_scale = columns[:, head + KVH : head + KVH + 1]
    for anchor, delta, scale, kept in (
        (key_anchor, key_delta, key_scale, keys),
        (val_anchor, val_delta, val_scale, vals),
    ):
        kept[0:number, :] = anchor[...]
        wide = anchor[...].astype(F32)
        for token in range(1, PAGE):
            kept[token * number : (token + 1) * number, :] = (
                wide + scale * delta[token - 1].astype(F32)
            ).astype(BF16)
    token_request = jnp.concatenate([requests[4:5, :]] * PAGE, axis=1) - plan[5, 0]
    rows = STEPS * QH // KVH
    eye = lax.broadcasted_iota(I32, (rows, rows), 0) == lax.broadcasted_iota(I32, (rows, rows), 1)
    pieces = []
    for slot, queries in enumerate((first, second, third)):
        wide = queries[0].astype(F32)
        picked = jnp.concatenate(
            [wide[:, group * HD : (group + 1) * HD] for group in range(QH // KVH)], axis=0
        ).astype(BF16)
        scores = lax.dot_general(
            picked, keys[...], (((1,), (1,)), ((), ())), preferred_element_type=F32
        ) * HD ** (-0.5)
        inside = token_request == slot
        scores = jnp.where(inside, scores, LOW)
        top = jnp.max(scores, axis=1, keepdims=True)
        exponent = jnp.where(inside, jnp.exp(scores - top), 0.0)
        total = jnp.maximum(jnp.sum(exponent, axis=1, keepdims=True), 1e-30)
        numer = jnp.dot(exponent.astype(BF16), vals[...], preferred_element_type=F32)
        mean = (numer * (1.0 / total)).astype(BF16)
        quarter = rows // 4
        for part in range(4):
            out[part, slot * quarter : (slot + 1) * quarter, :] = mean[
                part * quarter : (part + 1) * quarter
            ]
        level = top + jnp.log(total)
        line = jnp.sum(jnp.where(eye, level, 0.0), axis=0, keepdims=True)
        for _ in range(3):
            piece = line.astype(BF16).astype(F32)
            pieces.append(piece)
            line = line - piece
    pieces.append(jnp.zeros((16 - len(pieces), rows), F32))
    stats = jnp.concatenate(pieces, axis=0).astype(BF16)
    for part in range(4):
        out[part, 96:112, :] = stats


def attend(head, plan, queries, anchors, deltas, scales, after):
    number = anchors.shape[0]
    rows = STEPS * QH // KVH
    return pl.pallas_call(
        functools.partial(attend_kernel, head),
        grid_spec=pltpu.PrefetchScalarGridSpec(
            num_scalar_prefetch=1,
            grid=(1,),
            in_specs=[
                pl.BlockSpec((8, number), lambda i, *_: (0, 0)),
                *[
                    pl.BlockSpec((1, STEPS, rows * HD // STEPS), lambda i, p, k=k: (p[5, 0] + k, 0, head))
                    for k in range(SPAN)
                ],
                pl.BlockSpec((number, HD), lambda i, *_: (0, head)),
                pl.BlockSpec((number, HD), lambda i, *_: (0, head + KVH)),
                pl.BlockSpec((PAGE - 1, number, HD), lambda i, *_: (0, 0, head)),
                pl.BlockSpec((PAGE - 1, number, HD), lambda i, *_: (0, 0, head + KVH)),
                pl.BlockSpec((2 * KVH, number), lambda i, *_: (0, 0)),
                pl.BlockSpec(memory_space=pl.ANY),
            ],
            out_specs=pl.BlockSpec((4, 112, HD), lambda i, *_: (head, 0, 0)),
            scratch_shapes=[
                pltpu.VMEM((PAGE * number, HD), BF16),
                pltpu.VMEM((PAGE * number, HD), BF16),
            ],
        ),
        out_shape=jax.ShapeDtypeStruct((16, 112, HD), BF16),
        input_output_aliases={} if head == 0 else {10: 0},
        compiler_params=pltpu.CompilerParams(vmem_limit_bytes=VMEM_LIMIT),
        name=f"attend_{head}",
    )(plan, plan, queries, queries, queries, anchors, anchors, deltas, deltas, scales, after)


def merge_kernel(plan, place, parts, out, level, top, total, numer):
    quarter = 32
    row = lax.broadcasted_iota(I32, (quarter, HD), 0)
    lane = lax.broadcasted_iota(I32, (quarter, HD), 1)
    mine = lane == row + quarter * ((place[0] & 1) * 2 + place[1])
    top[...] = jnp.full(top.shape, LOW, F32)
    total[...] = jnp.zeros(total.shape, F32)
    numer[...] = jnp.zeros(numer.shape, F32)
    for sender in range(16):
        stats = parts[sender, 96:112, :].astype(F32)
        for slot in range(SPAN):
            line = stats[3 * slot : 3 * slot + 1] + (
                stats[3 * slot + 1 : 3 * slot + 2] + stats[3 * slot + 2 : 3 * slot + 3]
            )
            column = jnp.sum(jnp.where(mine, line, 0.0), axis=1, keepdims=True)
            column = jnp.broadcast_to(column, (quarter, HD))
            level[sender * SPAN + slot] = column
            request = plan[3, sender] + slot
            top[request] = jnp.maximum(top[request], column)
    for sender in range(16):
        for slot in range(SPAN):
            request = plan[3, sender] + slot
            weight = jnp.exp(level[sender * SPAN + slot] - top[request])
            mean = parts[sender, slot * quarter : (slot + 1) * quarter, :].astype(F32)
            total[request] += weight
            numer[request] += weight * mean
    for request in range(REQS):
        result = (numer[request] / total[request]).astype(BF16)
        for group in range(4):
            out[request, :, group * HD : (group + 1) * HD] = result[
                group * STEPS : (group + 1) * STEPS
            ]


def merge(plan, place, parts):
    return pl.pallas_call(
        merge_kernel,
        grid_spec=pltpu.PrefetchScalarGridSpec(
            num_scalar_prefetch=2,
            grid=(1,),
            in_specs=[pl.BlockSpec((16, 112, HD), lambda i, *_: (0, 0, 0))],
            out_specs=pl.BlockSpec((REQS, STEPS, 4 * HD), lambda i, *_: (0, 0, 0)),
            scratch_shapes=[
                pltpu.VMEM((16 * SPAN, 32, HD), F32),
                pltpu.VMEM((REQS, 32, HD), F32),
                pltpu.VMEM((REQS, 32, HD), F32),
                pltpu.VMEM((REQS, 32, HD), F32),
            ],
        ),
        out_shape=jax.ShapeDtypeStruct((REQS, STEPS, 4 * HD), BF16),
        compiler_params=pltpu.CompilerParams(vmem_limit_bytes=VMEM_LIMIT),
        name="merge",
    )(plan, place, parts)


def assemble_kernel(flags, blocks, arrived, out, staged, in_sems, out_sems):
    reads, writes = [], []
    for sender in range(16):
        rows = pl.ds(blocks[sender] * PAGE, PAGE)
        source = arrived.at[pl.ds(sender * PAGE, PAGE)]
        reads.append(pltpu.make_async_copy(source, staged.at[rows], in_sems.at[sender]))
        writes.append(pltpu.make_async_copy(staged.at[rows], out.at[rows], out_sems.at[sender]))
    for sender in range(16):
        pl.when(flags[sender] > 0)(reads[sender].start)
    for sender in range(16):

        @pl.when(flags[sender] > 0)
        def forward():
            reads[sender].wait()
            writes[sender].start()

    for sender in range(16):
        pl.when(flags[sender] > 0)(writes[sender].wait)


def assemble(flags, blocks, arrived, number):
    return pl.pallas_call(
        assemble_kernel,
        grid_spec=pltpu.PrefetchScalarGridSpec(
            num_scalar_prefetch=2,
            grid=(1,),
            in_specs=[pl.BlockSpec(memory_space=pl.ANY)],
            out_specs=pl.BlockSpec(memory_space=pl.ANY),
            scratch_shapes=[
                pltpu.VMEM((number, PAGE, KVW), BF16),
                pltpu.SemaphoreType.DMA((16,)),
                pltpu.SemaphoreType.DMA((16,)),
            ],
        ),
        out_shape=jax.ShapeDtypeStruct((number, PAGE, KVW), BF16),
        compiler_params=pltpu.CompilerParams(vmem_limit_bytes=VMEM_LIMIT),
        name="assemble",
    )(flags, blocks, arrived)


ROUNDS = 9
LIMIT = 12
UNIT = 2
LAG = 2
SIDE_LAG = 3
SLOTS = 7
SIDE = (3, 0, 3, 0, 3, 0, 2, 2, 1)
HALF = PAGE // 2
FAR = 1e6


def units_of(port, time):
    if port < 2:
        return UNIT
    return SIDE[time] if time < len(SIDE) else 2


def plan_kernel(place, lengths, owners, out):
    chip = place[0]
    row = lax.broadcasted_iota(I32, (16, 128), 0)
    lanes = lax.broadcasted_iota(I32, (16, 128), 1)
    sender_of = lanes >> 3
    turn = (lanes & 7).astype(F32)
    table = owners[...]
    running = jnp.zeros((16, 1), F32)
    sends = []
    targets = jnp.zeros((16, 128), F32)
    for owner in range(16):
        flag = jnp.max(jnp.where(table == owner, 1.0, 0.0), axis=1, keepdims=True)
        targets += jnp.where(turn == running, flag * owner, 0.0)
        sends.append(flag)
        running = running + flag
    dest = jnp.sum(jnp.where(row == sender_of, targets, 0.0), axis=0, keepdims=True)
    hits = jnp.zeros((16, 128), F32)
    for owner in range(16):
        hits += sends[owner] * jnp.where(dest == owner, 1.0, 0.0)
    rank = jnp.sum(jnp.where(row < sender_of, hits, 0.0), axis=0, keepdims=True).astype(I32)
    dest = dest.astype(I32)
    lane = lax.broadcasted_iota(I32, (1, 128), 1)
    sender = lane >> 3
    from_z, from_x = sender >> 2, (sender >> 1) & 1
    to_z, to_x = dest >> 2, (dest >> 1) & 1
    crosses = (from_z >> 1) != (to_z >> 1)
    below = jnp.where(
        lax.broadcasted_iota(I32, (128, 128), 0) < lax.broadcasted_iota(I32, (128, 128), 1), 1.0, 0.0
    )
    line = from_x
    for side in range(2):
        leaving = crosses & ((from_z >> 1) == side)
        free = jnp.where(leaving & (from_x != to_x), 1.0, 0.0)
        fixed = jnp.where(leaving & (from_x == to_x), 1.0, 0.0)
        tilt = jnp.sum(fixed * (2 * from_x - 1).astype(F32), axis=1, keepdims=True)
        count = jnp.sum(free, axis=1, keepdims=True)
        share = jnp.clip(jnp.floor((tilt + count) * 0.5), 0.0, count)
        step = share / jnp.maximum(count, 1.0)
        index = jnp.dot(jnp.broadcast_to(free, (8, 128)), below, preferred_element_type=F32)[0:1]
        first = jnp.floor((index + 1.0) * step + 1e-3) > jnp.floor(index * step + 1e-3)
        line = jnp.where(free > 0.0, jnp.where(first, 0, 1), line)
    chips = lax.broadcasted_iota(I32, (8, 128), 0)
    mine = lax.broadcasted_iota(I32, (8, 1), 0) == chip

    def round_step(time, carry):
        at_z, at_x, ready, code, steps, needed = carry
        waits = crosses & ((at_z >> 1) == (from_z >> 1))
        turns = ((at_z == to_z) & (at_x != to_x)) | (waits & (line != at_x))
        along = jnp.logical_not(turns) & (at_z != to_z)
        left = jnp.abs(to_z - at_z) + jnp.where(at_x != to_x, 1, 0)
        key = ((8 - left) * 128 + lane).astype(F32)
        here = (at_z * 2 + at_x == chips) & (ready <= time)
        heading = jnp.where(turns, 2, jnp.where(along, jnp.where(to_z > at_z, 0, 1), 3))
        moved = jnp.zeros((1, 128), F32)
        landed = jnp.zeros((1, 128), F32)
        value = (code + 1).astype(F32)
        side = sum(jnp.where(time == t, units_of(2, t), 0) for t in range(LIMIT))
        for port in range(3):
            keys = jnp.where(here & (heading == port), key, FAR)
            for unit in range(UNIT if port < 2 else 3):
                if port == 2:
                    keys = jnp.where(unit < side, keys, FAR)
                least = jnp.min(keys, axis=1, keepdims=True)
                chosen = jnp.where((keys == least) & (keys < FAR), 1.0, 0.0)
                source = jnp.sum(chosen * value, axis=1, keepdims=True)
                source = jnp.sum(jnp.where(mine, source, 0.0), axis=0, keepdims=True)
                slot = SLOTS * time + UNIT * port + unit
                steps = steps + jnp.where(lane == slot, source, 0.0)
                taken = jnp.sum(chosen, axis=0, keepdims=True)
                moved = moved + taken * (port + 1)
                landed = landed + taken * (slot + 16).astype(F32)
                keys = jnp.where(chosen > 0.0, FAR, keys)
        went = moved.astype(I32)
        at_z = at_z + jnp.where(went == 1, 1, 0) - jnp.where(went == 2, 1, 0)
        at_x = jnp.where(went == 3, 1 - at_x, at_x)
        ready = jnp.where(went > 0, time + jnp.where(went == 3, SIDE_LAG, LAG), ready)
        code = jnp.where(went > 0, landed.astype(I32), code)
        any_move = jnp.max(moved, axis=1, keepdims=True)
        needed = jnp.where(any_move > 0.0, (time + 1).astype(F32), needed)
        return at_z, at_x, ready, code, steps, needed

    start = (
        from_z,
        from_x,
        jnp.zeros((1, 128), I32),
        (sender & 1) * 8 + (lane & 7),
        jnp.zeros((1, 128), F32),
        jnp.zeros((1, 1), F32),
    )
    at_z, at_x, ready, code, steps, needed = lax.fori_loop(0, LIMIT, round_step, start)
    undone = jnp.where((at_z == to_z) & (at_x == to_x), 0.0, 1.0)
    undone = jnp.max(undone, axis=1, keepdims=True)
    needed = jnp.where(undone > 0.0, float(LIMIT + 1), needed)
    arrives = (dest >> 1) == chip
    slots = (dest & 1) * 8 + rank
    final = jnp.sum(
        jnp.where((row == slots) & arrives, (code + 1).astype(F32), 0.0), axis=1, keepdims=True
    )
    final = jnp.sum(jnp.where(row == lanes, final, 0.0), axis=0, keepdims=True)
    out[0:1, :] = steps.astype(I32)
    out[1:2, :] = final.astype(I32)
    out[2:3, :] = jnp.broadcast_to(needed, (1, 128)).astype(I32)
    page = (2 * chip + place[1]) * 128 + lane
    requests = jnp.zeros((1, 128), I32)
    bases = jnp.zeros((1, 128), I32)
    end = 0
    for request in range(REQS):
        end = end + lengths[request]
        requests = requests + jnp.where(page >= end, 1, 0)
        bases = bases + jnp.where(lane * 128 >= end, 1, 0)
    bases = jnp.minimum(bases, REQS - SPAN)
    base = jnp.sum(jnp.where(lane == 2 * chip + place[1], bases, 0).astype(F32), axis=1, keepdims=True)
    out[3:4, :] = bases
    out[4:5, :] = requests
    out[5:6, :] = jnp.broadcast_to(base, (1, 128)).astype(I32)
    out[6:8, :] = jnp.zeros((2, 128), I32)


def make_plan(place, lengths, page_owner):
    return pl.pallas_call(
        plan_kernel,
        grid_spec=pltpu.PrefetchScalarGridSpec(
            num_scalar_prefetch=2,
            grid=(1,),
            in_specs=[pl.BlockSpec((16, 128), lambda i, *_: (0, 0))],
            out_specs=pl.BlockSpec((8, 128), lambda i, *_: (0, 0)),
        ),
        out_shape=jax.ShapeDtypeStruct((8, 128), I32),
        name="make_plan",
    )(place, lengths, page_owner.reshape(16, 128))


def halves_kernel(place, owners, anchors, deltas, scales, keep, give, swap, columns, ranks, order, rows, staged, sems):
    step = pl.program_id(0)
    count = PAGE * PAGE

    @pl.when(step == 0)
    def build():
        row = lax.broadcasted_iota(I32, (count, count), 0)
        lane = lax.broadcasted_iota(I32, (count, count), 1)
        swap[...] = jnp.where(lane == (row & 15) * PAGE + (row >> 4), 1.0, 0.0).astype(BF16)
        columns[...] = jnp.transpose(scales[...])
        number = owners.shape[1]
        row = lax.broadcasted_iota(I32, (number, number), 0)
        lane = lax.broadcasted_iota(I32, (number, number), 1)
        across = owners[pl.ds(2 * place[0] + place[1], 1), :].astype(F32)
        down = jnp.sum(jnp.where(row == lane, across, 0.0), axis=1, keepdims=True)
        ahead = (down < across) | ((down == across) & (row < lane))
        ranks[...] = jnp.sum(jnp.where(ahead, 1.0, 0.0), axis=0, keepdims=True).astype(I32)
        pltpu.make_async_copy(ranks, order, sems.at[2]).start()

    core = place[1]
    for part in range(anchors.shape[0] // PAGE):
        pages = slice(part * PAGE, (part + 1) * PAGE)
        for head in range(2 * KVH):
            cols = slice(head * HD, (head + 1) * HD)
            start = pl.multiple_of(step * anchors.shape[0] + part * PAGE, PAGE)
            scale = jnp.broadcast_to(columns[pl.ds(start, PAGE), head : head + 1], (PAGE, HD))
            first = anchors[pages, cols]
            anchor = first.astype(F32)
            rows[0:PAGE, cols] = first
            for token in range(1, PAGE):
                rebuilt = anchor + scale * deltas[token - 1, pages, cols].astype(F32)
                rows[token * PAGE : (token + 1) * PAGE, cols] = rebuilt.astype(BF16)
        turned = jnp.dot(swap[...], rows[...], preferred_element_type=F32).astype(BF16)
        if part == 0:

            @pl.when(step == 0)
            def ordered():
                pltpu.make_async_copy(ranks, order, sems.at[2]).wait()

        for page in range(PAGE):
            rank = order[0, step * anchors.shape[0] + part * PAGE + page]
            half = (rank >> 3) & 1
            slot = (half ^ core) * 64 + (rank >> 4) * HALF + (rank & 7)
            staged[slot] = turned[page * PAGE : (page + 1) * PAGE]

    @pl.when(step == pl.num_programs(0) - 1)
    def flush():
        copies = [
            pltpu.make_async_copy(staged.at[pl.ds(64, 64)], give, sems.at[0]),
            pltpu.make_async_copy(staged.at[pl.ds(0, 64)], keep, sems.at[1]),
        ]
        for copy in copies:
            copy.start()
        for copy in copies:
            copy.wait()


def decode_halves(place, page_owner, anchors, deltas, scales):
    number = anchors.shape[0]
    chunk = 2 * PAGE
    half = jax.ShapeDtypeStruct((number // 2, PAGE, KVW), BF16)
    return pl.pallas_call(
        halves_kernel,
        grid_spec=pltpu.PrefetchScalarGridSpec(
            num_scalar_prefetch=1,
            grid=(number // chunk,),
            in_specs=[
                pl.BlockSpec((16, number), lambda i, *_: (0, 0)),
                pl.BlockSpec((chunk, KVW), lambda i, *_: (i, 0)),
                pl.BlockSpec((PAGE - 1, chunk, KVW), lambda i, *_: (0, i, 0)),
                pl.BlockSpec((2 * KVH, number), lambda i, *_: (0, 0)),
            ],
            out_specs=[pl.BlockSpec(memory_space=pl.ANY)] * 2,
            scratch_shapes=[
                pltpu.VMEM((PAGE * PAGE, PAGE * PAGE), BF16),
                pltpu.VMEM((number, 2 * KVH), F32),
                pltpu.VMEM((1, number), I32),
                pltpu.SMEM((1, number), I32),
                pltpu.VMEM((PAGE * PAGE, KVW), BF16),
                pltpu.VMEM((number, PAGE, KVW), BF16),
                pltpu.SemaphoreType.DMA((3,)),
            ],
        ),
        out_shape=(half, half),
        compiler_params=pltpu.CompilerParams(vmem_limit_bytes=VMEM_LIMIT),
        name="decode_halves",
    )(place, page_owner.reshape(16, number), anchors, deltas, scales)


def fetch(code, core, own, landed, ports, target, sem):
    value = code - 1
    keep, got = own

    @pl.when((value >= 0) & (value < 16))
    def from_own():
        rows = pl.ds((value & 7) * HALF, HALF)

        @pl.when((value >> 3) == core)
        def kept():
            pltpu.make_async_copy(keep.at[rows], target, sem).start()

        @pl.when((value >> 3) != core)
        def gotten():
            pltpu.make_async_copy(got.at[rows], target, sem).start()

    for time, port, arrivals in landed:
        if port in ports:
            offset = value - 16 - SLOTS * time - UNIT * port

            @pl.when((offset >= 0) & (offset < units_of(port, time)))
            def from_round():
                rows = pl.ds(offset * HALF, HALF)
                pltpu.make_async_copy(arrivals.at[rows], target, sem).start()


def settle(code, own, target, sem):
    @pl.when(code > 0)
    def wait():
        pltpu.make_async_copy(own[0].at[pl.ds(0, HALF)], target, sem).wait()


def pick_kernel(time, tags, plan, place, *refs):
    own, landed = refs[:2], [tag + (ref,) for tag, ref in zip(tags, refs[2:])]
    used = [port for port in range(3) if units_of(port, time)]
    outs, sems = refs[-1 - len(used) : -1], refs[-1]
    for phase in range(2):
        for port, out in zip(used, outs):
            ports = (0, 1) if port == 2 else (port, 2)
            for unit in range(units_of(port, time)):
                code = plan[0, SLOTS * time + UNIT * port + unit]
                target = out.at[pl.ds(unit * HALF, HALF)]
                sem = sems.at[UNIT * port + unit]
                if phase == 0:
                    fetch(code, place[1], own, landed, ports, target, sem)
                else:
                    settle(code, own, target, sem)


def pick(time, plan, place, own, landed, after):
    landed = [item for item in landed if item[0] + (SIDE_LAG if item[1] == 2 else LAG) <= time]
    sources = list(own) + [item[2] for item in landed] + [after]
    pieces = [
        jax.ShapeDtypeStruct((units_of(port, time) * HALF, PAGE, KVW), BF16)
        for port in range(3)
        if units_of(port, time)
    ]
    return pl.pallas_call(
        functools.partial(pick_kernel, time, [item[:2] for item in landed]),
        grid_spec=pltpu.PrefetchScalarGridSpec(
            num_scalar_prefetch=2,
            grid=(1,),
            in_specs=[pl.BlockSpec(memory_space=pl.ANY)] * len(sources),
            out_specs=[pl.BlockSpec(piece.shape, lambda i, *_: (0, 0, 0)) for piece in pieces],
            scratch_shapes=[pltpu.SemaphoreType.DMA((SLOTS,))],
        ),
        out_shape=pieces,
        compiler_params=pltpu.CompilerParams(vmem_limit_bytes=VMEM_LIMIT),
        name=f"pick_{time}",
    )(plan, place, *sources)


def known(code, tags):
    return jnp.where(code > 16 + SLOTS * (1 + max(time for time, _ in tags)), 0, code)


def give_kernel(tags, plan, place, *refs):
    own, landed = refs[:2], [tag + (ref,) for tag, ref in zip(tags, refs[2:])]
    out, sems = refs[-2:]
    core = place[1]
    codes = [known(plan[1, (1 - core) * 8 + slot], tags) for slot in range(8)]
    targets = [out.at[pl.ds(slot * HALF, HALF)] for slot in range(8)]
    for slot in range(8):
        fetch(codes[slot], core, own, landed, (0, 1, 2), targets[slot], sems.at[slot])
    for slot in range(8):
        settle(codes[slot], own, targets[slot], sems.at[slot])


def gather_give(plan, place, own, landed, after):
    sources = list(own) + [item[2] for item in landed] + [after]
    shape = (8 * HALF, PAGE, KVW)
    return pl.pallas_call(
        functools.partial(give_kernel, [item[:2] for item in landed]),
        grid_spec=pltpu.PrefetchScalarGridSpec(
            num_scalar_prefetch=2,
            grid=(1,),
            in_specs=[pl.BlockSpec(memory_space=pl.ANY)] * len(sources),
            out_specs=pl.BlockSpec(shape, lambda i, *_: (0, 0, 0)),
            scratch_shapes=[pltpu.SemaphoreType.DMA((8,))],
        ),
        out_shape=jax.ShapeDtypeStruct(shape, BF16),
        compiler_params=pltpu.CompilerParams(vmem_limit_bytes=VMEM_LIMIT),
        name="gather_give",
    )(plan, place, *sources)


def own_kernel(tags, plan, place, *refs):
    own, landed = refs[:2], [tag + (ref,) for tag, ref in zip(tags, refs[2:])]
    out, staged, in_sems, out_sems = refs[-4:]
    core = place[1]
    codes = [known(plan[1, core * 8 + slot], tags) for slot in range(8)]
    targets = [staged.at[pl.ds(slot * HALF, HALF)] for slot in range(8)]
    for slot in range(8):
        fetch(codes[slot], core, own, landed, (0, 1, 2), targets[slot], in_sems.at[slot])
    writes = []
    for slot in range(8):
        start = slot * PAGE + core * HALF
        writes.append(
            pltpu.make_async_copy(targets[slot], out.at[pl.ds(start, HALF)], out_sems.at[slot])
        )
        settle(codes[slot], own, targets[slot], in_sems.at[slot])
        writes[slot].start()
    for write in writes:
        write.wait()


def gather_own(plan, place, own, landed):
    sources = list(own) + [item[2] for item in landed]
    return pl.pallas_call(
        functools.partial(own_kernel, [item[:2] for item in landed]),
        grid_spec=pltpu.PrefetchScalarGridSpec(
            num_scalar_prefetch=2,
            grid=(1,),
            in_specs=[pl.BlockSpec(memory_space=pl.ANY)] * len(sources),
            out_specs=pl.BlockSpec(memory_space=pl.ANY),
            scratch_shapes=[
                pltpu.VMEM((8 * HALF, PAGE, KVW), BF16),
                pltpu.SemaphoreType.DMA((8,)),
                pltpu.SemaphoreType.DMA((8,)),
            ],
        ),
        out_shape=jax.ShapeDtypeStruct((8 * PAGE, PAGE, KVW), BF16),
        compiler_params=pltpu.CompilerParams(vmem_limit_bytes=VMEM_LIMIT),
        name="gather_own",
    )(plan, place, *sources)


def fill_kernel(place, cache, other, out, staged, in_sems, out_sems):
    half = 1 - place[1]
    reads, writes = [], []
    for slot in range(8):
        rows = pl.ds(slot * HALF, HALF)
        reads.append(pltpu.make_async_copy(other.at[rows], staged.at[rows], in_sems.at[slot]))
        writes.append(
            pltpu.make_async_copy(
                staged.at[rows], out.at[pl.ds(slot * PAGE + half * HALF, HALF)], out_sems.at[slot]
            )
        )
    for read in reads:
        read.start()
    for read, write in zip(reads, writes):
        read.wait()
        write.start()
    for write in writes:
        write.wait()


def fill(place, cache, other):
    return pl.pallas_call(
        fill_kernel,
        grid_spec=pltpu.PrefetchScalarGridSpec(
            num_scalar_prefetch=1,
            grid=(1,),
            in_specs=[pl.BlockSpec(memory_space=pl.ANY)] * 2,
            out_specs=pl.BlockSpec(memory_space=pl.ANY),
            scratch_shapes=[
                pltpu.VMEM((8 * HALF, PAGE, KVW), BF16),
                pltpu.SemaphoreType.DMA((8,)),
                pltpu.SemaphoreType.DMA((8,)),
            ],
        ),
        out_shape=jax.ShapeDtypeStruct(cache.shape, cache.dtype),
        input_output_aliases={1: 0},
        compiler_params=pltpu.CompilerParams(vmem_limit_bytes=VMEM_LIMIT),
        name="fill",
    )(place, cache, other)


UP = tuple((i, i + 4) for i in range(12))
DOWN = tuple((i + 4, i) for i in range(12))
ACROSS = tuple((i, i ^ 2) for i in range(16))
TWIN = tuple((i, i ^ 1) for i in range(16))


def ship(time, parts):
    used = [port for port in range(3) if units_of(port, time)]
    hops = (UP, DOWN, ACROSS)
    return [(time, port, lax.ppermute(part, "pool", hops[port])) for port, part in zip(used, parts)]


def finish(plan, place, own, landed, after):
    other = lax.ppermute(gather_give(plan, place, own, landed, after), "pool", TWIN)
    return fill(place, gather_own(plan, place, own, landed), other)


def local_lanes(anchors, deltas, scales, queries, lengths, page_owner):
    position = lax.axis_index("pool")
    number = anchors.shape[0]
    by_token = jnp.transpose(deltas, (1, 0, 2))
    place = jnp.stack([position >> 1, position & 1]).astype(I32)
    lines = jnp.transpose(scales)
    keep, give = decode_halves(place, page_owner, anchors, by_token, lines)
    got = lax.ppermute(give, "pool", TWIN)
    plan = make_plan(place, lengths, page_owner)
    own = (keep, got)
    landed = []
    after = partial = plan
    for time in range(ROUNDS):
        parts = pick(time, plan, place, own, landed, after)
        landed += ship(time, parts)
        after = parts[0]
        if 1 <= time <= KVH:
            seen, _ = lax.optimization_barrier((plan, after))
            after = partial = attend(time - 1, seen, queries, anchors, by_token, lines, partial)
    partial, _ = lax.optimization_barrier((partial, after))
    swapped = lax.all_to_all(partial, "pool", split_axis=0, concat_axis=0, tiled=True)
    attention = merge(plan, place, swapped)
    cache = finish(plan, place, own, landed, attention)

    def in_time(cache):
        return cache

    def late(cache):
        more, last = list(landed), plan
        for time in range(ROUNDS, LIMIT):
            parts = pick(time, plan, place, own, more, last)
            more += ship(time, parts)
            last = parts[0]
        return finish(plan, place, own, more, last)

    def padded(cache):
        owners = lax.dynamic_slice_in_dim(page_owner, position * number, number, 0)
        index = jnp.arange(number, dtype=I32)
        ahead = (owners[None, :] < owners[:, None]) | (
            (owners[None, :] == owners[:, None]) & (index[None, :] < index[:, None])
        )
        order = jnp.sum(ahead.astype(I32), axis=1)
        devices = jnp.arange(16, dtype=I32)
        sent = jnp.any(owners[None, :] == devices[:, None], axis=1).astype(I32)
        slabs = decode_sorted(order, sent, jnp.cumsum(sent) - sent, anchors, by_token, scales)
        arrived = lax.all_to_all(slabs, "pool", split_axis=0, concat_axis=0, tiled=True)
        taken = jnp.any((page_owner == position).reshape(16, number), axis=1).astype(I32)
        return assemble(taken, jnp.cumsum(taken) - taken, arrived, number)

    needed = plan[2, 0]
    branch = (needed > ROUNDS).astype(I32) + (needed > LIMIT).astype(I32)
    branch, attention = lax.optimization_barrier((branch, attention))
    cache = lax.switch(branch, (in_time, late, padded), cache)
    return (cache, attention)


def decode_pages(anchors, deltas, scales):
    block_scale = jnp.repeat(scales, HD, axis=1)
    rebuilt = anchors[:, None, :].astype(jnp.float32) + block_scale[:, None, :] * deltas.astype(
        jnp.float32
    )
    return jnp.concatenate([anchors[:, None, :], rebuilt.astype(jnp.bfloat16)], axis=1)


def page_scores(work_pages, queries, requests):
    number = work_pages.shape[0]
    key_rows = work_pages[:, :, : KVH * HD].reshape(number, PAGE, KVH, HD)
    picked = jnp.take(queries, requests, axis=0).reshape(number, STEPS, KVH, QH // KVH, HD)
    scores = jnp.einsum(
        "nskgd,ntkd->nskgt", picked, key_rows, preferred_element_type=jnp.float32
    ) * HD ** (-0.5)
    return (scores, jnp.max(scores, axis=4))


def accumulate(scores, page_max, work_pages, requests, shift_max):
    number = work_pages.shape[0]
    rows_out = shift_max.shape[0]
    block_size = min(32, number)
    blocks = number // block_size
    value_rows = work_pages[:, :, KVH * HD :].reshape(blocks, block_size, PAGE, KVH, HD)
    score_blocks = scores.reshape((blocks, block_size) + scores.shape[1:])
    max_blocks = page_max.reshape((blocks, block_size) + page_max.shape[1:])
    request_blocks = requests.reshape(blocks, block_size)

    def block_step(running, pieces):
        totals, numerator = running
        block_scores, block_max, block_values, block_requests = pieces
        exponent = jnp.exp(block_scores - block_max[..., None])
        weights = exponent.astype(jnp.bfloat16)
        page_out = jnp.einsum(
            "nskgt,ntkd->nskgd", weights, block_values, preferred_element_type=jnp.float32
        )
        factor = jnp.exp(block_max - jnp.take(shift_max, block_requests, axis=0))
        select = (block_requests[None, :] == jnp.arange(rows_out, dtype=jnp.int32)[:, None]).astype(
            jnp.float32
        )
        spread = select[:, :, None, None, None] * factor[None]
        totals = totals + jnp.sum(spread * jnp.sum(exponent, axis=4)[None], axis=1)
        numerator = numerator + jnp.einsum(
            "rnskg,nskgd->rskgd", spread, page_out, precision=lax.Precision.HIGHEST
        )
        return ((totals, numerator), None)

    start_totals = jnp.zeros(shift_max.shape, jnp.float32)
    start_numer = jnp.zeros(shift_max.shape + (HD,), jnp.float32)
    finals, ignored = lax.scan(
        block_step,
        (start_totals, start_numer),
        (score_blocks, max_blocks, value_rows, request_blocks),
    )
    return finals


def request_of(index, request_ends):
    return jnp.sum((index[:, None] >= request_ends[None, :]).astype(jnp.int32), axis=1)


def local(anchors, deltas, scales, queries, lengths, page_owner):
    devices = lax.axis_size("pool")
    position = lax.axis_index("pool")
    number = anchors.shape[0]
    capacity = max(2, 2 * number // devices)
    pages = decode_pages(anchors, deltas, scales)
    request_ends = jnp.cumsum(lengths)
    owners = lax.dynamic_slice_in_dim(page_owner, position * number, number, 0)
    marked = (owners[:, None] == jnp.arange(devices, dtype=jnp.int32)[None, :]).astype(jnp.int32)
    ranking = jnp.sum((jnp.cumsum(marked, axis=0) - 1) * marked, axis=1)
    slot_ids = owners * capacity + ranking
    matches = slot_ids[None, :] == jnp.arange(devices * capacity, dtype=jnp.int32)[:, None]
    sources = jnp.sum(jnp.where(matches, jnp.arange(number, dtype=jnp.int32)[None, :], 0), axis=1)
    outgoing = jnp.take(pages, sources, axis=0)
    arrived = lax.all_to_all(outgoing, "pool", split_axis=0, concat_axis=0, tiled=True)
    held_pages = jnp.nonzero(page_owner == position, size=number)[0].astype(jnp.int32)
    senders = held_pages // number
    before = jnp.sum((held_pages[None, :] < (senders * number)[:, None]).astype(jnp.int32), axis=1)
    row_ids = senders * capacity + jnp.arange(number, dtype=jnp.int32) - before
    cache = jnp.take(arrived, row_ids, axis=0)
    columns = QH * HD // devices
    requests = request_of(held_pages, request_ends)
    scores, page_max = page_scores(cache, queries, requests)
    onehot = requests[None, :] == jnp.arange(REQS, dtype=jnp.int32)[:, None]
    local_max = jnp.max(jnp.where(onehot[:, :, None, None, None], page_max[None], -1e30), axis=1)
    global_max = lax.pmax(local_max.astype(jnp.bfloat16), "pool").astype(local_max.dtype)
    totals, numerator = accumulate(scores, page_max, cache, requests, global_max)
    summed, numerator = lax.psum((totals, numerator), "pool")
    whole = (numerator / summed[..., None]).reshape(REQS, STEPS, QH * HD)
    result = lax.dynamic_slice_in_dim(whole, position * columns, columns, 2)
    return (cache, result.astype(jnp.bfloat16))


def solution(mesh):
    placed = (
        P(("groups", "pool"), None),
        P(("groups", "pool"), None, None),
        P(("groups", "pool"), None),
        P("groups", None, None),
        P("groups"),
        P("groups"),
    )
    lanes = mesh.shape["pool"] == 16
    return jax.shard_map(
        local_lanes if lanes else local,
        mesh=mesh,
        in_specs=placed,
        out_specs=(P(("groups", "pool"), None, None), P("groups", None, "pool")),
        check_vma=False,
    )
```

```python
import functools
import jax
import jax.numpy as jnp
from jax import lax
from jax.experimental import pallas as pl
from jax.experimental.pallas import tpu as pltpu
from jax.sharding import PartitionSpec as P

QH = 64
KVH = 4
HD = 128
PAGE = 16
STEPS = 8
REQS = 16
KVW = 2 * KVH * HD
SPAN = 3
LOW = -1e30
VMEM_LIMIT = 48 * 1024 * 1024
F32 = jnp.float32
BF16 = jnp.bfloat16
I32 = jnp.int32


def decode_kernel(chunk, place, flags, blocks, anchors, deltas, scales, out, rows, staged, sems):
    step = pl.program_id(0)
    for head in range(2 * KVH):
        cols = slice(head * HD, (head + 1) * HD)
        scale = jnp.broadcast_to(scales[:, head : head + 1], (chunk, HD))
        anchor = anchors[:, cols].astype(F32)
        rows[head * PAGE * chunk : head * PAGE * chunk + chunk, :] = anchor
        for token in range(1, PAGE):
            start = (head * PAGE + token) * chunk
            rows[start : start + chunk, :] = anchor + scale * deltas[token - 1, :, cols].astype(F32)
    for page in range(chunk):
        picked = [
            rows[pl.ds(head * PAGE * chunk + page, PAGE, stride=chunk), :]
            for head in range(2 * KVH)
        ]
        staged[place[step * chunk + page]] = jnp.concatenate(picked, axis=1).astype(BF16)

    @pl.when(step == pl.num_programs(0) - 1)
    def flush():
        copies = []
        for owner in range(16):
            copy = pltpu.make_async_copy(
                staged.at[pl.ds(blocks[owner] * PAGE, PAGE)],
                out.at[pl.ds(owner * PAGE, PAGE)],
                sems.at[owner],
            )
            pl.when(flags[owner] > 0)(copy.start)
            copies.append(copy)
        for owner in range(16):
            pl.when(flags[owner] > 0)(copies[owner].wait)


def decode_sorted(place, flags, blocks, anchors, deltas, scales):
    number = anchors.shape[0]
    chunk = 16
    return pl.pallas_call(
        functools.partial(decode_kernel, chunk),
        grid_spec=pltpu.PrefetchScalarGridSpec(
            num_scalar_prefetch=3,
            grid=(number // chunk,),
            in_specs=[
                pl.BlockSpec((chunk, KVW), lambda i, *_: (i, 0)),
                pl.BlockSpec((PAGE - 1, chunk, KVW), lambda i, *_: (0, i, 0)),
                pl.BlockSpec((chunk, 2 * KVH), lambda i, *_: (i, 0)),
            ],
            out_specs=pl.BlockSpec(memory_space=pl.ANY),
            scratch_shapes=[
                pltpu.VMEM((2 * KVH * PAGE * chunk, HD), F32),
                pltpu.VMEM((number, PAGE, KVW), BF16),
                pltpu.SemaphoreType.DMA((16,)),
            ],
        ),
        out_shape=jax.ShapeDtypeStruct((16 * PAGE, PAGE, KVW), BF16),
        compiler_params=pltpu.CompilerParams(vmem_limit_bytes=VMEM_LIMIT),
        name="decode_sorted",
    )(place, flags, blocks, anchors, deltas, scales)


def attend_kernel(head, plan, requests, first, second, third, key_anchor, val_anchor, key_delta, val_delta, scales, after, out, keys, vals):
    number = key_anchor.shape[0]
    columns = jnp.transpose(scales[...])
    key_scale = columns[:, head : head + 1]
    val_scale = columns[:, head + KVH : head + KVH + 1]
    for anchor, delta, scale, kept in (
        (key_anchor, key_delta, key_scale, keys),
        (val_anchor, val_delta, val_scale, vals),
    ):
        kept[0:number, :] = anchor[...]
        wide = anchor[...].astype(F32)
        for token in range(1, PAGE):
            kept[token * number : (token + 1) * number, :] = (
                wide + scale * delta[token - 1].astype(F32)
            ).astype(BF16)
    token_request = jnp.concatenate([requests[4:5, :]] * PAGE, axis=1) - plan[5, 0]
    rows = STEPS * QH // KVH
    eye = lax.broadcasted_iota(I32, (rows, rows), 0) == lax.broadcasted_iota(I32, (rows, rows), 1)
    pieces = []
    for slot, queries in enumerate((first, second, third)):
        wide = queries[0].astype(F32)
        picked = jnp.concatenate(
            [wide[:, group * HD : (group + 1) * HD] for group in range(QH // KVH)], axis=0
        ).astype(BF16)
        scores = lax.dot_general(
            picked, keys[...], (((1,), (1,)), ((), ())), preferred_element_type=F32
        ) * HD ** (-0.5)
        inside = token_request == slot
        scores = jnp.where(inside, scores, LOW)
        top = jnp.max(scores, axis=1, keepdims=True)
        exponent = jnp.where(inside, jnp.exp(scores - top), 0.0)
        total = jnp.maximum(jnp.sum(exponent, axis=1, keepdims=True), 1e-30)
        numer = jnp.dot(exponent.astype(BF16), vals[...], preferred_element_type=F32)
        mean = (numer * (1.0 / total)).astype(BF16)
        quarter = rows // 4
        for part in range(4):
            out[part, slot * quarter : (slot + 1) * quarter, :] = mean[
                part * quarter : (part + 1) * quarter
            ]
        level = top + jnp.log(total)
        line = jnp.sum(jnp.where(eye, level, 0.0), axis=0, keepdims=True)
        for _ in range(3):
            piece = line.astype(BF16).astype(F32)
            pieces.append(piece)
            line = line - piece
    pieces.append(jnp.zeros((16 - len(pieces), rows), F32))
    stats = jnp.concatenate(pieces, axis=0).astype(BF16)
    for part in range(4):
        out[part, 96:112, :] = stats


def attend(head, plan, queries, anchors, deltas, scales, after):
    number = anchors.shape[0]
    rows = STEPS * QH // KVH
    return pl.pallas_call(
        functools.partial(attend_kernel, head),
        grid_spec=pltpu.PrefetchScalarGridSpec(
            num_scalar_prefetch=1,
            grid=(1,),
            in_specs=[
                pl.BlockSpec((8, number), lambda i, *_: (0, 0)),
                *[
                    pl.BlockSpec((1, STEPS, rows * HD // STEPS), lambda i, p, k=k: (p[5, 0] + k, 0, head))
                    for k in range(SPAN)
                ],
                pl.BlockSpec((number, HD), lambda i, *_: (0, head)),
                pl.BlockSpec((number, HD), lambda i, *_: (0, head + KVH)),
                pl.BlockSpec((PAGE - 1, number, HD), lambda i, *_: (0, 0, head)),
                pl.BlockSpec((PAGE - 1, number, HD), lambda i, *_: (0, 0, head + KVH)),
                pl.BlockSpec((2 * KVH, number), lambda i, *_: (0, 0)),
                pl.BlockSpec(memory_space=pl.ANY),
            ],
            out_specs=pl.BlockSpec((4, 112, HD), lambda i, *_: (head, 0, 0)),
            scratch_shapes=[
                pltpu.VMEM((PAGE * number, HD), BF16),
                pltpu.VMEM((PAGE * number, HD), BF16),
            ],
        ),
        out_shape=jax.ShapeDtypeStruct((16, 112, HD), BF16),
        input_output_aliases={} if head == 0 else {10: 0},
        compiler_params=pltpu.CompilerParams(vmem_limit_bytes=VMEM_LIMIT),
        name=f"attend_{head}",
    )(plan, plan, queries, queries, queries, anchors, anchors, deltas, deltas, scales, after)


def merge_kernel(plan, place, parts, after, out, level, top, total, numer):
    quarter = 32
    row = lax.broadcasted_iota(I32, (quarter, HD), 0)
    lane = lax.broadcasted_iota(I32, (quarter, HD), 1)
    mine = lane == row + quarter * ((place[0] & 1) * 2 + place[1])
    top[...] = jnp.full(top.shape, LOW, F32)
    total[...] = jnp.zeros(total.shape, F32)
    numer[...] = jnp.zeros(numer.shape, F32)
    for sender in range(16):
        stats = parts[sender, 96:112, :].astype(F32)
        for slot in range(SPAN):
            line = stats[3 * slot : 3 * slot + 1] + (
                stats[3 * slot + 1 : 3 * slot + 2] + stats[3 * slot + 2 : 3 * slot + 3]
            )
            column = jnp.sum(jnp.where(mine, line, 0.0), axis=1, keepdims=True)
            column = jnp.broadcast_to(column, (quarter, HD))
            level[sender * SPAN + slot] = column
            request = plan[3, sender] + slot
            top[request] = jnp.maximum(top[request], column)
    for sender in range(16):
        for slot in range(SPAN):
            request = plan[3, sender] + slot
            weight = jnp.exp(level[sender * SPAN + slot] - top[request])
            mean = parts[sender, slot * quarter : (slot + 1) * quarter, :].astype(F32)
            total[request] += weight
            numer[request] += weight * mean
    for request in range(REQS):
        result = (numer[request] / total[request]).astype(BF16)
        for group in range(4):
            out[request, :, group * HD : (group + 1) * HD] = result[
                group * STEPS : (group + 1) * STEPS
            ]


def merge(plan, place, parts, after):
    return pl.pallas_call(
        merge_kernel,
        grid_spec=pltpu.PrefetchScalarGridSpec(
            num_scalar_prefetch=2,
            grid=(1,),
            in_specs=[
                pl.BlockSpec((16, 112, HD), lambda i, *_: (0, 0, 0)),
                pl.BlockSpec(memory_space=pl.ANY),
            ],
            out_specs=pl.BlockSpec((REQS, STEPS, 4 * HD), lambda i, *_: (0, 0, 0)),
            scratch_shapes=[
                pltpu.VMEM((16 * SPAN, 32, HD), F32),
                pltpu.VMEM((REQS, 32, HD), F32),
                pltpu.VMEM((REQS, 32, HD), F32),
                pltpu.VMEM((REQS, 32, HD), F32),
            ],
        ),
        out_shape=jax.ShapeDtypeStruct((REQS, STEPS, 4 * HD), BF16),
        compiler_params=pltpu.CompilerParams(vmem_limit_bytes=VMEM_LIMIT),
        name="merge",
    )(plan, place, parts, after)


def assemble_kernel(flags, blocks, arrived, out, staged, in_sems, out_sems):
    reads, writes = [], []
    for sender in range(16):
        rows = pl.ds(blocks[sender] * PAGE, PAGE)
        source = arrived.at[pl.ds(sender * PAGE, PAGE)]
        reads.append(pltpu.make_async_copy(source, staged.at[rows], in_sems.at[sender]))
        writes.append(pltpu.make_async_copy(staged.at[rows], out.at[rows], out_sems.at[sender]))
    for sender in range(16):
        pl.when(flags[sender] > 0)(reads[sender].start)
    for sender in range(16):

        @pl.when(flags[sender] > 0)
        def forward():
            reads[sender].wait()
            writes[sender].start()

    for sender in range(16):
        pl.when(flags[sender] > 0)(writes[sender].wait)


def assemble(flags, blocks, arrived, number):
    return pl.pallas_call(
        assemble_kernel,
        grid_spec=pltpu.PrefetchScalarGridSpec(
            num_scalar_prefetch=2,
            grid=(1,),
            in_specs=[pl.BlockSpec(memory_space=pl.ANY)],
            out_specs=pl.BlockSpec(memory_space=pl.ANY),
            scratch_shapes=[
                pltpu.VMEM((number, PAGE, KVW), BF16),
                pltpu.SemaphoreType.DMA((16,)),
                pltpu.SemaphoreType.DMA((16,)),
            ],
        ),
        out_shape=jax.ShapeDtypeStruct((number, PAGE, KVW), BF16),
        compiler_params=pltpu.CompilerParams(vmem_limit_bytes=VMEM_LIMIT),
        name="assemble",
    )(flags, blocks, arrived)


ROUNDS = 9
LIMIT = 12
UNIT = 2
LAG = 2
SIDE_LAG = 3
SLOTS = 7
SIDE = (3, 0, 3, 0, 3, 0, 2, 2, 1)
HALF = PAGE // 2
FAR = 1e6


def units_of(port, time):
    if port < 2:
        return UNIT
    return SIDE[time] if time < len(SIDE) else 2


def plan_kernel(place, lengths, owners, out):
    chip = place[0]
    row = lax.broadcasted_iota(I32, (16, 128), 0)
    lanes = lax.broadcasted_iota(I32, (16, 128), 1)
    sender_of = lanes >> 3
    turn = (lanes & 7).astype(F32)
    table = owners[...]
    running = jnp.zeros((16, 1), F32)
    sends = []
    targets = jnp.zeros((16, 128), F32)
    for owner in range(16):
        flag = jnp.max(jnp.where(table == owner, 1.0, 0.0), axis=1, keepdims=True)
        targets += jnp.where(turn == running, flag * owner, 0.0)
        sends.append(flag)
        running = running + flag
    dest = jnp.sum(jnp.where(row == sender_of, targets, 0.0), axis=0, keepdims=True)
    hits = jnp.zeros((16, 128), F32)
    for owner in range(16):
        hits += sends[owner] * jnp.where(dest == owner, 1.0, 0.0)
    rank = jnp.sum(jnp.where(row < sender_of, hits, 0.0), axis=0, keepdims=True).astype(I32)
    dest = dest.astype(I32)
    lane = lax.broadcasted_iota(I32, (1, 128), 1)
    sender = lane >> 3
    from_z, from_x = sender >> 2, (sender >> 1) & 1
    to_z, to_x = dest >> 2, (dest >> 1) & 1
    crosses = (from_z >> 1) != (to_z >> 1)
    below = jnp.where(
        lax.broadcasted_iota(I32, (128, 128), 0) < lax.broadcasted_iota(I32, (128, 128), 1), 1.0, 0.0
    )
    line = from_x
    for side in range(2):
        leaving = crosses & ((from_z >> 1) == side)
        free = jnp.where(leaving & (from_x != to_x), 1.0, 0.0)
        fixed = jnp.where(leaving & (from_x == to_x), 1.0, 0.0)
        tilt = jnp.sum(fixed * (2 * from_x - 1).astype(F32), axis=1, keepdims=True)
        count = jnp.sum(free, axis=1, keepdims=True)
        share = jnp.clip(jnp.floor((tilt + count) * 0.5), 0.0, count)
        step = share / jnp.maximum(count, 1.0)
        index = jnp.dot(jnp.broadcast_to(free, (8, 128)), below, preferred_element_type=F32)[0:1]
        first = jnp.floor((index + 1.0) * step + 1e-3) > jnp.floor(index * step + 1e-3)
        line = jnp.where(free > 0.0, jnp.where(first, 0, 1), line)
    chips = lax.broadcasted_iota(I32, (8, 128), 0)
    mine = lax.broadcasted_iota(I32, (8, 1), 0) == chip

    def round_step(time, carry):
        at_z, at_x, ready, code, steps, needed = carry
        waits = crosses & ((at_z >> 1) == (from_z >> 1))
        turns = ((at_z == to_z) & (at_x != to_x)) | (waits & (line != at_x))
        along = jnp.logical_not(turns) & (at_z != to_z)
        left = jnp.abs(to_z - at_z) + jnp.where(at_x != to_x, 1, 0)
        key = ((8 - left) * 128 + lane).astype(F32)
        here = (at_z * 2 + at_x == chips) & (ready <= time)
        heading = jnp.where(turns, 2, jnp.where(along, jnp.where(to_z > at_z, 0, 1), 3))
        moved = jnp.zeros((1, 128), F32)
        landed = jnp.zeros((1, 128), F32)
        value = (code + 1).astype(F32)
        side = sum(jnp.where(time == t, units_of(2, t), 0) for t in range(LIMIT))
        for port in range(3):
            keys = jnp.where(here & (heading == port), key, FAR)
            for unit in range(UNIT if port < 2 else 3):
                if port == 2:
                    keys = jnp.where(unit < side, keys, FAR)
                least = jnp.min(keys, axis=1, keepdims=True)
                chosen = jnp.where((keys == least) & (keys < FAR), 1.0, 0.0)
                source = jnp.sum(chosen * value, axis=1, keepdims=True)
                source = jnp.sum(jnp.where(mine, source, 0.0), axis=0, keepdims=True)
                slot = SLOTS * time + UNIT * port + unit
                steps = steps + jnp.where(lane == slot, source, 0.0)
                taken = jnp.sum(chosen, axis=0, keepdims=True)
                moved = moved + taken * (port + 1)
                landed = landed + taken * (slot + 16).astype(F32)
                keys = jnp.where(chosen > 0.0, FAR, keys)
        went = moved.astype(I32)
        at_z = at_z + jnp.where(went == 1, 1, 0) - jnp.where(went == 2, 1, 0)
        at_x = jnp.where(went == 3, 1 - at_x, at_x)
        ready = jnp.where(went > 0, time + jnp.where(went == 3, SIDE_LAG, LAG), ready)
        code = jnp.where(went > 0, landed.astype(I32), code)
        any_move = jnp.max(moved, axis=1, keepdims=True)
        needed = jnp.where(any_move > 0.0, (time + 1).astype(F32), needed)
        return at_z, at_x, ready, code, steps, needed

    start = (
        from_z,
        from_x,
        jnp.zeros((1, 128), I32),
        (sender & 1) * 8 + (lane & 7),
        jnp.zeros((1, 128), F32),
        jnp.zeros((1, 1), F32),
    )
    at_z, at_x, ready, code, steps, needed = lax.fori_loop(0, LIMIT, round_step, start)
    undone = jnp.where((at_z == to_z) & (at_x == to_x), 0.0, 1.0)
    undone = jnp.max(undone, axis=1, keepdims=True)
    needed = jnp.where(undone > 0.0, float(LIMIT + 1), needed)
    arrives = (dest >> 1) == chip
    slots = (dest & 1) * 8 + rank
    final = jnp.sum(
        jnp.where((row == slots) & arrives, (code + 1).astype(F32), 0.0), axis=1, keepdims=True
    )
    final = jnp.sum(jnp.where(row == lanes, final, 0.0), axis=0, keepdims=True)
    out[0:1, :] = steps.astype(I32)
    out[1:2, :] = final.astype(I32)
    out[2:3, :] = jnp.broadcast_to(needed, (1, 128)).astype(I32)
    page = (2 * chip + place[1]) * 128 + lane
    requests = jnp.zeros((1, 128), I32)
    bases = jnp.zeros((1, 128), I32)
    end = 0
    for request in range(REQS):
        end = end + lengths[request]
        requests = requests + jnp.where(page >= end, 1, 0)
        bases = bases + jnp.where(lane * 128 >= end, 1, 0)
    bases = jnp.minimum(bases, REQS - SPAN)
    base = jnp.sum(jnp.where(lane == 2 * chip + place[1], bases, 0).astype(F32), axis=1, keepdims=True)
    out[3:4, :] = bases
    out[4:5, :] = requests
    out[5:6, :] = jnp.broadcast_to(base, (1, 128)).astype(I32)
    out[6:8, :] = jnp.zeros((2, 128), I32)


def make_plan(place, lengths, page_owner):
    return pl.pallas_call(
        plan_kernel,
        grid_spec=pltpu.PrefetchScalarGridSpec(
            num_scalar_prefetch=2,
            grid=(1,),
            in_specs=[pl.BlockSpec((16, 128), lambda i, *_: (0, 0))],
            out_specs=pl.BlockSpec((8, 128), lambda i, *_: (0, 0)),
        ),
        out_shape=jax.ShapeDtypeStruct((8, 128), I32),
        name="make_plan",
    )(place, lengths, page_owner.reshape(16, 128))


def halves_kernel(place, owners, anchors, deltas, scales, keep, give, swap, columns, ranks, order, rows, staged, sems):
    step = pl.program_id(0)
    count = PAGE * PAGE

    @pl.when(step == 0)
    def build():
        row = lax.broadcasted_iota(I32, (count, count), 0)
        lane = lax.broadcasted_iota(I32, (count, count), 1)
        swap[...] = jnp.where(lane == (row & 15) * PAGE + (row >> 4), 1.0, 0.0).astype(BF16)
        columns[...] = jnp.transpose(scales[...])
        number = owners.shape[1]
        row = lax.broadcasted_iota(I32, (number, number), 0)
        lane = lax.broadcasted_iota(I32, (number, number), 1)
        across = owners[pl.ds(2 * place[0] + place[1], 1), :].astype(F32)
        down = jnp.sum(jnp.where(row == lane, across, 0.0), axis=1, keepdims=True)
        ahead = (down < across) | ((down == across) & (row < lane))
        ranks[...] = jnp.sum(jnp.where(ahead, 1.0, 0.0), axis=0, keepdims=True).astype(I32)
        pltpu.make_async_copy(ranks, order, sems.at[2]).start()

    core = place[1]
    for part in range(anchors.shape[0] // PAGE):
        pages = slice(part * PAGE, (part + 1) * PAGE)
        for head in range(2 * KVH):
            cols = slice(head * HD, (head + 1) * HD)
            start = pl.multiple_of(step * anchors.shape[0] + part * PAGE, PAGE)
            scale = jnp.broadcast_to(columns[pl.ds(start, PAGE), head : head + 1], (PAGE, HD))
            first = anchors[pages, cols]
            anchor = first.astype(F32)
            rows[0:PAGE, cols] = first
            for token in range(1, PAGE):
                rebuilt = anchor + scale * deltas[token - 1, pages, cols].astype(F32)
                rows[token * PAGE : (token + 1) * PAGE, cols] = rebuilt.astype(BF16)
        turned = jnp.dot(swap[...], rows[...], preferred_element_type=F32).astype(BF16)
        if part == 0:

            @pl.when(step == 0)
            def ordered():
                pltpu.make_async_copy(ranks, order, sems.at[2]).wait()

        for page in range(PAGE):
            rank = order[0, step * anchors.shape[0] + part * PAGE + page]
            half = (rank >> 3) & 1
            slot = (half ^ core) * 64 + (rank >> 4) * HALF + (rank & 7)
            staged[slot] = turned[page * PAGE : (page + 1) * PAGE]

    @pl.when(step == pl.num_programs(0) - 1)
    def flush():
        copies = [
            pltpu.make_async_copy(staged.at[pl.ds(64, 64)], give, sems.at[0]),
            pltpu.make_async_copy(staged.at[pl.ds(0, 64)], keep, sems.at[1]),
        ]
        for copy in copies:
            copy.start()
        for copy in copies:
            copy.wait()


def decode_halves(place, page_owner, anchors, deltas, scales):
    number = anchors.shape[0]
    chunk = 2 * PAGE
    half = jax.ShapeDtypeStruct((number // 2, PAGE, KVW), BF16)
    return pl.pallas_call(
        halves_kernel,
        grid_spec=pltpu.PrefetchScalarGridSpec(
            num_scalar_prefetch=1,
            grid=(number // chunk,),
            in_specs=[
                pl.BlockSpec((16, number), lambda i, *_: (0, 0)),
                pl.BlockSpec((chunk, KVW), lambda i, *_: (i, 0)),
                pl.BlockSpec((PAGE - 1, chunk, KVW), lambda i, *_: (0, i, 0)),
                pl.BlockSpec((2 * KVH, number), lambda i, *_: (0, 0)),
            ],
            out_specs=[pl.BlockSpec(memory_space=pl.ANY)] * 2,
            scratch_shapes=[
                pltpu.VMEM((PAGE * PAGE, PAGE * PAGE), BF16),
                pltpu.VMEM((number, 2 * KVH), F32),
                pltpu.VMEM((1, number), I32),
                pltpu.SMEM((1, number), I32),
                pltpu.VMEM((PAGE * PAGE, KVW), BF16),
                pltpu.VMEM((number, PAGE, KVW), BF16),
                pltpu.SemaphoreType.DMA((3,)),
            ],
        ),
        out_shape=(half, half),
        compiler_params=pltpu.CompilerParams(vmem_limit_bytes=VMEM_LIMIT),
        name="decode_halves",
    )(place, page_owner.reshape(16, number), anchors, deltas, scales)


def fetch(code, core, own, landed, ports, target, sem):
    value = code - 1
    keep, got = own

    @pl.when((value >= 0) & (value < 16))
    def from_own():
        rows = pl.ds((value & 7) * HALF, HALF)

        @pl.when((value >> 3) == core)
        def kept():
            pltpu.make_async_copy(keep.at[rows], target, sem).start()

        @pl.when((value >> 3) != core)
        def gotten():
            pltpu.make_async_copy(got.at[rows], target, sem).start()

    for time, port, arrivals in landed:
        if port in ports:
            offset = value - 16 - SLOTS * time - UNIT * port

            @pl.when((offset >= 0) & (offset < units_of(port, time)))
            def from_round():
                rows = pl.ds(offset * HALF, HALF)
                pltpu.make_async_copy(arrivals.at[rows], target, sem).start()


def settle(code, own, target, sem):
    @pl.when(code > 0)
    def wait():
        pltpu.make_async_copy(own[0].at[pl.ds(0, HALF)], target, sem).wait()


def pick_kernel(time, tags, plan, place, *refs):
    own, landed = refs[:2], [tag + (ref,) for tag, ref in zip(tags, refs[2:])]
    used = [port for port in range(3) if units_of(port, time)]
    outs, sems = refs[-1 - len(used) : -1], refs[-1]
    for phase in range(2):
        for port, out in zip(used, outs):
            ports = (0, 1) if port == 2 else (port, 2)
            for unit in range(units_of(port, time)):
                code = plan[0, SLOTS * time + UNIT * port + unit]
                target = out.at[pl.ds(unit * HALF, HALF)]
                sem = sems.at[UNIT * port + unit]
                if phase == 0:
                    fetch(code, place[1], own, landed, ports, target, sem)
                else:
                    settle(code, own, target, sem)


def pick(time, plan, place, own, landed, after):
    landed = [item for item in landed if item[0] + (SIDE_LAG if item[1] == 2 else LAG) <= time]
    sources = list(own) + [item[2] for item in landed] + [after]
    pieces = [
        jax.ShapeDtypeStruct((units_of(port, time) * HALF, PAGE, KVW), BF16)
        for port in range(3)
        if units_of(port, time)
    ]
    return pl.pallas_call(
        functools.partial(pick_kernel, time, [item[:2] for item in landed]),
        grid_spec=pltpu.PrefetchScalarGridSpec(
            num_scalar_prefetch=2,
            grid=(1,),
            in_specs=[pl.BlockSpec(memory_space=pl.ANY)] * len(sources),
            out_specs=[pl.BlockSpec(piece.shape, lambda i, *_: (0, 0, 0)) for piece in pieces],
            scratch_shapes=[pltpu.SemaphoreType.DMA((SLOTS,))],
        ),
        out_shape=pieces,
        compiler_params=pltpu.CompilerParams(vmem_limit_bytes=VMEM_LIMIT),
        name=f"pick_{time}",
    )(plan, place, *sources)


def gather_kernel(mode, low, tags, plan, place, *refs):
    own, landed = refs[:2], [tag + (ref,) for tag, ref in zip(tags, refs[2:])]
    out, staged, in_sems, out_sems = refs[-4:]
    core = place[1]
    half = core if mode == "own" else 1 - core
    high = 16 + SLOTS * (1 + max(time for time, _ in tags))
    codes = [plan[1, half * 8 + slot] for slot in range(8)]
    codes = [jnp.where((code > low) & (code <= high), code, 0) for code in codes]
    targets = [staged.at[pl.ds(slot * HALF, HALF)] for slot in range(8)]
    for slot in range(8):
        fetch(codes[slot], core, own, landed, (0, 1, 2), targets[slot], in_sems.at[slot])
    writes = []
    for slot in range(8):
        start = slot * PAGE + core * HALF if mode == "own" else slot * HALF
        write = pltpu.make_async_copy(
            targets[slot], out.at[pl.ds(start, HALF)], out_sems.at[slot]
        )
        settle(codes[slot], own, targets[slot], in_sems.at[slot])
        pl.when(codes[slot] > 0)(write.start)
        writes.append(write)
    for slot in range(8):
        pl.when(codes[slot] > 0)(writes[slot].wait)


def gather(mode, low, plan, place, own, landed, after, base=None):
    sources = list(own) + [item[2] for item in landed] + [after]
    if base is not None:
        sources.append(base)
    pages = 8 * (PAGE if mode == "own" else HALF)
    return pl.pallas_call(
        functools.partial(gather_kernel, mode, low, [item[:2] for item in landed]),
        grid_spec=pltpu.PrefetchScalarGridSpec(
            num_scalar_prefetch=2,
            grid=(1,),
            in_specs=[pl.BlockSpec(memory_space=pl.ANY)] * len(sources),
            out_specs=pl.BlockSpec(memory_space=pl.ANY),
            scratch_shapes=[
                pltpu.VMEM((8 * HALF, PAGE, KVW), BF16),
                pltpu.SemaphoreType.DMA((8,)),
                pltpu.SemaphoreType.DMA((8,)),
            ],
        ),
        out_shape=jax.ShapeDtypeStruct((pages, PAGE, KVW), BF16),
        input_output_aliases={} if base is None else {1 + len(sources): 0},
        compiler_params=pltpu.CompilerParams(vmem_limit_bytes=VMEM_LIMIT),
        name=f"gather_{mode}",
    )(plan, place, *sources)


def fill_kernel(place, cache, other, out, staged, in_sems, out_sems):
    half = 1 - place[1]
    reads, writes = [], []
    for slot in range(8):
        rows = pl.ds(slot * HALF, HALF)
        reads.append(pltpu.make_async_copy(other.at[rows], staged.at[rows], in_sems.at[slot]))
        writes.append(
            pltpu.make_async_copy(
                staged.at[rows], out.at[pl.ds(slot * PAGE + half * HALF, HALF)], out_sems.at[slot]
            )
        )
    for read in reads:
        read.start()
    for read, write in zip(reads, writes):
        read.wait()
        write.start()
    for write in writes:
        write.wait()


def fill(place, cache, other):
    return pl.pallas_call(
        fill_kernel,
        grid_spec=pltpu.PrefetchScalarGridSpec(
            num_scalar_prefetch=1,
            grid=(1,),
            in_specs=[pl.BlockSpec(memory_space=pl.ANY)] * 2,
            out_specs=pl.BlockSpec(memory_space=pl.ANY),
            scratch_shapes=[
                pltpu.VMEM((8 * HALF, PAGE, KVW), BF16),
                pltpu.SemaphoreType.DMA((8,)),
                pltpu.SemaphoreType.DMA((8,)),
            ],
        ),
        out_shape=jax.ShapeDtypeStruct(cache.shape, cache.dtype),
        input_output_aliases={1: 0},
        compiler_params=pltpu.CompilerParams(vmem_limit_bytes=VMEM_LIMIT),
        name="fill",
    )(place, cache, other)


UP = tuple((i, i + 4) for i in range(12))
DOWN = tuple((i + 4, i) for i in range(12))
ACROSS = tuple((i, i ^ 2) for i in range(16))
TWIN = tuple((i, i ^ 1) for i in range(16))


def ship(time, parts):
    used = [port for port in range(3) if units_of(port, time)]
    hops = (UP, DOWN, ACROSS)
    return [(time, port, lax.ppermute(part, "pool", hops[port])) for port, part in zip(used, parts)]


def finish(plan, place, own, landed, after):
    give = gather("give", 0, plan, place, own, landed, after)
    other = lax.ppermute(give, "pool", TWIN)
    return fill(place, gather("own", 0, plan, place, own, landed, give), other)


def finish_in_two(plan, place, own, landed, after):
    early = [item for item in landed if item[0] < ROUNDS - 1]
    last = [item for item in landed if item[0] >= ROUNDS - 1]
    low = 16 + SLOTS * (ROUNDS - 1)
    give = gather("give", 0, plan, place, own, early, after)
    keep = gather("own", 0, plan, place, own, early, after)
    give = gather("give", low, plan, place, own, last, keep, give)
    other = lax.ppermute(give, "pool", TWIN)
    return fill(place, gather("own", low, plan, place, own, last, give, keep), other)


def local_lanes(anchors, deltas, scales, queries, lengths, page_owner):
    position = lax.axis_index("pool")
    number = anchors.shape[0]
    by_token = jnp.transpose(deltas, (1, 0, 2))
    place = jnp.stack([position >> 1, position & 1]).astype(I32)
    lines = jnp.transpose(scales)
    keep, give = decode_halves(place, page_owner, anchors, by_token, lines)
    got = lax.ppermute(give, "pool", TWIN)
    plan = make_plan(place, lengths, page_owner)
    own = (keep, got)
    landed = []
    after = partial = plan
    for time in range(ROUNDS):
        if time == ROUNDS - 2:
            swapped = lax.all_to_all(partial, "pool", split_axis=0, concat_axis=0, tiled=True)
            after = attention = merge(plan, place, swapped, after)
        parts = pick(time, plan, place, own, landed, after)
        landed += ship(time, parts)
        after = parts[0]
        if 1 <= time <= KVH:
            seen, _ = lax.optimization_barrier((plan, after))
            after = partial = attend(time - 1, seen, queries, anchors, by_token, lines, partial)
    cache = finish_in_two(plan, place, own, landed, after)

    def in_time(cache):
        return cache

    def late(cache):
        more, last = list(landed), plan
        for time in range(ROUNDS, LIMIT):
            parts = pick(time, plan, place, own, more, last)
            more += ship(time, parts)
            last = parts[0]
        return finish(plan, place, own, more, last)

    def padded(cache):
        owners = lax.dynamic_slice_in_dim(page_owner, position * number, number, 0)
        index = jnp.arange(number, dtype=I32)
        ahead = (owners[None, :] < owners[:, None]) | (
            (owners[None, :] == owners[:, None]) & (index[None, :] < index[:, None])
        )
        order = jnp.sum(ahead.astype(I32), axis=1)
        devices = jnp.arange(16, dtype=I32)
        sent = jnp.any(owners[None, :] == devices[:, None], axis=1).astype(I32)
        slabs = decode_sorted(order, sent, jnp.cumsum(sent) - sent, anchors, by_token, scales)
        arrived = lax.all_to_all(slabs, "pool", split_axis=0, concat_axis=0, tiled=True)
        taken = jnp.any((page_owner == position).reshape(16, number), axis=1).astype(I32)
        return assemble(taken, jnp.cumsum(taken) - taken, arrived, number)

    needed = plan[2, 0]
    branch = (needed > ROUNDS).astype(I32) + (needed > LIMIT).astype(I32)
    cache = lax.switch(branch, (in_time, late, padded), cache)
    return (cache, attention)


def decode_pages(anchors, deltas, scales):
    block_scale = jnp.repeat(scales, HD, axis=1)
    rebuilt = anchors[:, None, :].astype(jnp.float32) + block_scale[:, None, :] * deltas.astype(
        jnp.float32
    )
    return jnp.concatenate([anchors[:, None, :], rebuilt.astype(jnp.bfloat16)], axis=1)


def page_scores(work_pages, queries, requests):
    number = work_pages.shape[0]
    key_rows = work_pages[:, :, : KVH * HD].reshape(number, PAGE, KVH, HD)
    picked = jnp.take(queries, requests, axis=0).reshape(number, STEPS, KVH, QH // KVH, HD)
    scores = jnp.einsum(
        "nskgd,ntkd->nskgt", picked, key_rows, preferred_element_type=jnp.float32
    ) * HD ** (-0.5)
    return (scores, jnp.max(scores, axis=4))


def accumulate(scores, page_max, work_pages, requests, shift_max):
    number = work_pages.shape[0]
    rows_out = shift_max.shape[0]
    block_size = min(32, number)
    blocks = number // block_size
    value_rows = work_pages[:, :, KVH * HD :].reshape(blocks, block_size, PAGE, KVH, HD)
    score_blocks = scores.reshape((blocks, block_size) + scores.shape[1:])
    max_blocks = page_max.reshape((blocks, block_size) + page_max.shape[1:])
    request_blocks = requests.reshape(blocks, block_size)

    def block_step(running, pieces):
        totals, numerator = running
        block_scores, block_max, block_values, block_requests = pieces
        exponent = jnp.exp(block_scores - block_max[..., None])
        weights = exponent.astype(jnp.bfloat16)
        page_out = jnp.einsum(
            "nskgt,ntkd->nskgd", weights, block_values, preferred_element_type=jnp.float32
        )
        factor = jnp.exp(block_max - jnp.take(shift_max, block_requests, axis=0))
        select = (block_requests[None, :] == jnp.arange(rows_out, dtype=jnp.int32)[:, None]).astype(
            jnp.float32
        )
        spread = select[:, :, None, None, None] * factor[None]
        totals = totals + jnp.sum(spread * jnp.sum(exponent, axis=4)[None], axis=1)
        numerator = numerator + jnp.einsum(
            "rnskg,nskgd->rskgd", spread, page_out, precision=lax.Precision.HIGHEST
        )
        return ((totals, numerator), None)

    start_totals = jnp.zeros(shift_max.shape, jnp.float32)
    start_numer = jnp.zeros(shift_max.shape + (HD,), jnp.float32)
    finals, ignored = lax.scan(
        block_step,
        (start_totals, start_numer),
        (score_blocks, max_blocks, value_rows, request_blocks),
    )
    return finals


def request_of(index, request_ends):
    return jnp.sum((index[:, None] >= request_ends[None, :]).astype(jnp.int32), axis=1)


def local(anchors, deltas, scales, queries, lengths, page_owner):
    devices = lax.axis_size("pool")
    position = lax.axis_index("pool")
    number = anchors.shape[0]
    capacity = max(2, 2 * number // devices)
    pages = decode_pages(anchors, deltas, scales)
    request_ends = jnp.cumsum(lengths)
    owners = lax.dynamic_slice_in_dim(page_owner, position * number, number, 0)
    marked = (owners[:, None] == jnp.arange(devices, dtype=jnp.int32)[None, :]).astype(jnp.int32)
    ranking = jnp.sum((jnp.cumsum(marked, axis=0) - 1) * marked, axis=1)
    slot_ids = owners * capacity + ranking
    matches = slot_ids[None, :] == jnp.arange(devices * capacity, dtype=jnp.int32)[:, None]
    sources = jnp.sum(jnp.where(matches, jnp.arange(number, dtype=jnp.int32)[None, :], 0), axis=1)
    outgoing = jnp.take(pages, sources, axis=0)
    arrived = lax.all_to_all(outgoing, "pool", split_axis=0, concat_axis=0, tiled=True)
    held_pages = jnp.nonzero(page_owner == position, size=number)[0].astype(jnp.int32)
    senders = held_pages // number
    before = jnp.sum((held_pages[None, :] < (senders * number)[:, None]).astype(jnp.int32), axis=1)
    row_ids = senders * capacity + jnp.arange(number, dtype=jnp.int32) - before
    cache = jnp.take(arrived, row_ids, axis=0)
    columns = QH * HD // devices
    requests = request_of(held_pages, request_ends)
    scores, page_max = page_scores(cache, queries, requests)
    onehot = requests[None, :] == jnp.arange(REQS, dtype=jnp.int32)[:, None]
    local_max = jnp.max(jnp.where(onehot[:, :, None, None, None], page_max[None], -1e30), axis=1)
    global_max = lax.pmax(local_max.astype(jnp.bfloat16), "pool").astype(local_max.dtype)
    totals, numerator = accumulate(scores, page_max, cache, requests, global_max)
    summed, numerator = lax.psum((totals, numerator), "pool")
    whole = (numerator / summed[..., None]).reshape(REQS, STEPS, QH * HD)
    result = lax.dynamic_slice_in_dim(whole, position * columns, columns, 2)
    return (cache, result.astype(jnp.bfloat16))


def solution(mesh):
    placed = (
        P(("groups", "pool"), None),
        P(("groups", "pool"), None, None),
        P(("groups", "pool"), None),
        P("groups", None, None),
        P("groups"),
        P("groups"),
    )
    lanes = mesh.shape["pool"] == 16
    return jax.shard_map(
        local_lanes if lanes else local,
        mesh=mesh,
        in_specs=placed,
        out_specs=(P(("groups", "pool"), None, None), P("groups", None, "pool")),
        check_vma=False,
    )
```

```python
import functools
import jax
import jax.numpy as jnp
from jax import lax
from jax.experimental import pallas as pl
from jax.experimental.pallas import tpu as pltpu
from jax.sharding import PartitionSpec as P

QH = 64
KVH = 4
HD = 128
PAGE = 16
STEPS = 8
REQS = 16
KVW = 2 * KVH * HD
SPAN = 3
LOW = -1e30
VMEM_LIMIT = 48 * 1024 * 1024
F32 = jnp.float32
BF16 = jnp.bfloat16
I32 = jnp.int32


def decode_kernel(chunk, place, flags, blocks, anchors, deltas, scales, out, rows, staged, sems):
    step = pl.program_id(0)
    for head in range(2 * KVH):
        cols = slice(head * HD, (head + 1) * HD)
        scale = jnp.broadcast_to(scales[:, head : head + 1], (chunk, HD))
        anchor = anchors[:, cols].astype(F32)
        rows[head * PAGE * chunk : head * PAGE * chunk + chunk, :] = anchor
        for token in range(1, PAGE):
            start = (head * PAGE + token) * chunk
            rows[start : start + chunk, :] = anchor + scale * deltas[token - 1, :, cols].astype(F32)
    for page in range(chunk):
        picked = [
            rows[pl.ds(head * PAGE * chunk + page, PAGE, stride=chunk), :]
            for head in range(2 * KVH)
        ]
        staged[place[step * chunk + page]] = jnp.concatenate(picked, axis=1).astype(BF16)

    @pl.when(step == pl.num_programs(0) - 1)
    def flush():
        copies = []
        for owner in range(16):
            copy = pltpu.make_async_copy(
                staged.at[pl.ds(blocks[owner] * PAGE, PAGE)],
                out.at[pl.ds(owner * PAGE, PAGE)],
                sems.at[owner],
            )
            pl.when(flags[owner] > 0)(copy.start)
            copies.append(copy)
        for owner in range(16):
            pl.when(flags[owner] > 0)(copies[owner].wait)


def decode_sorted(place, flags, blocks, anchors, deltas, scales):
    number = anchors.shape[0]
    chunk = 16
    return pl.pallas_call(
        functools.partial(decode_kernel, chunk),
        grid_spec=pltpu.PrefetchScalarGridSpec(
            num_scalar_prefetch=3,
            grid=(number // chunk,),
            in_specs=[
                pl.BlockSpec((chunk, KVW), lambda i, *_: (i, 0)),
                pl.BlockSpec((PAGE - 1, chunk, KVW), lambda i, *_: (0, i, 0)),
                pl.BlockSpec((chunk, 2 * KVH), lambda i, *_: (i, 0)),
            ],
            out_specs=pl.BlockSpec(memory_space=pl.ANY),
            scratch_shapes=[
                pltpu.VMEM((2 * KVH * PAGE * chunk, HD), F32),
                pltpu.VMEM((number, PAGE, KVW), BF16),
                pltpu.SemaphoreType.DMA((16,)),
            ],
        ),
        out_shape=jax.ShapeDtypeStruct((16 * PAGE, PAGE, KVW), BF16),
        compiler_params=pltpu.CompilerParams(vmem_limit_bytes=VMEM_LIMIT),
        name="decode_sorted",
    )(place, flags, blocks, anchors, deltas, scales)


def attend_kernel(head, plan, requests, first, second, third, key_anchor, val_anchor, key_delta, val_delta, scales, after, out, keys, vals):
    number = key_anchor.shape[0]
    columns = jnp.transpose(scales[...])
    key_scale = columns[:, head : head + 1]
    val_scale = columns[:, head + KVH : head + KVH + 1]
    for anchor, delta, scale, kept in (
        (key_anchor, key_delta, key_scale, keys),
        (val_anchor, val_delta, val_scale, vals),
    ):
        kept[0:number, :] = anchor[...]
        wide = anchor[...].astype(F32)
        for token in range(1, PAGE):
            kept[token * number : (token + 1) * number, :] = (
                wide + scale * delta[token - 1].astype(F32)
            ).astype(BF16)
    token_request = jnp.concatenate([requests[4:5, :]] * PAGE, axis=1) - plan[5, 0]
    rows = STEPS * QH // KVH
    eye = lax.broadcasted_iota(I32, (rows, rows), 0) == lax.broadcasted_iota(I32, (rows, rows), 1)
    pieces = []
    for slot, queries in enumerate((first, second, third)):
        wide = queries[0].astype(F32)
        picked = jnp.concatenate(
            [wide[:, group * HD : (group + 1) * HD] for group in range(QH // KVH)], axis=0
        ).astype(BF16)
        scores = lax.dot_general(
            picked, keys[...], (((1,), (1,)), ((), ())), preferred_element_type=F32
        ) * HD ** (-0.5)
        inside = token_request == slot
        scores = jnp.where(inside, scores, LOW)
        top = jnp.max(scores, axis=1, keepdims=True)
        exponent = jnp.where(inside, jnp.exp(scores - top), 0.0)
        total = jnp.maximum(jnp.sum(exponent, axis=1, keepdims=True), 1e-30)
        numer = jnp.dot(exponent.astype(BF16), vals[...], preferred_element_type=F32)
        mean = (numer * (1.0 / total)).astype(BF16)
        quarter = rows // 4
        for part in range(4):
            out[part, slot * quarter : (slot + 1) * quarter, :] = mean[
                part * quarter : (part + 1) * quarter
            ]
        level = top + jnp.log(total)
        line = jnp.sum(jnp.where(eye, level, 0.0), axis=0, keepdims=True)
        for _ in range(3):
            piece = line.astype(BF16).astype(F32)
            pieces.append(piece)
            line = line - piece
    pieces.append(jnp.zeros((16 - len(pieces), rows), F32))
    stats = jnp.concatenate(pieces, axis=0).astype(BF16)
    for part in range(4):
        out[part, 96:112, :] = stats


def attend(head, plan, queries, anchors, deltas, scales, after):
    number = anchors.shape[0]
    rows = STEPS * QH // KVH
    return pl.pallas_call(
        functools.partial(attend_kernel, head),
        grid_spec=pltpu.PrefetchScalarGridSpec(
            num_scalar_prefetch=1,
            grid=(1,),
            in_specs=[
                pl.BlockSpec((8, number), lambda i, *_: (0, 0)),
                *[
                    pl.BlockSpec((1, STEPS, rows * HD // STEPS), lambda i, p, k=k: (p[5, 0] + k, 0, head))
                    for k in range(SPAN)
                ],
                pl.BlockSpec((number, HD), lambda i, *_: (0, head)),
                pl.BlockSpec((number, HD), lambda i, *_: (0, head + KVH)),
                pl.BlockSpec((PAGE - 1, number, HD), lambda i, *_: (0, 0, head)),
                pl.BlockSpec((PAGE - 1, number, HD), lambda i, *_: (0, 0, head + KVH)),
                pl.BlockSpec((2 * KVH, number), lambda i, *_: (0, 0)),
                pl.BlockSpec(memory_space=pl.ANY),
            ],
            out_specs=pl.BlockSpec((4, 112, HD), lambda i, *_: (head, 0, 0)),
            scratch_shapes=[
                pltpu.VMEM((PAGE * number, HD), BF16),
                pltpu.VMEM((PAGE * number, HD), BF16),
            ],
        ),
        out_shape=jax.ShapeDtypeStruct((16, 112, HD), BF16),
        input_output_aliases={} if head == 0 else {10: 0},
        compiler_params=pltpu.CompilerParams(vmem_limit_bytes=VMEM_LIMIT),
        name=f"attend_{head}",
    )(plan, plan, queries, queries, queries, anchors, anchors, deltas, deltas, scales, after)


def merge_kernel(plan, place, parts, after, out, level, top, total, numer):
    quarter = 32
    row = lax.broadcasted_iota(I32, (quarter, HD), 0)
    lane = lax.broadcasted_iota(I32, (quarter, HD), 1)
    mine = lane == row + quarter * ((place[0] & 1) * 2 + place[1])
    top[...] = jnp.full(top.shape, LOW, F32)
    total[...] = jnp.zeros(total.shape, F32)
    numer[...] = jnp.zeros(numer.shape, F32)
    for sender in range(16):
        stats = parts[sender, 96:112, :].astype(F32)
        for slot in range(SPAN):
            line = stats[3 * slot : 3 * slot + 1] + (
                stats[3 * slot + 1 : 3 * slot + 2] + stats[3 * slot + 2 : 3 * slot + 3]
            )
            column = jnp.sum(jnp.where(mine, line, 0.0), axis=1, keepdims=True)
            column = jnp.broadcast_to(column, (quarter, HD))
            level[sender * SPAN + slot] = column
            request = plan[3, sender] + slot
            top[request] = jnp.maximum(top[request], column)
    for sender in range(16):
        for slot in range(SPAN):
            request = plan[3, sender] + slot
            weight = jnp.exp(level[sender * SPAN + slot] - top[request])
            mean = parts[sender, slot * quarter : (slot + 1) * quarter, :].astype(F32)
            total[request] += weight
            numer[request] += weight * mean
    for request in range(REQS):
        result = (numer[request] / total[request]).astype(BF16)
        for group in range(4):
            out[request, :, group * HD : (group + 1) * HD] = result[
                group * STEPS : (group + 1) * STEPS
            ]


def merge(plan, place, parts, after):
    return pl.pallas_call(
        merge_kernel,
        grid_spec=pltpu.PrefetchScalarGridSpec(
            num_scalar_prefetch=2,
            grid=(1,),
            in_specs=[
                pl.BlockSpec((16, 112, HD), lambda i, *_: (0, 0, 0)),
                pl.BlockSpec(memory_space=pl.ANY),
            ],
            out_specs=pl.BlockSpec((REQS, STEPS, 4 * HD), lambda i, *_: (0, 0, 0)),
            scratch_shapes=[
                pltpu.VMEM((16 * SPAN, 32, HD), F32),
                pltpu.VMEM((REQS, 32, HD), F32),
                pltpu.VMEM((REQS, 32, HD), F32),
                pltpu.VMEM((REQS, 32, HD), F32),
            ],
        ),
        out_shape=jax.ShapeDtypeStruct((REQS, STEPS, 4 * HD), BF16),
        compiler_params=pltpu.CompilerParams(vmem_limit_bytes=VMEM_LIMIT),
        name="merge",
    )(plan, place, parts, after)


def assemble_kernel(flags, blocks, arrived, out, staged, in_sems, out_sems):
    reads, writes = [], []
    for sender in range(16):
        rows = pl.ds(blocks[sender] * PAGE, PAGE)
        source = arrived.at[pl.ds(sender * PAGE, PAGE)]
        reads.append(pltpu.make_async_copy(source, staged.at[rows], in_sems.at[sender]))
        writes.append(pltpu.make_async_copy(staged.at[rows], out.at[rows], out_sems.at[sender]))
    for sender in range(16):
        pl.when(flags[sender] > 0)(reads[sender].start)
    for sender in range(16):

        @pl.when(flags[sender] > 0)
        def forward():
            reads[sender].wait()
            writes[sender].start()

    for sender in range(16):
        pl.when(flags[sender] > 0)(writes[sender].wait)


def assemble(flags, blocks, arrived, number):
    return pl.pallas_call(
        assemble_kernel,
        grid_spec=pltpu.PrefetchScalarGridSpec(
            num_scalar_prefetch=2,
            grid=(1,),
            in_specs=[pl.BlockSpec(memory_space=pl.ANY)],
            out_specs=pl.BlockSpec(memory_space=pl.ANY),
            scratch_shapes=[
                pltpu.VMEM((number, PAGE, KVW), BF16),
                pltpu.SemaphoreType.DMA((16,)),
                pltpu.SemaphoreType.DMA((16,)),
            ],
        ),
        out_shape=jax.ShapeDtypeStruct((number, PAGE, KVW), BF16),
        compiler_params=pltpu.CompilerParams(vmem_limit_bytes=VMEM_LIMIT),
        name="assemble",
    )(flags, blocks, arrived)


ROUNDS = 9
LIMIT = 12
UNIT = 2
LAG = 2
SIDE_LAG = 3
SLOTS = 7
SIDE = (3, 0, 3, 0, 3, 0, 2, 2, 1)
HALF = PAGE // 2
FAR = 1e6


def units_of(port, time):
    if port < 2:
        return UNIT
    return SIDE[time] if time < len(SIDE) else 2


def plan_kernel(place, lengths, owners, out):
    chip = place[0]
    row = lax.broadcasted_iota(I32, (16, 128), 0)
    lanes = lax.broadcasted_iota(I32, (16, 128), 1)
    sender_of = lanes >> 3
    turn = (lanes & 7).astype(F32)
    table = owners[...]
    running = jnp.zeros((16, 1), F32)
    sends = []
    targets = jnp.zeros((16, 128), F32)
    for owner in range(16):
        flag = jnp.max(jnp.where(table == owner, 1.0, 0.0), axis=1, keepdims=True)
        targets += jnp.where(turn == running, flag * owner, 0.0)
        sends.append(flag)
        running = running + flag
    dest = jnp.sum(jnp.where(row == sender_of, targets, 0.0), axis=0, keepdims=True)
    hits = jnp.zeros((16, 128), F32)
    for owner in range(16):
        hits += sends[owner] * jnp.where(dest == owner, 1.0, 0.0)
    rank = jnp.sum(jnp.where(row < sender_of, hits, 0.0), axis=0, keepdims=True).astype(I32)
    dest = dest.astype(I32)
    lane = lax.broadcasted_iota(I32, (1, 128), 1)
    sender = lane >> 3
    from_z, from_x = sender >> 2, (sender >> 1) & 1
    to_z, to_x = dest >> 2, (dest >> 1) & 1
    crosses = (from_z >> 1) != (to_z >> 1)
    below = jnp.where(
        lax.broadcasted_iota(I32, (128, 128), 0) < lax.broadcasted_iota(I32, (128, 128), 1), 1.0, 0.0
    )
    line = from_x
    for side in range(2):
        leaving = crosses & ((from_z >> 1) == side)
        free = jnp.where(leaving & (from_x != to_x), 1.0, 0.0)
        fixed = jnp.where(leaving & (from_x == to_x), 1.0, 0.0)
        tilt = jnp.sum(fixed * (2 * from_x - 1).astype(F32), axis=1, keepdims=True)
        count = jnp.sum(free, axis=1, keepdims=True)
        share = jnp.clip(jnp.floor((tilt + count) * 0.5), 0.0, count)
        step = share / jnp.maximum(count, 1.0)
        index = jnp.dot(jnp.broadcast_to(free, (8, 128)), below, preferred_element_type=F32)[0:1]
        first = jnp.floor((index + 1.0) * step + 1e-3) > jnp.floor(index * step + 1e-3)
        line = jnp.where(free > 0.0, jnp.where(first, 0, 1), line)
    chips = lax.broadcasted_iota(I32, (8, 128), 0)
    mine = lax.broadcasted_iota(I32, (8, 1), 0) == chip

    def round_step(time, carry):
        at_z, at_x, ready, code, steps, needed = carry
        waits = crosses & ((at_z >> 1) == (from_z >> 1))
        turns = ((at_z == to_z) & (at_x != to_x)) | (waits & (line != at_x))
        along = jnp.logical_not(turns) & (at_z != to_z)
        left = jnp.abs(to_z - at_z) + jnp.where(at_x != to_x, 1, 0)
        key = ((8 - left) * 128 + lane).astype(F32)
        here = (at_z * 2 + at_x == chips) & (ready <= time)
        heading = jnp.where(turns, 2, jnp.where(along, jnp.where(to_z > at_z, 0, 1), 3))
        moved = jnp.zeros((1, 128), F32)
        landed = jnp.zeros((1, 128), F32)
        value = (code + 1).astype(F32)
        side = sum(jnp.where(time == t, units_of(2, t), 0) for t in range(LIMIT))
        for port in range(3):
            keys = jnp.where(here & (heading == port), key, FAR)
            for unit in range(UNIT if port < 2 else 3):
                if port == 2:
                    keys = jnp.where(unit < side, keys, FAR)
                least = jnp.min(keys, axis=1, keepdims=True)
                chosen = jnp.where((keys == least) & (keys < FAR), 1.0, 0.0)
                source = jnp.sum(chosen * value, axis=1, keepdims=True)
                source = jnp.sum(jnp.where(mine, source, 0.0), axis=0, keepdims=True)
                slot = SLOTS * time + UNIT * port + unit
                steps = steps + jnp.where(lane == slot, source, 0.0)
                taken = jnp.sum(chosen, axis=0, keepdims=True)
                moved = moved + taken * (port + 1)
                landed = landed + taken * (slot + 16).astype(F32)
                keys = jnp.where(chosen > 0.0, FAR, keys)
        went = moved.astype(I32)
        at_z = at_z + jnp.where(went == 1, 1, 0) - jnp.where(went == 2, 1, 0)
        at_x = jnp.where(went == 3, 1 - at_x, at_x)
        ready = jnp.where(went > 0, time + jnp.where(went == 3, SIDE_LAG, LAG), ready)
        code = jnp.where(went > 0, landed.astype(I32), code)
        any_move = jnp.max(moved, axis=1, keepdims=True)
        needed = jnp.where(any_move > 0.0, (time + 1).astype(F32), needed)
        return at_z, at_x, ready, code, steps, needed

    start = (
        from_z,
        from_x,
        jnp.zeros((1, 128), I32),
        (sender & 1) * 8 + (lane & 7),
        jnp.zeros((1, 128), F32),
        jnp.zeros((1, 1), F32),
    )
    at_z, at_x, ready, code, steps, needed = lax.fori_loop(0, LIMIT, round_step, start)
    undone = jnp.where((at_z == to_z) & (at_x == to_x), 0.0, 1.0)
    undone = jnp.max(undone, axis=1, keepdims=True)
    needed = jnp.where(undone > 0.0, float(LIMIT + 1), needed)
    arrives = (dest >> 1) == chip
    slots = (dest & 1) * 8 + rank
    final = jnp.sum(
        jnp.where((row == slots) & arrives, (code + 1).astype(F32), 0.0), axis=1, keepdims=True
    )
    final = jnp.sum(jnp.where(row == lanes, final, 0.0), axis=0, keepdims=True)
    out[0:1, :] = steps.astype(I32)
    out[1:2, :] = final.astype(I32)
    out[2:3, :] = jnp.broadcast_to(needed, (1, 128)).astype(I32)
    page = (2 * chip + place[1]) * 128 + lane
    requests = jnp.zeros((1, 128), I32)
    bases = jnp.zeros((1, 128), I32)
    end = 0
    for request in range(REQS):
        end = end + lengths[request]
        requests = requests + jnp.where(page >= end, 1, 0)
        bases = bases + jnp.where(lane * 128 >= end, 1, 0)
    bases = jnp.minimum(bases, REQS - SPAN)
    base = jnp.sum(jnp.where(lane == 2 * chip + place[1], bases, 0).astype(F32), axis=1, keepdims=True)
    out[3:4, :] = bases
    out[4:5, :] = requests
    out[5:6, :] = jnp.broadcast_to(base, (1, 128)).astype(I32)
    out[6:8, :] = jnp.zeros((2, 128), I32)


def make_plan(place, lengths, page_owner):
    return pl.pallas_call(
        plan_kernel,
        grid_spec=pltpu.PrefetchScalarGridSpec(
            num_scalar_prefetch=2,
            grid=(1,),
            in_specs=[pl.BlockSpec((16, 128), lambda i, *_: (0, 0))],
            out_specs=pl.BlockSpec((8, 128), lambda i, *_: (0, 0)),
        ),
        out_shape=jax.ShapeDtypeStruct((8, 128), I32),
        name="make_plan",
    )(place, lengths, page_owner.reshape(16, 128))


def halves_kernel(place, owners, anchors, deltas, scales, keep, give, swap, columns, ranks, order, rows, staged, sems):
    step = pl.program_id(0)
    count = PAGE * PAGE

    @pl.when(step == 0)
    def build():
        row = lax.broadcasted_iota(I32, (count, count), 0)
        lane = lax.broadcasted_iota(I32, (count, count), 1)
        swap[...] = jnp.where(lane == (row & 15) * PAGE + (row >> 4), 1.0, 0.0).astype(BF16)
        columns[...] = jnp.transpose(scales[...])
        number = owners.shape[1]
        row = lax.broadcasted_iota(I32, (number, number), 0)
        lane = lax.broadcasted_iota(I32, (number, number), 1)
        across = owners[pl.ds(2 * place[0] + place[1], 1), :].astype(F32)
        down = jnp.sum(jnp.where(row == lane, across, 0.0), axis=1, keepdims=True)
        ahead = (down < across) | ((down == across) & (row < lane))
        ranks[...] = jnp.sum(jnp.where(ahead, 1.0, 0.0), axis=0, keepdims=True).astype(I32)
        pltpu.make_async_copy(ranks, order, sems.at[2]).start()

    core = place[1]
    for part in range(anchors.shape[0] // PAGE):
        pages = slice(part * PAGE, (part + 1) * PAGE)
        for head in range(2 * KVH):
            cols = slice(head * HD, (head + 1) * HD)
            start = pl.multiple_of(step * anchors.shape[0] + part * PAGE, PAGE)
            scale = jnp.broadcast_to(columns[pl.ds(start, PAGE), head : head + 1], (PAGE, HD))
            first = anchors[pages, cols]
            anchor = first.astype(F32)
            rows[0:PAGE, cols] = first
            for token in range(1, PAGE):
                rebuilt = anchor + scale * deltas[token - 1, pages, cols].astype(F32)
                rows[token * PAGE : (token + 1) * PAGE, cols] = rebuilt.astype(BF16)
        turned = jnp.dot(swap[...], rows[...], preferred_element_type=F32).astype(BF16)
        if part == 0:

            @pl.when(step == 0)
            def ordered():
                pltpu.make_async_copy(ranks, order, sems.at[2]).wait()

        for page in range(PAGE):
            rank = order[0, step * anchors.shape[0] + part * PAGE + page]
            half = (rank >> 3) & 1
            slot = (half ^ core) * 64 + (rank >> 4) * HALF + (rank & 7)
            staged[slot] = turned[page * PAGE : (page + 1) * PAGE]

    @pl.when(step == pl.num_programs(0) - 1)
    def flush():
        copies = [
            pltpu.make_async_copy(staged.at[pl.ds(64, 64)], give, sems.at[0]),
            pltpu.make_async_copy(staged.at[pl.ds(0, 64)], keep, sems.at[1]),
        ]
        for copy in copies:
            copy.start()
        for copy in copies:
            copy.wait()


def decode_halves(place, page_owner, anchors, deltas, scales):
    number = anchors.shape[0]
    chunk = 2 * PAGE
    half = jax.ShapeDtypeStruct((number // 2, PAGE, KVW), BF16)
    return pl.pallas_call(
        halves_kernel,
        grid_spec=pltpu.PrefetchScalarGridSpec(
            num_scalar_prefetch=1,
            grid=(number // chunk,),
            in_specs=[
                pl.BlockSpec((16, number), lambda i, *_: (0, 0)),
                pl.BlockSpec((chunk, KVW), lambda i, *_: (i, 0)),
                pl.BlockSpec((PAGE - 1, chunk, KVW), lambda i, *_: (0, i, 0)),
                pl.BlockSpec((2 * KVH, number), lambda i, *_: (0, 0)),
            ],
            out_specs=[pl.BlockSpec(memory_space=pl.ANY)] * 2,
            scratch_shapes=[
                pltpu.VMEM((PAGE * PAGE, PAGE * PAGE), BF16),
                pltpu.VMEM((number, 2 * KVH), F32),
                pltpu.VMEM((1, number), I32),
                pltpu.SMEM((1, number), I32),
                pltpu.VMEM((PAGE * PAGE, KVW), BF16),
                pltpu.VMEM((number, PAGE, KVW), BF16),
                pltpu.SemaphoreType.DMA((3,)),
            ],
        ),
        out_shape=(half, half),
        compiler_params=pltpu.CompilerParams(vmem_limit_bytes=VMEM_LIMIT),
        name="decode_halves",
    )(place, page_owner.reshape(16, number), anchors, deltas, scales)


def fetch(code, core, own, landed, ports, target, sem):
    value = code - 1
    keep, got = own

    @pl.when((value >= 0) & (value < 16))
    def from_own():
        rows = pl.ds((value & 7) * HALF, HALF)

        @pl.when((value >> 3) == core)
        def kept():
            pltpu.make_async_copy(keep.at[rows], target, sem).start()

        @pl.when((value >> 3) != core)
        def gotten():
            pltpu.make_async_copy(got.at[rows], target, sem).start()

    for time, port, arrivals in landed:
        if port in ports:
            offset = value - 16 - SLOTS * time - UNIT * port

            @pl.when((offset >= 0) & (offset < units_of(port, time)))
            def from_round():
                rows = pl.ds(offset * HALF, HALF)
                pltpu.make_async_copy(arrivals.at[rows], target, sem).start()


def settle(code, own, target, sem):
    @pl.when(code > 0)
    def wait():
        pltpu.make_async_copy(own[0].at[pl.ds(0, HALF)], target, sem).wait()


def pick_kernel(time, tags, plan, place, *refs):
    own, landed = refs[:2], [tag + (ref,) for tag, ref in zip(tags, refs[2:])]
    used = [port for port in range(3) if units_of(port, time)]
    outs, sems = refs[-1 - len(used) : -1], refs[-1]
    for phase in range(2):
        for port, out in zip(used, outs):
            ports = (0, 1) if port == 2 else (port, 2)
            for unit in range(units_of(port, time)):
                code = plan[0, SLOTS * time + UNIT * port + unit]
                target = out.at[pl.ds(unit * HALF, HALF)]
                sem = sems.at[UNIT * port + unit]
                if phase == 0:
                    fetch(code, place[1], own, landed, ports, target, sem)
                else:
                    settle(code, own, target, sem)


def pick(time, plan, place, own, landed, after):
    landed = [item for item in landed if item[0] + (SIDE_LAG if item[1] == 2 else LAG) <= time]
    sources = list(own) + [item[2] for item in landed] + [after]
    pieces = [
        jax.ShapeDtypeStruct((units_of(port, time) * HALF, PAGE, KVW), BF16)
        for port in range(3)
        if units_of(port, time)
    ]
    return pl.pallas_call(
        functools.partial(pick_kernel, time, [item[:2] for item in landed]),
        grid_spec=pltpu.PrefetchScalarGridSpec(
            num_scalar_prefetch=2,
            grid=(1,),
            in_specs=[pl.BlockSpec(memory_space=pl.ANY)] * len(sources),
            out_specs=[pl.BlockSpec(piece.shape, lambda i, *_: (0, 0, 0)) for piece in pieces],
            scratch_shapes=[pltpu.SemaphoreType.DMA((SLOTS,))],
        ),
        out_shape=pieces,
        compiler_params=pltpu.CompilerParams(vmem_limit_bytes=VMEM_LIMIT),
        name=f"pick_{time}",
    )(plan, place, *sources)


def gather_kernel(mode, low, tags, plan, place, *refs):
    own, landed = refs[:2], [tag + (ref,) for tag, ref in zip(tags, refs[2:])]
    out, staged, in_sems, out_sems = refs[-4:]
    core = place[1]
    half = core if mode == "own" else 1 - core
    high = 16 + SLOTS * (1 + max(time for time, _ in tags))
    codes = [plan[1, half * 8 + slot] for slot in range(8)]
    codes = [jnp.where((code > low) & (code <= high), code, 0) for code in codes]
    targets = [staged.at[pl.ds(slot * HALF, HALF)] for slot in range(8)]
    for slot in range(8):
        fetch(codes[slot], core, own, landed, (0, 1, 2), targets[slot], in_sems.at[slot])
    writes = []
    for slot in range(8):
        start = slot * PAGE + core * HALF if mode == "own" else slot * HALF
        write = pltpu.make_async_copy(
            targets[slot], out.at[pl.ds(start, HALF)], out_sems.at[slot]
        )
        settle(codes[slot], own, targets[slot], in_sems.at[slot])
        pl.when(codes[slot] > 0)(write.start)
        writes.append(write)
    for slot in range(8):
        pl.when(codes[slot] > 0)(writes[slot].wait)


def gather(mode, low, plan, place, own, landed, after, base=None):
    sources = list(own) + [item[2] for item in landed] + [after]
    if base is not None:
        sources.append(base)
    pages = 8 * (PAGE if mode == "own" else HALF)
    return pl.pallas_call(
        functools.partial(gather_kernel, mode, low, [item[:2] for item in landed]),
        grid_spec=pltpu.PrefetchScalarGridSpec(
            num_scalar_prefetch=2,
            grid=(1,),
            in_specs=[pl.BlockSpec(memory_space=pl.ANY)] * len(sources),
            out_specs=pl.BlockSpec(memory_space=pl.ANY),
            scratch_shapes=[
                pltpu.VMEM((8 * HALF, PAGE, KVW), BF16),
                pltpu.SemaphoreType.DMA((8,)),
                pltpu.SemaphoreType.DMA((8,)),
            ],
        ),
        out_shape=jax.ShapeDtypeStruct((pages, PAGE, KVW), BF16),
        input_output_aliases={} if base is None else {1 + len(sources): 0},
        compiler_params=pltpu.CompilerParams(vmem_limit_bytes=VMEM_LIMIT),
        name=f"gather_{mode}",
    )(plan, place, *sources)


def fill_kernel(place, cache, other, out, staged, in_sems, out_sems):
    half = 1 - place[1]
    reads, writes = [], []
    for slot in range(8):
        rows = pl.ds(slot * HALF, HALF)
        reads.append(pltpu.make_async_copy(other.at[rows], staged.at[rows], in_sems.at[slot]))
        writes.append(
            pltpu.make_async_copy(
                staged.at[rows], out.at[pl.ds(slot * PAGE + half * HALF, HALF)], out_sems.at[slot]
            )
        )
    for read in reads:
        read.start()
    for read, write in zip(reads, writes):
        read.wait()
        write.start()
    for write in writes:
        write.wait()


def fill(place, cache, other):
    return pl.pallas_call(
        fill_kernel,
        grid_spec=pltpu.PrefetchScalarGridSpec(
            num_scalar_prefetch=1,
            grid=(1,),
            in_specs=[pl.BlockSpec(memory_space=pl.ANY)] * 2,
            out_specs=pl.BlockSpec(memory_space=pl.ANY),
            scratch_shapes=[
                pltpu.VMEM((8 * HALF, PAGE, KVW), BF16),
                pltpu.SemaphoreType.DMA((8,)),
                pltpu.SemaphoreType.DMA((8,)),
            ],
        ),
        out_shape=jax.ShapeDtypeStruct(cache.shape, cache.dtype),
        input_output_aliases={1: 0},
        compiler_params=pltpu.CompilerParams(vmem_limit_bytes=VMEM_LIMIT),
        name="fill",
    )(place, cache, other)


UP = tuple((i, i + 4) for i in range(12))
DOWN = tuple((i + 4, i) for i in range(12))
ACROSS = tuple((i, i ^ 2) for i in range(16))
TWIN = tuple((i, i ^ 1) for i in range(16))


def ship(time, parts):
    used = [port for port in range(3) if units_of(port, time)]
    hops = (UP, DOWN, ACROSS)
    return [(time, port, lax.ppermute(part, "pool", hops[port])) for port, part in zip(used, parts)]


def finish(plan, place, own, landed, after):
    give = gather("give", 0, plan, place, own, landed, after)
    other = lax.ppermute(give, "pool", TWIN)
    return fill(place, gather("own", 0, plan, place, own, landed, give), other)


def finish_in_two(plan, place, own, landed, after, attention):
    early = [item for item in landed if item[0] < ROUNDS - 1]
    last = [item for item in landed if item[0] >= ROUNDS - 1]
    low = 16 + SLOTS * (ROUNDS - 1)
    give = gather("give", 0, plan, place, own, early, after)
    keep = gather("own", 0, plan, place, own, early, after)
    keep, _ = lax.optimization_barrier((keep, attention))
    give = gather("give", low, plan, place, own, last, keep, give)
    other = lax.ppermute(give, "pool", TWIN)
    return fill(place, gather("own", low, plan, place, own, last, give, keep), other)


def local_lanes(anchors, deltas, scales, queries, lengths, page_owner):
    position = lax.axis_index("pool")
    number = anchors.shape[0]
    by_token = jnp.transpose(deltas, (1, 0, 2))
    place = jnp.stack([position >> 1, position & 1]).astype(I32)
    lines = jnp.transpose(scales)
    keep, give = decode_halves(place, page_owner, anchors, by_token, lines)
    got = lax.ppermute(give, "pool", TWIN)
    plan = make_plan(place, lengths, page_owner)
    own = (keep, got)
    landed = []
    after = partial = plan
    for time in range(ROUNDS):
        parts = pick(time, plan, place, own, landed, after)
        landed += ship(time, parts)
        after = parts[0]
        if 1 <= time <= KVH:
            seen, _ = lax.optimization_barrier((plan, after))
            after = partial = attend(time - 1, seen, queries, anchors, by_token, lines, partial)
    partial, _ = lax.optimization_barrier((partial, after))
    swapped = lax.all_to_all(partial, "pool", split_axis=0, concat_axis=0, tiled=True)
    attention = merge(plan, place, swapped, after)
    cache = finish_in_two(plan, place, own, landed, after, attention)

    def in_time(cache):
        return cache

    def late(cache):
        more, last = list(landed), plan
        for time in range(ROUNDS, LIMIT):
            parts = pick(time, plan, place, own, more, last)
            more += ship(time, parts)
            last = parts[0]
        return finish(plan, place, own, more, last)

    def padded(cache):
        owners = lax.dynamic_slice_in_dim(page_owner, position * number, number, 0)
        index = jnp.arange(number, dtype=I32)
        ahead = (owners[None, :] < owners[:, None]) | (
            (owners[None, :] == owners[:, None]) & (index[None, :] < index[:, None])
        )
        order = jnp.sum(ahead.astype(I32), axis=1)
        devices = jnp.arange(16, dtype=I32)
        sent = jnp.any(owners[None, :] == devices[:, None], axis=1).astype(I32)
        slabs = decode_sorted(order, sent, jnp.cumsum(sent) - sent, anchors, by_token, scales)
        arrived = lax.all_to_all(slabs, "pool", split_axis=0, concat_axis=0, tiled=True)
        taken = jnp.any((page_owner == position).reshape(16, number), axis=1).astype(I32)
        return assemble(taken, jnp.cumsum(taken) - taken, arrived, number)

    needed = plan[2, 0]
    branch = (needed > ROUNDS).astype(I32) + (needed > LIMIT).astype(I32)
    cache = lax.switch(branch, (in_time, late, padded), cache)
    return (cache, attention)


def decode_pages(anchors, deltas, scales):
    block_scale = jnp.repeat(scales, HD, axis=1)
    rebuilt = anchors[:, None, :].astype(jnp.float32) + block_scale[:, None, :] * deltas.astype(
        jnp.float32
    )
    return jnp.concatenate([anchors[:, None, :], rebuilt.astype(jnp.bfloat16)], axis=1)


def page_scores(work_pages, queries, requests):
    number = work_pages.shape[0]
    key_rows = work_pages[:, :, : KVH * HD].reshape(number, PAGE, KVH, HD)
    picked = jnp.take(queries, requests, axis=0).reshape(number, STEPS, KVH, QH // KVH, HD)
    scores = jnp.einsum(
        "nskgd,ntkd->nskgt", picked, key_rows, preferred_element_type=jnp.float32
    ) * HD ** (-0.5)
    return (scores, jnp.max(scores, axis=4))


def accumulate(scores, page_max, work_pages, requests, shift_max):
    number = work_pages.shape[0]
    rows_out = shift_max.shape[0]
    block_size = min(32, number)
    blocks = number // block_size
    value_rows = work_pages[:, :, KVH * HD :].reshape(blocks, block_size, PAGE, KVH, HD)
    score_blocks = scores.reshape((blocks, block_size) + scores.shape[1:])
    max_blocks = page_max.reshape((blocks, block_size) + page_max.shape[1:])
    request_blocks = requests.reshape(blocks, block_size)

    def block_step(running, pieces):
        totals, numerator = running
        block_scores, block_max, block_values, block_requests = pieces
        exponent = jnp.exp(block_scores - block_max[..., None])
        weights = exponent.astype(jnp.bfloat16)
        page_out = jnp.einsum(
            "nskgt,ntkd->nskgd", weights, block_values, preferred_element_type=jnp.float32
        )
        factor = jnp.exp(block_max - jnp.take(shift_max, block_requests, axis=0))
        select = (block_requests[None, :] == jnp.arange(rows_out, dtype=jnp.int32)[:, None]).astype(
            jnp.float32
        )
        spread = select[:, :, None, None, None] * factor[None]
        totals = totals + jnp.sum(spread * jnp.sum(exponent, axis=4)[None], axis=1)
        numerator = numerator + jnp.einsum(
            "rnskg,nskgd->rskgd", spread, page_out, precision=lax.Precision.HIGHEST
        )
        return ((totals, numerator), None)

    start_totals = jnp.zeros(shift_max.shape, jnp.float32)
    start_numer = jnp.zeros(shift_max.shape + (HD,), jnp.float32)
    finals, ignored = lax.scan(
        block_step,
        (start_totals, start_numer),
        (score_blocks, max_blocks, value_rows, request_blocks),
    )
    return finals


def request_of(index, request_ends):
    return jnp.sum((index[:, None] >= request_ends[None, :]).astype(jnp.int32), axis=1)


def local(anchors, deltas, scales, queries, lengths, page_owner):
    devices = lax.axis_size("pool")
    position = lax.axis_index("pool")
    number = anchors.shape[0]
    capacity = max(2, 2 * number // devices)
    pages = decode_pages(anchors, deltas, scales)
    request_ends = jnp.cumsum(lengths)
    owners = lax.dynamic_slice_in_dim(page_owner, position * number, number, 0)
    marked = (owners[:, None] == jnp.arange(devices, dtype=jnp.int32)[None, :]).astype(jnp.int32)
    ranking = jnp.sum((jnp.cumsum(marked, axis=0) - 1) * marked, axis=1)
    slot_ids = owners * capacity + ranking
    matches = slot_ids[None, :] == jnp.arange(devices * capacity, dtype=jnp.int32)[:, None]
    sources = jnp.sum(jnp.where(matches, jnp.arange(number, dtype=jnp.int32)[None, :], 0), axis=1)
    outgoing = jnp.take(pages, sources, axis=0)
    arrived = lax.all_to_all(outgoing, "pool", split_axis=0, concat_axis=0, tiled=True)
    held_pages = jnp.nonzero(page_owner == position, size=number)[0].astype(jnp.int32)
    senders = held_pages // number
    before = jnp.sum((held_pages[None, :] < (senders * number)[:, None]).astype(jnp.int32), axis=1)
    row_ids = senders * capacity + jnp.arange(number, dtype=jnp.int32) - before
    cache = jnp.take(arrived, row_ids, axis=0)
    columns = QH * HD // devices
    requests = request_of(held_pages, request_ends)
    scores, page_max = page_scores(cache, queries, requests)
    onehot = requests[None, :] == jnp.arange(REQS, dtype=jnp.int32)[:, None]
    local_max = jnp.max(jnp.where(onehot[:, :, None, None, None], page_max[None], -1e30), axis=1)
    global_max = lax.pmax(local_max.astype(jnp.bfloat16), "pool").astype(local_max.dtype)
    totals, numerator = accumulate(scores, page_max, cache, requests, global_max)
    summed, numerator = lax.psum((totals, numerator), "pool")
    whole = (numerator / summed[..., None]).reshape(REQS, STEPS, QH * HD)
    result = lax.dynamic_slice_in_dim(whole, position * columns, columns, 2)
    return (cache, result.astype(jnp.bfloat16))


def solution(mesh):
    placed = (
        P(("groups", "pool"), None),
        P(("groups", "pool"), None, None),
        P(("groups", "pool"), None),
        P("groups", None, None),
        P("groups"),
        P("groups"),
    )
    lanes = mesh.shape["pool"] == 16
    return jax.shard_map(
        local_lanes if lanes else local,
        mesh=mesh,
        in_specs=placed,
        out_specs=(P(("groups", "pool"), None, None), P("groups", None, "pool")),
        check_vma=False,
    )
```

```python
import functools
import jax
import jax.numpy as jnp
from jax import lax
from jax.experimental import pallas as pl
from jax.experimental.pallas import tpu as pltpu
from jax.sharding import PartitionSpec as P

QH = 64
KVH = 4
HD = 128
PAGE = 16
STEPS = 8
REQS = 16
KVW = 2 * KVH * HD
SPAN = 3
LOW = -1e30
VMEM_LIMIT = 48 * 1024 * 1024
F32 = jnp.float32
BF16 = jnp.bfloat16
I32 = jnp.int32


def decode_kernel(chunk, place, flags, blocks, anchors, deltas, scales, out, rows, staged, sems):
    step = pl.program_id(0)
    for head in range(2 * KVH):
        cols = slice(head * HD, (head + 1) * HD)
        scale = jnp.broadcast_to(scales[:, head : head + 1], (chunk, HD))
        anchor = anchors[:, cols].astype(F32)
        rows[head * PAGE * chunk : head * PAGE * chunk + chunk, :] = anchor
        for token in range(1, PAGE):
            start = (head * PAGE + token) * chunk
            rows[start : start + chunk, :] = anchor + scale * deltas[token - 1, :, cols].astype(F32)
    for page in range(chunk):
        picked = [
            rows[pl.ds(head * PAGE * chunk + page, PAGE, stride=chunk), :]
            for head in range(2 * KVH)
        ]
        staged[place[step * chunk + page]] = jnp.concatenate(picked, axis=1).astype(BF16)

    @pl.when(step == pl.num_programs(0) - 1)
    def flush():
        copies = []
        for owner in range(16):
            copy = pltpu.make_async_copy(
                staged.at[pl.ds(blocks[owner] * PAGE, PAGE)],
                out.at[pl.ds(owner * PAGE, PAGE)],
                sems.at[owner],
            )
            pl.when(flags[owner] > 0)(copy.start)
            copies.append(copy)
        for owner in range(16):
            pl.when(flags[owner] > 0)(copies[owner].wait)


def decode_sorted(place, flags, blocks, anchors, deltas, scales):
    number = anchors.shape[0]
    chunk = 16
    return pl.pallas_call(
        functools.partial(decode_kernel, chunk),
        grid_spec=pltpu.PrefetchScalarGridSpec(
            num_scalar_prefetch=3,
            grid=(number // chunk,),
            in_specs=[
                pl.BlockSpec((chunk, KVW), lambda i, *_: (i, 0)),
                pl.BlockSpec((PAGE - 1, chunk, KVW), lambda i, *_: (0, i, 0)),
                pl.BlockSpec((chunk, 2 * KVH), lambda i, *_: (i, 0)),
            ],
            out_specs=pl.BlockSpec(memory_space=pl.ANY),
            scratch_shapes=[
                pltpu.VMEM((2 * KVH * PAGE * chunk, HD), F32),
                pltpu.VMEM((number, PAGE, KVW), BF16),
                pltpu.SemaphoreType.DMA((16,)),
            ],
        ),
        out_shape=jax.ShapeDtypeStruct((16 * PAGE, PAGE, KVW), BF16),
        compiler_params=pltpu.CompilerParams(vmem_limit_bytes=VMEM_LIMIT),
        name="decode_sorted",
    )(place, flags, blocks, anchors, deltas, scales)


def attend_kernel(head, plan, requests, first, second, third, key_anchor, val_anchor, key_delta, val_delta, scales, after, out, keys, vals):
    number = key_anchor.shape[0]
    columns = jnp.transpose(scales[...])
    key_scale = columns[:, head : head + 1]
    val_scale = columns[:, head + KVH : head + KVH + 1]
    for anchor, delta, scale, kept in (
        (key_anchor, key_delta, key_scale, keys),
        (val_anchor, val_delta, val_scale, vals),
    ):
        kept[0:number, :] = anchor[...]
        wide = anchor[...].astype(F32)
        for token in range(1, PAGE):
            kept[token * number : (token + 1) * number, :] = (
                wide + scale * delta[token - 1].astype(F32)
            ).astype(BF16)
    token_request = jnp.concatenate([requests[4:5, :]] * PAGE, axis=1) - plan[5, 0]
    rows = STEPS * QH // KVH
    eye = lax.broadcasted_iota(I32, (rows, rows), 0) == lax.broadcasted_iota(I32, (rows, rows), 1)
    pieces = []
    for slot, queries in enumerate((first, second, third)):
        wide = queries[0].astype(F32)
        picked = jnp.concatenate(
            [wide[:, group * HD : (group + 1) * HD] for group in range(QH // KVH)], axis=0
        ).astype(BF16)
        scores = lax.dot_general(
            picked, keys[...], (((1,), (1,)), ((), ())), preferred_element_type=F32
        ) * HD ** (-0.5)
        inside = token_request == slot
        scores = jnp.where(inside, scores, LOW)
        top = jnp.max(scores, axis=1, keepdims=True)
        exponent = jnp.where(inside, jnp.exp(scores - top), 0.0)
        total = jnp.maximum(jnp.sum(exponent, axis=1, keepdims=True), 1e-30)
        numer = jnp.dot(exponent.astype(BF16), vals[...], preferred_element_type=F32)
        mean = (numer * (1.0 / total)).astype(BF16)
        quarter = rows // 4
        for part in range(4):
            out[part, slot * quarter : (slot + 1) * quarter, :] = mean[
                part * quarter : (part + 1) * quarter
            ]
        level = top + jnp.log(total)
        line = jnp.sum(jnp.where(eye, level, 0.0), axis=0, keepdims=True)
        for _ in range(3):
            piece = line.astype(BF16).astype(F32)
            pieces.append(piece)
            line = line - piece
    pieces.append(jnp.zeros((16 - len(pieces), rows), F32))
    stats = jnp.concatenate(pieces, axis=0).astype(BF16)
    for part in range(4):
        out[part, 96:112, :] = stats


def attend(head, plan, queries, anchors, deltas, scales, after):
    number = anchors.shape[0]
    rows = STEPS * QH // KVH
    return pl.pallas_call(
        functools.partial(attend_kernel, head),
        grid_spec=pltpu.PrefetchScalarGridSpec(
            num_scalar_prefetch=1,
            grid=(1,),
            in_specs=[
                pl.BlockSpec((8, number), lambda i, *_: (0, 0)),
                *[
                    pl.BlockSpec((1, STEPS, rows * HD // STEPS), lambda i, p, k=k: (p[5, 0] + k, 0, head))
                    for k in range(SPAN)
                ],
                pl.BlockSpec((number, HD), lambda i, *_: (0, head)),
                pl.BlockSpec((number, HD), lambda i, *_: (0, head + KVH)),
                pl.BlockSpec((PAGE - 1, number, HD), lambda i, *_: (0, 0, head)),
                pl.BlockSpec((PAGE - 1, number, HD), lambda i, *_: (0, 0, head + KVH)),
                pl.BlockSpec((2 * KVH, number), lambda i, *_: (0, 0)),
                pl.BlockSpec(memory_space=pl.ANY),
            ],
            out_specs=pl.BlockSpec((4, 112, HD), lambda i, *_: (head, 0, 0)),
            scratch_shapes=[
                pltpu.VMEM((PAGE * number, HD), BF16),
                pltpu.VMEM((PAGE * number, HD), BF16),
            ],
        ),
        out_shape=jax.ShapeDtypeStruct((16, 112, HD), BF16),
        input_output_aliases={} if head == 0 else {10: 0},
        compiler_params=pltpu.CompilerParams(vmem_limit_bytes=VMEM_LIMIT),
        name=f"attend_{head}",
    )(plan, plan, queries, queries, queries, anchors, anchors, deltas, deltas, scales, after)


def merge_kernel(plan, place, parts, after, out, level, top, total, numer):
    quarter = 32
    row = lax.broadcasted_iota(I32, (quarter, HD), 0)
    lane = lax.broadcasted_iota(I32, (quarter, HD), 1)
    mine = lane == row + quarter * ((place[0] & 1) * 2 + place[1])
    top[...] = jnp.full(top.shape, LOW, F32)
    total[...] = jnp.zeros(total.shape, F32)
    numer[...] = jnp.zeros(numer.shape, F32)
    for sender in range(16):
        stats = parts[sender, 96:112, :].astype(F32)
        for slot in range(SPAN):
            line = stats[3 * slot : 3 * slot + 1] + (
                stats[3 * slot + 1 : 3 * slot + 2] + stats[3 * slot + 2 : 3 * slot + 3]
            )
            column = jnp.sum(jnp.where(mine, line, 0.0), axis=1, keepdims=True)
            column = jnp.broadcast_to(column, (quarter, HD))
            level[sender * SPAN + slot] = column
            request = plan[3, sender] + slot
            top[request] = jnp.maximum(top[request], column)
    for sender in range(16):
        for slot in range(SPAN):
            request = plan[3, sender] + slot
            weight = jnp.exp(level[sender * SPAN + slot] - top[request])
            mean = parts[sender, slot * quarter : (slot + 1) * quarter, :].astype(F32)
            total[request] += weight
            numer[request] += weight * mean
    for request in range(REQS):
        result = (numer[request] / total[request]).astype(BF16)
        for group in range(4):
            out[request, :, group * HD : (group + 1) * HD] = result[
                group * STEPS : (group + 1) * STEPS
            ]


def merge(plan, place, parts, after):
    return pl.pallas_call(
        merge_kernel,
        grid_spec=pltpu.PrefetchScalarGridSpec(
            num_scalar_prefetch=2,
            grid=(1,),
            in_specs=[
                pl.BlockSpec((16, 112, HD), lambda i, *_: (0, 0, 0)),
                pl.BlockSpec(memory_space=pl.ANY),
            ],
            out_specs=pl.BlockSpec((REQS, STEPS, 4 * HD), lambda i, *_: (0, 0, 0)),
            scratch_shapes=[
                pltpu.VMEM((16 * SPAN, 32, HD), F32),
                pltpu.VMEM((REQS, 32, HD), F32),
                pltpu.VMEM((REQS, 32, HD), F32),
                pltpu.VMEM((REQS, 32, HD), F32),
            ],
        ),
        out_shape=jax.ShapeDtypeStruct((REQS, STEPS, 4 * HD), BF16),
        compiler_params=pltpu.CompilerParams(vmem_limit_bytes=VMEM_LIMIT),
        name="merge",
    )(plan, place, parts, after)


def assemble_kernel(flags, blocks, arrived, out, staged, in_sems, out_sems):
    reads, writes = [], []
    for sender in range(16):
        rows = pl.ds(blocks[sender] * PAGE, PAGE)
        source = arrived.at[pl.ds(sender * PAGE, PAGE)]
        reads.append(pltpu.make_async_copy(source, staged.at[rows], in_sems.at[sender]))
        writes.append(pltpu.make_async_copy(staged.at[rows], out.at[rows], out_sems.at[sender]))
    for sender in range(16):
        pl.when(flags[sender] > 0)(reads[sender].start)
    for sender in range(16):

        @pl.when(flags[sender] > 0)
        def forward():
            reads[sender].wait()
            writes[sender].start()

    for sender in range(16):
        pl.when(flags[sender] > 0)(writes[sender].wait)


def assemble(flags, blocks, arrived, number):
    return pl.pallas_call(
        assemble_kernel,
        grid_spec=pltpu.PrefetchScalarGridSpec(
            num_scalar_prefetch=2,
            grid=(1,),
            in_specs=[pl.BlockSpec(memory_space=pl.ANY)],
            out_specs=pl.BlockSpec(memory_space=pl.ANY),
            scratch_shapes=[
                pltpu.VMEM((number, PAGE, KVW), BF16),
                pltpu.SemaphoreType.DMA((16,)),
                pltpu.SemaphoreType.DMA((16,)),
            ],
        ),
        out_shape=jax.ShapeDtypeStruct((number, PAGE, KVW), BF16),
        compiler_params=pltpu.CompilerParams(vmem_limit_bytes=VMEM_LIMIT),
        name="assemble",
    )(flags, blocks, arrived)


ROUNDS = 9
LIMIT = 10
UNIT = 2
LAG = 2
SIDE_LAG = 3
SLOTS = 7
SIDE = (3, 0, 3, 0, 3, 0, 2, 2, 1)
HALF = PAGE // 2
FAR = 1e6


def units_of(port, time):
    if port < 2:
        return UNIT
    return SIDE[time] if time < len(SIDE) else 2


def plan_kernel(place, lengths, owners, out):
    chip = place[0]
    row = lax.broadcasted_iota(I32, (16, 128), 0)
    lanes = lax.broadcasted_iota(I32, (16, 128), 1)
    sender_of = lanes >> 3
    turn = (lanes & 7).astype(F32)
    table = owners[...]
    running = jnp.zeros((16, 1), F32)
    sends = []
    targets = jnp.zeros((16, 128), F32)
    for owner in range(16):
        flag = jnp.max(jnp.where(table == owner, 1.0, 0.0), axis=1, keepdims=True)
        targets += jnp.where(turn == running, flag * owner, 0.0)
        sends.append(flag)
        running = running + flag
    dest = jnp.sum(jnp.where(row == sender_of, targets, 0.0), axis=0, keepdims=True)
    hits = jnp.zeros((16, 128), F32)
    for owner in range(16):
        hits += sends[owner] * jnp.where(dest == owner, 1.0, 0.0)
    rank = jnp.sum(jnp.where(row < sender_of, hits, 0.0), axis=0, keepdims=True).astype(I32)
    dest = dest.astype(I32)
    lane = lax.broadcasted_iota(I32, (1, 128), 1)
    sender = lane >> 3
    from_z, from_x = sender >> 2, (sender >> 1) & 1
    to_z, to_x = dest >> 2, (dest >> 1) & 1
    crosses = (from_z >> 1) != (to_z >> 1)
    below = jnp.where(
        lax.broadcasted_iota(I32, (128, 128), 0) < lax.broadcasted_iota(I32, (128, 128), 1), 1.0, 0.0
    )
    line = from_x
    for side in range(2):
        leaving = crosses & ((from_z >> 1) == side)
        free = jnp.where(leaving & (from_x != to_x), 1.0, 0.0)
        fixed = jnp.where(leaving & (from_x == to_x), 1.0, 0.0)
        tilt = jnp.sum(fixed * (2 * from_x - 1).astype(F32), axis=1, keepdims=True)
        count = jnp.sum(free, axis=1, keepdims=True)
        share = jnp.clip(jnp.floor((tilt + count) * 0.5), 0.0, count)
        step = share / jnp.maximum(count, 1.0)
        index = jnp.dot(jnp.broadcast_to(free, (8, 128)), below, preferred_element_type=F32)[0:1]
        first = jnp.floor((index + 1.0) * step + 1e-3) > jnp.floor(index * step + 1e-3)
        line = jnp.where(free > 0.0, jnp.where(first, 0, 1), line)
    chips = lax.broadcasted_iota(I32, (8, 128), 0)
    mine = lax.broadcasted_iota(I32, (8, 1), 0) == chip

    def round_step(time, carry):
        at_z, at_x, ready, code, steps, needed = carry
        waits = crosses & ((at_z >> 1) == (from_z >> 1))
        turns = ((at_z == to_z) & (at_x != to_x)) | (waits & (line != at_x))
        along = jnp.logical_not(turns) & (at_z != to_z)
        left = jnp.abs(to_z - at_z) + jnp.where(at_x != to_x, 1, 0)
        key = ((8 - left) * 128 + lane).astype(F32)
        here = (at_z * 2 + at_x == chips) & (ready <= time)
        heading = jnp.where(turns, 2, jnp.where(along, jnp.where(to_z > at_z, 0, 1), 3))
        moved = jnp.zeros((1, 128), F32)
        landed = jnp.zeros((1, 128), F32)
        value = (code + 1).astype(F32)
        side = sum(jnp.where(time == t, units_of(2, t), 0) for t in range(LIMIT))
        for port in range(3):
            keys = jnp.where(here & (heading == port), key, FAR)
            for unit in range(UNIT if port < 2 else 3):
                if port == 2:
                    keys = jnp.where(unit < side, keys, FAR)
                least = jnp.min(keys, axis=1, keepdims=True)
                chosen = jnp.where((keys == least) & (keys < FAR), 1.0, 0.0)
                source = jnp.sum(chosen * value, axis=1, keepdims=True)
                source = jnp.sum(jnp.where(mine, source, 0.0), axis=0, keepdims=True)
                slot = SLOTS * time + UNIT * port + unit
                steps = steps + jnp.where(lane == slot, source, 0.0)
                taken = jnp.sum(chosen, axis=0, keepdims=True)
                moved = moved + taken * (port + 1)
                landed = landed + taken * (slot + 16).astype(F32)
                keys = jnp.where(chosen > 0.0, FAR, keys)
        went = moved.astype(I32)
        at_z = at_z + jnp.where(went == 1, 1, 0) - jnp.where(went == 2, 1, 0)
        at_x = jnp.where(went == 3, 1 - at_x, at_x)
        ready = jnp.where(went > 0, time + jnp.where(went == 3, SIDE_LAG, LAG), ready)
        code = jnp.where(went > 0, landed.astype(I32), code)
        any_move = jnp.max(moved, axis=1, keepdims=True)
        needed = jnp.where(any_move > 0.0, (time + 1).astype(F32), needed)
        return at_z, at_x, ready, code, steps, needed

    start = (
        from_z,
        from_x,
        jnp.zeros((1, 128), I32),
        (sender & 1) * 8 + (lane & 7),
        jnp.zeros((1, 128), F32),
        jnp.zeros((1, 1), F32),
    )
    at_z, at_x, ready, code, steps, needed = lax.fori_loop(0, LIMIT, round_step, start)
    undone = jnp.where((at_z == to_z) & (at_x == to_x), 0.0, 1.0)
    undone = jnp.max(undone, axis=1, keepdims=True)
    needed = jnp.where(undone > 0.0, float(LIMIT + 1), needed)
    arrives = (dest >> 1) == chip
    slots = (dest & 1) * 8 + rank
    final = jnp.sum(
        jnp.where((row == slots) & arrives, (code + 1).astype(F32), 0.0), axis=1, keepdims=True
    )
    final = jnp.sum(jnp.where(row == lanes, final, 0.0), axis=0, keepdims=True)
    out[0:1, :] = steps.astype(I32)
    out[1:2, :] = final.astype(I32)
    out[2:3, :] = jnp.broadcast_to(needed, (1, 128)).astype(I32)
    page = (2 * chip + place[1]) * 128 + lane
    requests = jnp.zeros((1, 128), I32)
    bases = jnp.zeros((1, 128), I32)
    end = 0
    for request in range(REQS):
        end = end + lengths[request]
        requests = requests + jnp.where(page >= end, 1, 0)
        bases = bases + jnp.where(lane * 128 >= end, 1, 0)
    bases = jnp.minimum(bases, REQS - SPAN)
    base = jnp.sum(jnp.where(lane == 2 * chip + place[1], bases, 0).astype(F32), axis=1, keepdims=True)
    out[3:4, :] = bases
    out[4:5, :] = requests
    out[5:6, :] = jnp.broadcast_to(base, (1, 128)).astype(I32)
    out[6:8, :] = jnp.zeros((2, 128), I32)


def make_plan(place, lengths, page_owner):
    return pl.pallas_call(
        plan_kernel,
        grid_spec=pltpu.PrefetchScalarGridSpec(
            num_scalar_prefetch=2,
            grid=(1,),
            in_specs=[pl.BlockSpec((16, 128), lambda i, *_: (0, 0))],
            out_specs=pl.BlockSpec((8, 128), lambda i, *_: (0, 0)),
        ),
        out_shape=jax.ShapeDtypeStruct((8, 128), I32),
        name="make_plan",
    )(place, lengths, page_owner.reshape(16, 128))


def halves_kernel(place, owners, anchors, deltas, scales, keep, give, swap, columns, ranks, order, rows, staged, sems):
    step = pl.program_id(0)
    count = PAGE * PAGE

    @pl.when(step == 0)
    def build():
        row = lax.broadcasted_iota(I32, (count, count), 0)
        lane = lax.broadcasted_iota(I32, (count, count), 1)
        swap[...] = jnp.where(lane == (row & 15) * PAGE + (row >> 4), 1.0, 0.0).astype(BF16)
        columns[...] = jnp.transpose(scales[...])
        number = owners.shape[1]
        row = lax.broadcasted_iota(I32, (number, number), 0)
        lane = lax.broadcasted_iota(I32, (number, number), 1)
        across = owners[pl.ds(2 * place[0] + place[1], 1), :].astype(F32)
        down = jnp.sum(jnp.where(row == lane, across, 0.0), axis=1, keepdims=True)
        ahead = (down < across) | ((down == across) & (row < lane))
        ranks[...] = jnp.sum(jnp.where(ahead, 1.0, 0.0), axis=0, keepdims=True).astype(I32)
        pltpu.make_async_copy(ranks, order, sems.at[2]).start()

    core = place[1]
    for part in range(anchors.shape[0] // PAGE):
        pages = slice(part * PAGE, (part + 1) * PAGE)
        for head in range(2 * KVH):
            cols = slice(head * HD, (head + 1) * HD)
            start = pl.multiple_of(step * anchors.shape[0] + part * PAGE, PAGE)
            scale = jnp.broadcast_to(columns[pl.ds(start, PAGE), head : head + 1], (PAGE, HD))
            first = anchors[pages, cols]
            anchor = first.astype(F32)
            rows[0:PAGE, cols] = first
            for token in range(1, PAGE):
                rebuilt = anchor + scale * deltas[token - 1, pages, cols].astype(F32)
                rows[token * PAGE : (token + 1) * PAGE, cols] = rebuilt.astype(BF16)
        turned = jnp.dot(swap[...], rows[...], preferred_element_type=F32).astype(BF16)
        if part == 0:

            @pl.when(step == 0)
            def ordered():
                pltpu.make_async_copy(ranks, order, sems.at[2]).wait()

        for page in range(PAGE):
            rank = order[0, step * anchors.shape[0] + part * PAGE + page]
            half = (rank >> 3) & 1
            slot = (half ^ core) * 64 + (rank >> 4) * HALF + (rank & 7)
            staged[slot] = turned[page * PAGE : (page + 1) * PAGE]

    @pl.when(step == pl.num_programs(0) - 1)
    def flush():
        copies = [
            pltpu.make_async_copy(staged.at[pl.ds(64, 64)], give, sems.at[0]),
            pltpu.make_async_copy(staged.at[pl.ds(0, 64)], keep, sems.at[1]),
        ]
        for copy in copies:
            copy.start()
        for copy in copies:
            copy.wait()


def decode_halves(place, page_owner, anchors, deltas, scales):
    number = anchors.shape[0]
    chunk = 2 * PAGE
    half = jax.ShapeDtypeStruct((number // 2, PAGE, KVW), BF16)
    return pl.pallas_call(
        halves_kernel,
        grid_spec=pltpu.PrefetchScalarGridSpec(
            num_scalar_prefetch=1,
            grid=(number // chunk,),
            in_specs=[
                pl.BlockSpec((16, number), lambda i, *_: (0, 0)),
                pl.BlockSpec((chunk, KVW), lambda i, *_: (i, 0)),
                pl.BlockSpec((PAGE - 1, chunk, KVW), lambda i, *_: (0, i, 0)),
                pl.BlockSpec((2 * KVH, number), lambda i, *_: (0, 0)),
            ],
            out_specs=[pl.BlockSpec(memory_space=pl.ANY)] * 2,
            scratch_shapes=[
                pltpu.VMEM((PAGE * PAGE, PAGE * PAGE), BF16),
                pltpu.VMEM((number, 2 * KVH), F32),
                pltpu.VMEM((1, number), I32),
                pltpu.SMEM((1, number), I32),
                pltpu.VMEM((PAGE * PAGE, KVW), BF16),
                pltpu.VMEM((number, PAGE, KVW), BF16),
                pltpu.SemaphoreType.DMA((3,)),
            ],
        ),
        out_shape=(half, half),
        compiler_params=pltpu.CompilerParams(vmem_limit_bytes=VMEM_LIMIT),
        name="decode_halves",
    )(place, page_owner.reshape(16, number), anchors, deltas, scales)


def fetch(code, core, own, landed, ports, target, sem):
    value = code - 1
    keep, got = own

    @pl.when((value >= 0) & (value < 16))
    def from_own():
        rows = pl.ds((value & 7) * HALF, HALF)

        @pl.when((value >> 3) == core)
        def kept():
            pltpu.make_async_copy(keep.at[rows], target, sem).start()

        @pl.when((value >> 3) != core)
        def gotten():
            pltpu.make_async_copy(got.at[rows], target, sem).start()

    for time, port, arrivals in landed:
        if port in ports:
            offset = value - 16 - SLOTS * time - UNIT * port

            @pl.when((offset >= 0) & (offset < units_of(port, time)))
            def from_round():
                rows = pl.ds(offset * HALF, HALF)
                pltpu.make_async_copy(arrivals.at[rows], target, sem).start()


def settle(code, own, target, sem):
    @pl.when(code > 0)
    def wait():
        pltpu.make_async_copy(own[0].at[pl.ds(0, HALF)], target, sem).wait()


def pick_kernel(time, tags, plan, place, *refs):
    own, landed = refs[:2], [tag + (ref,) for tag, ref in zip(tags, refs[2:])]
    used = [port for port in range(3) if units_of(port, time)]
    outs, sems = refs[-1 - len(used) : -1], refs[-1]
    for phase in range(2):
        for port, out in zip(used, outs):
            ports = (0, 1) if port == 2 else (port, 2)
            for unit in range(units_of(port, time)):
                code = plan[0, SLOTS * time + UNIT * port + unit]
                target = out.at[pl.ds(unit * HALF, HALF)]
                sem = sems.at[UNIT * port + unit]
                if phase == 0:
                    fetch(code, place[1], own, landed, ports, target, sem)
                else:
                    settle(code, own, target, sem)


def pick(time, plan, place, own, landed, after):
    landed = [item for item in landed if item[0] + (SIDE_LAG if item[1] == 2 else LAG) <= time]
    sources = list(own) + [item[2] for item in landed] + [after]
    pieces = [
        jax.ShapeDtypeStruct((units_of(port, time) * HALF, PAGE, KVW), BF16)
        for port in range(3)
        if units_of(port, time)
    ]
    return pl.pallas_call(
        functools.partial(pick_kernel, time, [item[:2] for item in landed]),
        grid_spec=pltpu.PrefetchScalarGridSpec(
            num_scalar_prefetch=2,
            grid=(1,),
            in_specs=[pl.BlockSpec(memory_space=pl.ANY)] * len(sources),
            out_specs=[pl.BlockSpec(piece.shape, lambda i, *_: (0, 0, 0)) for piece in pieces],
            scratch_shapes=[pltpu.SemaphoreType.DMA((SLOTS,))],
        ),
        out_shape=pieces,
        compiler_params=pltpu.CompilerParams(vmem_limit_bytes=VMEM_LIMIT),
        name=f"pick_{time}",
    )(plan, place, *sources)


def gather_kernel(mode, low, tags, plan, place, *refs):
    own, landed = refs[:2], [tag + (ref,) for tag, ref in zip(tags, refs[2:])]
    out, staged, in_sems, out_sems = refs[-4:]
    core = place[1]
    half = core if mode == "own" else 1 - core
    high = 16 + SLOTS * (1 + max(time for time, _ in tags))

    def code_of(slot):
        code = plan[1, half * 8 + slot]
        return jnp.where((code > low) & (code <= high), code, 0)

    def target_of(slot):
        return staged.at[pl.ds(slot * HALF, HALF)]

    def write_of(slot):
        start = slot * PAGE + core * HALF if mode == "own" else slot * HALF
        return pltpu.make_async_copy(
            target_of(slot), out.at[pl.ds(start, HALF)], out_sems.at[slot]
        )

    @pl.loop(0, 8)
    def read(slot):
        fetch(code_of(slot), core, own, landed, (0, 1, 2), target_of(slot), in_sems.at[slot])

    @pl.loop(0, 8)
    def forward(slot):
        settle(code_of(slot), own, target_of(slot), in_sems.at[slot])
        pl.when(code_of(slot) > 0)(write_of(slot).start)

    @pl.loop(0, 8)
    def close(slot):
        pl.when(code_of(slot) > 0)(write_of(slot).wait)


def gather(mode, low, plan, place, own, landed, after, base=None):
    sources = list(own) + [item[2] for item in landed] + [after]
    if base is not None:
        sources.append(base)
    pages = 8 * (PAGE if mode == "own" else HALF)
    return pl.pallas_call(
        functools.partial(gather_kernel, mode, low, [item[:2] for item in landed]),
        grid_spec=pltpu.PrefetchScalarGridSpec(
            num_scalar_prefetch=2,
            grid=(1,),
            in_specs=[pl.BlockSpec(memory_space=pl.ANY)] * len(sources),
            out_specs=pl.BlockSpec(memory_space=pl.ANY),
            scratch_shapes=[
                pltpu.VMEM((8 * HALF, PAGE, KVW), BF16),
                pltpu.SemaphoreType.DMA((8,)),
                pltpu.SemaphoreType.DMA((8,)),
            ],
        ),
        out_shape=jax.ShapeDtypeStruct((pages, PAGE, KVW), BF16),
        input_output_aliases={} if base is None else {1 + len(sources): 0},
        compiler_params=pltpu.CompilerParams(vmem_limit_bytes=VMEM_LIMIT),
        name=f"gather_{mode}",
    )(plan, place, *sources)


def fill_kernel(place, cache, other, out, staged, in_sems, out_sems):
    half = 1 - place[1]
    reads, writes = [], []
    for slot in range(8):
        rows = pl.ds(slot * HALF, HALF)
        reads.append(pltpu.make_async_copy(other.at[rows], staged.at[rows], in_sems.at[slot]))
        writes.append(
            pltpu.make_async_copy(
                staged.at[rows], out.at[pl.ds(slot * PAGE + half * HALF, HALF)], out_sems.at[slot]
            )
        )
    for read in reads:
        read.start()
    for read, write in zip(reads, writes):
        read.wait()
        write.start()
    for write in writes:
        write.wait()


def fill(place, cache, other):
    return pl.pallas_call(
        fill_kernel,
        grid_spec=pltpu.PrefetchScalarGridSpec(
            num_scalar_prefetch=1,
            grid=(1,),
            in_specs=[pl.BlockSpec(memory_space=pl.ANY)] * 2,
            out_specs=pl.BlockSpec(memory_space=pl.ANY),
            scratch_shapes=[
                pltpu.VMEM((8 * HALF, PAGE, KVW), BF16),
                pltpu.SemaphoreType.DMA((8,)),
                pltpu.SemaphoreType.DMA((8,)),
            ],
        ),
        out_shape=jax.ShapeDtypeStruct(cache.shape, cache.dtype),
        input_output_aliases={1: 0},
        compiler_params=pltpu.CompilerParams(vmem_limit_bytes=VMEM_LIMIT),
        name="fill",
    )(place, cache, other)


UP = tuple((i, i + 4) for i in range(12))
DOWN = tuple((i + 4, i) for i in range(12))
ACROSS = tuple((i, i ^ 2) for i in range(16))
TWIN = tuple((i, i ^ 1) for i in range(16))


def ship(time, parts):
    used = [port for port in range(3) if units_of(port, time)]
    hops = (UP, DOWN, ACROSS)
    return [(time, port, lax.ppermute(part, "pool", hops[port])) for port, part in zip(used, parts)]


def finish(plan, place, own, landed, after):
    give = gather("give", 0, plan, place, own, landed, after)
    other = lax.ppermute(give, "pool", TWIN)
    return fill(place, gather("own", 0, plan, place, own, landed, give), other)


def finish_in_two(plan, place, own, landed, after, attention):
    early = [item for item in landed if item[0] < ROUNDS - 1]
    last = [item for item in landed if item[0] >= ROUNDS - 1]
    low = 16 + SLOTS * (ROUNDS - 1)
    give = gather("give", 0, plan, place, own, early, after)
    keep = gather("own", 0, plan, place, own, early, after)
    keep, _ = lax.optimization_barrier((keep, attention))
    give = gather("give", low, plan, place, own, last, keep, give)
    other = lax.ppermute(give, "pool", TWIN)
    return fill(place, gather("own", low, plan, place, own, last, give, keep), other)


def local_lanes(anchors, deltas, scales, queries, lengths, page_owner):
    position = lax.axis_index("pool")
    number = anchors.shape[0]
    by_token = jnp.transpose(deltas, (1, 0, 2))
    place = jnp.stack([position >> 1, position & 1]).astype(I32)
    lines = jnp.transpose(scales)
    keep, give = decode_halves(place, page_owner, anchors, by_token, lines)
    got = lax.ppermute(give, "pool", TWIN)
    plan = make_plan(place, lengths, page_owner)
    own = (keep, got)
    landed = []
    after = partial = plan
    for time in range(ROUNDS):
        parts = pick(time, plan, place, own, landed, after)
        landed += ship(time, parts)
        after = parts[0]
        if 1 <= time <= KVH:
            seen, _ = lax.optimization_barrier((plan, after))
            after = partial = attend(time - 1, seen, queries, anchors, by_token, lines, partial)
    partial, _ = lax.optimization_barrier((partial, after))
    swapped = lax.all_to_all(partial, "pool", split_axis=0, concat_axis=0, tiled=True)
    attention = merge(plan, place, swapped, after)
    cache = finish_in_two(plan, place, own, landed, after, attention)

    def in_time(cache):
        return cache

    def late(cache):
        more, last = list(landed), plan
        for time in range(ROUNDS, LIMIT):
            parts = pick(time, plan, place, own, more, last)
            more += ship(time, parts)
            last = parts[0]
        return finish(plan, place, own, more, last)

    def padded(cache):
        owners = lax.dynamic_slice_in_dim(page_owner, position * number, number, 0)
        index = jnp.arange(number, dtype=I32)
        ahead = (owners[None, :] < owners[:, None]) | (
            (owners[None, :] == owners[:, None]) & (index[None, :] < index[:, None])
        )
        order = jnp.sum(ahead.astype(I32), axis=1)
        devices = jnp.arange(16, dtype=I32)
        sent = jnp.any(owners[None, :] == devices[:, None], axis=1).astype(I32)
        slabs = decode_sorted(order, sent, jnp.cumsum(sent) - sent, anchors, by_token, scales)
        arrived = lax.all_to_all(slabs, "pool", split_axis=0, concat_axis=0, tiled=True)
        taken = jnp.any((page_owner == position).reshape(16, number), axis=1).astype(I32)
        return assemble(taken, jnp.cumsum(taken) - taken, arrived, number)

    needed = plan[2, 0]
    branch = (needed > ROUNDS).astype(I32) + (needed > LIMIT).astype(I32)
    cache = lax.switch(branch, (in_time, late, padded), cache)
    return (cache, attention)


def decode_pages(anchors, deltas, scales):
    block_scale = jnp.repeat(scales, HD, axis=1)
    rebuilt = anchors[:, None, :].astype(jnp.float32) + block_scale[:, None, :] * deltas.astype(
        jnp.float32
    )
    return jnp.concatenate([anchors[:, None, :], rebuilt.astype(jnp.bfloat16)], axis=1)


def page_scores(work_pages, queries, requests):
    number = work_pages.shape[0]
    key_rows = work_pages[:, :, : KVH * HD].reshape(number, PAGE, KVH, HD)
    picked = jnp.take(queries, requests, axis=0).reshape(number, STEPS, KVH, QH // KVH, HD)
    scores = jnp.einsum(
        "nskgd,ntkd->nskgt", picked, key_rows, preferred_element_type=jnp.float32
    ) * HD ** (-0.5)
    return (scores, jnp.max(scores, axis=4))


def accumulate(scores, page_max, work_pages, requests, shift_max):
    number = work_pages.shape[0]
    rows_out = shift_max.shape[0]
    block_size = min(32, number)
    blocks = number // block_size
    value_rows = work_pages[:, :, KVH * HD :].reshape(blocks, block_size, PAGE, KVH, HD)
    score_blocks = scores.reshape((blocks, block_size) + scores.shape[1:])
    max_blocks = page_max.reshape((blocks, block_size) + page_max.shape[1:])
    request_blocks = requests.reshape(blocks, block_size)

    def block_step(running, pieces):
        totals, numerator = running
        block_scores, block_max, block_values, block_requests = pieces
        exponent = jnp.exp(block_scores - block_max[..., None])
        weights = exponent.astype(jnp.bfloat16)
        page_out = jnp.einsum(
            "nskgt,ntkd->nskgd", weights, block_values, preferred_element_type=jnp.float32
        )
        factor = jnp.exp(block_max - jnp.take(shift_max, block_requests, axis=0))
        select = (block_requests[None, :] == jnp.arange(rows_out, dtype=jnp.int32)[:, None]).astype(
            jnp.float32
        )
        spread = select[:, :, None, None, None] * factor[None]
        totals = totals + jnp.sum(spread * jnp.sum(exponent, axis=4)[None], axis=1)
        numerator = numerator + jnp.einsum(
            "rnskg,nskgd->rskgd", spread, page_out, precision=lax.Precision.HIGHEST
        )
        return ((totals, numerator), None)

    start_totals = jnp.zeros(shift_max.shape, jnp.float32)
    start_numer = jnp.zeros(shift_max.shape + (HD,), jnp.float32)
    finals, ignored = lax.scan(
        block_step,
        (start_totals, start_numer),
        (score_blocks, max_blocks, value_rows, request_blocks),
    )
    return finals


def request_of(index, request_ends):
    return jnp.sum((index[:, None] >= request_ends[None, :]).astype(jnp.int32), axis=1)


def local(anchors, deltas, scales, queries, lengths, page_owner):
    devices = lax.axis_size("pool")
    position = lax.axis_index("pool")
    number = anchors.shape[0]
    capacity = max(2, 2 * number // devices)
    pages = decode_pages(anchors, deltas, scales)
    request_ends = jnp.cumsum(lengths)
    owners = lax.dynamic_slice_in_dim(page_owner, position * number, number, 0)
    marked = (owners[:, None] == jnp.arange(devices, dtype=jnp.int32)[None, :]).astype(jnp.int32)
    ranking = jnp.sum((jnp.cumsum(marked, axis=0) - 1) * marked, axis=1)
    slot_ids = owners * capacity + ranking
    matches = slot_ids[None, :] == jnp.arange(devices * capacity, dtype=jnp.int32)[:, None]
    sources = jnp.sum(jnp.where(matches, jnp.arange(number, dtype=jnp.int32)[None, :], 0), axis=1)
    outgoing = jnp.take(pages, sources, axis=0)
    arrived = lax.all_to_all(outgoing, "pool", split_axis=0, concat_axis=0, tiled=True)
    held_pages = jnp.nonzero(page_owner == position, size=number)[0].astype(jnp.int32)
    senders = held_pages // number
    before = jnp.sum((held_pages[None, :] < (senders * number)[:, None]).astype(jnp.int32), axis=1)
    row_ids = senders * capacity + jnp.arange(number, dtype=jnp.int32) - before
    cache = jnp.take(arrived, row_ids, axis=0)
    columns = QH * HD // devices
    requests = request_of(held_pages, request_ends)
    scores, page_max = page_scores(cache, queries, requests)
    onehot = requests[None, :] == jnp.arange(REQS, dtype=jnp.int32)[:, None]
    local_max = jnp.max(jnp.where(onehot[:, :, None, None, None], page_max[None], -1e30), axis=1)
    global_max = lax.pmax(local_max.astype(jnp.bfloat16), "pool").astype(local_max.dtype)
    totals, numerator = accumulate(scores, page_max, cache, requests, global_max)
    summed, numerator = lax.psum((totals, numerator), "pool")
    whole = (numerator / summed[..., None]).reshape(REQS, STEPS, QH * HD)
    result = lax.dynamic_slice_in_dim(whole, position * columns, columns, 2)
    return (cache, result.astype(jnp.bfloat16))


def solution(mesh):
    placed = (
        P(("groups", "pool"), None),
        P(("groups", "pool"), None, None),
        P(("groups", "pool"), None),
        P("groups", None, None),
        P("groups"),
        P("groups"),
    )
    lanes = mesh.shape["pool"] == 16
    return jax.shard_map(
        local_lanes if lanes else local,
        mesh=mesh,
        in_specs=placed,
        out_specs=(P(("groups", "pool"), None, None), P("groups", None, "pool")),
        check_vma=False,
    )
```

```python
import functools
import jax
import jax.numpy as jnp
from jax import lax
from jax.experimental import pallas as pl
from jax.experimental.pallas import tpu as pltpu
from jax.sharding import PartitionSpec as P

QH = 64
KVH = 4
HD = 128
PAGE = 16
STEPS = 8
REQS = 16
KVW = 2 * KVH * HD
SPAN = 3
LOW = -1e30
VMEM_LIMIT = 48 * 1024 * 1024
F32 = jnp.float32
BF16 = jnp.bfloat16
I32 = jnp.int32


def decode_kernel(chunk, place, flags, blocks, anchors, deltas, scales, out, rows, staged, sems):
    step = pl.program_id(0)
    for head in range(2 * KVH):
        cols = slice(head * HD, (head + 1) * HD)
        scale = jnp.broadcast_to(scales[:, head : head + 1], (chunk, HD))
        anchor = anchors[:, cols].astype(F32)
        rows[head * PAGE * chunk : head * PAGE * chunk + chunk, :] = anchor
        for token in range(1, PAGE):
            start = (head * PAGE + token) * chunk
            rows[start : start + chunk, :] = anchor + scale * deltas[token - 1, :, cols].astype(F32)
    for page in range(chunk):
        picked = [
            rows[pl.ds(head * PAGE * chunk + page, PAGE, stride=chunk), :]
            for head in range(2 * KVH)
        ]
        staged[place[step * chunk + page]] = jnp.concatenate(picked, axis=1).astype(BF16)

    @pl.when(step == pl.num_programs(0) - 1)
    def flush():
        copies = []
        for owner in range(16):
            copy = pltpu.make_async_copy(
                staged.at[pl.ds(blocks[owner] * PAGE, PAGE)],
                out.at[pl.ds(owner * PAGE, PAGE)],
                sems.at[owner],
            )
            pl.when(flags[owner] > 0)(copy.start)
            copies.append(copy)
        for owner in range(16):
            pl.when(flags[owner] > 0)(copies[owner].wait)


def decode_sorted(place, flags, blocks, anchors, deltas, scales):
    number = anchors.shape[0]
    chunk = 16
    return pl.pallas_call(
        functools.partial(decode_kernel, chunk),
        grid_spec=pltpu.PrefetchScalarGridSpec(
            num_scalar_prefetch=3,
            grid=(number // chunk,),
            in_specs=[
                pl.BlockSpec((chunk, KVW), lambda i, *_: (i, 0)),
                pl.BlockSpec((PAGE - 1, chunk, KVW), lambda i, *_: (0, i, 0)),
                pl.BlockSpec((chunk, 2 * KVH), lambda i, *_: (i, 0)),
            ],
            out_specs=pl.BlockSpec(memory_space=pl.ANY),
            scratch_shapes=[
                pltpu.VMEM((2 * KVH * PAGE * chunk, HD), F32),
                pltpu.VMEM((number, PAGE, KVW), BF16),
                pltpu.SemaphoreType.DMA((16,)),
            ],
        ),
        out_shape=jax.ShapeDtypeStruct((16 * PAGE, PAGE, KVW), BF16),
        compiler_params=pltpu.CompilerParams(vmem_limit_bytes=VMEM_LIMIT),
        name="decode_sorted",
    )(place, flags, blocks, anchors, deltas, scales)


def attend_kernel(head, plan, requests, first, second, third, key_anchor, val_anchor, key_delta, val_delta, scales, after, out, keys, vals):
    number = key_anchor.shape[0]
    columns = jnp.transpose(scales[...])
    key_scale = columns[:, head : head + 1]
    val_scale = columns[:, head + KVH : head + KVH + 1]
    for anchor, delta, scale, kept in (
        (key_anchor, key_delta, key_scale, keys),
        (val_anchor, val_delta, val_scale, vals),
    ):
        kept[0:number, :] = anchor[...]
        wide = anchor[...].astype(F32)
        for token in range(1, PAGE):
            kept[token * number : (token + 1) * number, :] = (
                wide + scale * delta[token - 1].astype(F32)
            ).astype(BF16)
    token_request = jnp.concatenate([requests[4:5, :]] * PAGE, axis=1) - plan[5, 0]
    rows = STEPS * QH // KVH
    eye = lax.broadcasted_iota(I32, (rows, rows), 0) == lax.broadcasted_iota(I32, (rows, rows), 1)
    pieces = []
    for slot, queries in enumerate((first, second, third)):
        wide = queries[0].astype(F32)
        picked = jnp.concatenate(
            [wide[:, group * HD : (group + 1) * HD] for group in range(QH // KVH)], axis=0
        ).astype(BF16)
        scores = lax.dot_general(
            picked, keys[...], (((1,), (1,)), ((), ())), preferred_element_type=F32
        ) * HD ** (-0.5)
        inside = token_request == slot
        scores = jnp.where(inside, scores, LOW)
        top = jnp.max(scores, axis=1, keepdims=True)
        exponent = jnp.where(inside, jnp.exp(scores - top), 0.0)
        total = jnp.maximum(jnp.sum(exponent, axis=1, keepdims=True), 1e-30)
        numer = jnp.dot(exponent.astype(BF16), vals[...], preferred_element_type=F32)
        mean = (numer * (1.0 / total)).astype(BF16)
        quarter = rows // 4
        for part in range(4):
            out[part, slot * quarter : (slot + 1) * quarter, :] = mean[
                part * quarter : (part + 1) * quarter
            ]
        level = top + jnp.log(total)
        line = jnp.sum(jnp.where(eye, level, 0.0), axis=0, keepdims=True)
        for _ in range(3):
            piece = line.astype(BF16).astype(F32)
            pieces.append(piece)
            line = line - piece
    pieces.append(jnp.zeros((16 - len(pieces), rows), F32))
    stats = jnp.concatenate(pieces, axis=0).astype(BF16)
    for part in range(4):
        out[part, 96:112, :] = stats


def attend(head, plan, queries, anchors, deltas, scales, after):
    number = anchors.shape[0]
    rows = STEPS * QH // KVH
    return pl.pallas_call(
        functools.partial(attend_kernel, head),
        grid_spec=pltpu.PrefetchScalarGridSpec(
            num_scalar_prefetch=1,
            grid=(1,),
            in_specs=[
                pl.BlockSpec((8, number), lambda i, *_: (0, 0)),
                *[
                    pl.BlockSpec((1, STEPS, rows * HD // STEPS), lambda i, p, k=k: (p[5, 0] + k, 0, head))
                    for k in range(SPAN)
                ],
                pl.BlockSpec((number, HD), lambda i, *_: (0, head)),
                pl.BlockSpec((number, HD), lambda i, *_: (0, head + KVH)),
                pl.BlockSpec((PAGE - 1, number, HD), lambda i, *_: (0, 0, head)),
                pl.BlockSpec((PAGE - 1, number, HD), lambda i, *_: (0, 0, head + KVH)),
                pl.BlockSpec((2 * KVH, number), lambda i, *_: (0, 0)),
                pl.BlockSpec(memory_space=pl.ANY),
            ],
            out_specs=pl.BlockSpec((4, 112, HD), lambda i, *_: (head, 0, 0)),
            scratch_shapes=[
                pltpu.VMEM((PAGE * number, HD), BF16),
                pltpu.VMEM((PAGE * number, HD), BF16),
            ],
        ),
        out_shape=jax.ShapeDtypeStruct((16, 112, HD), BF16),
        input_output_aliases={} if head == 0 else {10: 0},
        compiler_params=pltpu.CompilerParams(vmem_limit_bytes=VMEM_LIMIT),
        name=f"attend_{head}",
    )(plan, plan, queries, queries, queries, anchors, anchors, deltas, deltas, scales, after)


def merge_kernel(plan, place, parts, after, out, level, top, total, numer):
    quarter = 32
    row = lax.broadcasted_iota(I32, (quarter, HD), 0)
    lane = lax.broadcasted_iota(I32, (quarter, HD), 1)
    mine = lane == row + quarter * ((place[0] & 1) * 2 + place[1])
    top[...] = jnp.full(top.shape, LOW, F32)
    total[...] = jnp.zeros(total.shape, F32)
    numer[...] = jnp.zeros(numer.shape, F32)
    for sender in range(16):
        stats = parts[sender, 96:112, :].astype(F32)
        for slot in range(SPAN):
            line = stats[3 * slot : 3 * slot + 1] + (
                stats[3 * slot + 1 : 3 * slot + 2] + stats[3 * slot + 2 : 3 * slot + 3]
            )
            column = jnp.sum(jnp.where(mine, line, 0.0), axis=1, keepdims=True)
            column = jnp.broadcast_to(column, (quarter, HD))
            level[sender * SPAN + slot] = column
            request = plan[3, sender] + slot
            top[request] = jnp.maximum(top[request], column)
    for sender in range(16):
        for slot in range(SPAN):
            request = plan[3, sender] + slot
            weight = jnp.exp(level[sender * SPAN + slot] - top[request])
            mean = parts[sender, slot * quarter : (slot + 1) * quarter, :].astype(F32)
            total[request] += weight
            numer[request] += weight * mean
    for request in range(REQS):
        result = (numer[request] / total[request]).astype(BF16)
        for group in range(4):
            out[request, :, group * HD : (group + 1) * HD] = result[
                group * STEPS : (group + 1) * STEPS
            ]


def merge(plan, place, parts, after):
    return pl.pallas_call(
        merge_kernel,
        grid_spec=pltpu.PrefetchScalarGridSpec(
            num_scalar_prefetch=2,
            grid=(1,),
            in_specs=[
                pl.BlockSpec((16, 112, HD), lambda i, *_: (0, 0, 0)),
                pl.BlockSpec(memory_space=pl.ANY),
            ],
            out_specs=pl.BlockSpec((REQS, STEPS, 4 * HD), lambda i, *_: (0, 0, 0)),
            scratch_shapes=[
                pltpu.VMEM((16 * SPAN, 32, HD), F32),
                pltpu.VMEM((REQS, 32, HD), F32),
                pltpu.VMEM((REQS, 32, HD), F32),
                pltpu.VMEM((REQS, 32, HD), F32),
            ],
        ),
        out_shape=jax.ShapeDtypeStruct((REQS, STEPS, 4 * HD), BF16),
        compiler_params=pltpu.CompilerParams(vmem_limit_bytes=VMEM_LIMIT),
        name="merge",
    )(plan, place, parts, after)


def assemble_kernel(flags, blocks, arrived, out, staged, in_sems, out_sems):
    reads, writes = [], []
    for sender in range(16):
        rows = pl.ds(blocks[sender] * PAGE, PAGE)
        source = arrived.at[pl.ds(sender * PAGE, PAGE)]
        reads.append(pltpu.make_async_copy(source, staged.at[rows], in_sems.at[sender]))
        writes.append(pltpu.make_async_copy(staged.at[rows], out.at[rows], out_sems.at[sender]))
    for sender in range(16):
        pl.when(flags[sender] > 0)(reads[sender].start)
    for sender in range(16):

        @pl.when(flags[sender] > 0)
        def forward():
            reads[sender].wait()
            writes[sender].start()

    for sender in range(16):
        pl.when(flags[sender] > 0)(writes[sender].wait)


def assemble(flags, blocks, arrived, number):
    return pl.pallas_call(
        assemble_kernel,
        grid_spec=pltpu.PrefetchScalarGridSpec(
            num_scalar_prefetch=2,
            grid=(1,),
            in_specs=[pl.BlockSpec(memory_space=pl.ANY)],
            out_specs=pl.BlockSpec(memory_space=pl.ANY),
            scratch_shapes=[
                pltpu.VMEM((number, PAGE, KVW), BF16),
                pltpu.SemaphoreType.DMA((16,)),
                pltpu.SemaphoreType.DMA((16,)),
            ],
        ),
        out_shape=jax.ShapeDtypeStruct((number, PAGE, KVW), BF16),
        compiler_params=pltpu.CompilerParams(vmem_limit_bytes=VMEM_LIMIT),
        name="assemble",
    )(flags, blocks, arrived)


ROUNDS = 9
LIMIT = 10
UNIT = 2
LAG = 2
SIDE_LAG = 3
SLOTS = 7
SIDE = (3, 0, 3, 0, 3, 0, 2, 2, 1)
HALF = PAGE // 2
FAR = 1e6


def units_of(port, time):
    if port < 2:
        return UNIT
    return SIDE[time] if time < len(SIDE) else 2


def plan_kernel(place, lengths, owners, out):
    chip = place[0]
    row = lax.broadcasted_iota(I32, (16, 128), 0)
    lanes = lax.broadcasted_iota(I32, (16, 128), 1)
    sender_of = lanes >> 3
    turn = (lanes & 7).astype(F32)
    table = owners[...]
    running = jnp.zeros((16, 1), F32)
    sends = []
    targets = jnp.zeros((16, 128), F32)
    for owner in range(16):
        flag = jnp.max(jnp.where(table == owner, 1.0, 0.0), axis=1, keepdims=True)
        targets += jnp.where(turn == running, flag * owner, 0.0)
        sends.append(flag)
        running = running + flag
    dest = jnp.sum(jnp.where(row == sender_of, targets, 0.0), axis=0, keepdims=True)
    hits = jnp.zeros((16, 128), F32)
    for owner in range(16):
        hits += sends[owner] * jnp.where(dest == owner, 1.0, 0.0)
    rank = jnp.sum(jnp.where(row < sender_of, hits, 0.0), axis=0, keepdims=True).astype(I32)
    dest = dest.astype(I32)
    lane = lax.broadcasted_iota(I32, (1, 128), 1)
    sender = lane >> 3
    from_z, from_x = sender >> 2, (sender >> 1) & 1
    to_z, to_x = dest >> 2, (dest >> 1) & 1
    crosses = (from_z >> 1) != (to_z >> 1)
    below = jnp.where(
        lax.broadcasted_iota(I32, (128, 128), 0) < lax.broadcasted_iota(I32, (128, 128), 1), 1.0, 0.0
    )
    line = from_x
    for side in range(2):
        leaving = crosses & ((from_z >> 1) == side)
        free = jnp.where(leaving & (from_x != to_x), 1.0, 0.0)
        fixed = jnp.where(leaving & (from_x == to_x), 1.0, 0.0)
        tilt = jnp.sum(fixed * (2 * from_x - 1).astype(F32), axis=1, keepdims=True)
        count = jnp.sum(free, axis=1, keepdims=True)
        share = jnp.clip(jnp.floor((tilt + count) * 0.5), 0.0, count)
        step = share / jnp.maximum(count, 1.0)
        index = jnp.dot(jnp.broadcast_to(free, (8, 128)), below, preferred_element_type=F32)[0:1]
        first = jnp.floor((index + 1.0) * step + 1e-3) > jnp.floor(index * step + 1e-3)
        line = jnp.where(free > 0.0, jnp.where(first, 0, 1), line)
    chips = lax.broadcasted_iota(I32, (8, 128), 0)
    mine = lax.broadcasted_iota(I32, (8, 1), 0) == chip

    def round_step(time, carry):
        at_z, at_x, ready, code, steps, needed = carry
        waits = crosses & ((at_z >> 1) == (from_z >> 1))
        turns = ((at_z == to_z) & (at_x != to_x)) | (waits & (line != at_x))
        along = jnp.logical_not(turns) & (at_z != to_z)
        left = jnp.abs(to_z - at_z) + jnp.where(at_x != to_x, 1, 0)
        key = ((8 - left) * 128 + lane).astype(F32)
        here = (at_z * 2 + at_x == chips) & (ready <= time)
        heading = jnp.where(turns, 2, jnp.where(along, jnp.where(to_z > at_z, 0, 1), 3))
        moved = jnp.zeros((1, 128), F32)
        landed = jnp.zeros((1, 128), F32)
        value = (code + 1).astype(F32)
        side = sum(jnp.where(time == t, units_of(2, t), 0) for t in range(LIMIT))
        for port in range(3):
            keys = jnp.where(here & (heading == port), key, FAR)
            for unit in range(UNIT if port < 2 else 3):
                if port == 2:
                    keys = jnp.where(unit < side, keys, FAR)
                least = jnp.min(keys, axis=1, keepdims=True)
                chosen = jnp.where((keys == least) & (keys < FAR), 1.0, 0.0)
                source = jnp.sum(chosen * value, axis=1, keepdims=True)
                source = jnp.sum(jnp.where(mine, source, 0.0), axis=0, keepdims=True)
                slot = SLOTS * time + UNIT * port + unit
                steps = steps + jnp.where(lane == slot, source, 0.0)
                taken = jnp.sum(chosen, axis=0, keepdims=True)
                moved = moved + taken * (port + 1)
                landed = landed + taken * (slot + 16).astype(F32)
                keys = jnp.where(chosen > 0.0, FAR, keys)
        went = moved.astype(I32)
        at_z = at_z + jnp.where(went == 1, 1, 0) - jnp.where(went == 2, 1, 0)
        at_x = jnp.where(went == 3, 1 - at_x, at_x)
        ready = jnp.where(went > 0, time + jnp.where(went == 3, SIDE_LAG, LAG), ready)
        code = jnp.where(went > 0, landed.astype(I32), code)
        any_move = jnp.max(moved, axis=1, keepdims=True)
        needed = jnp.where(any_move > 0.0, (time + 1).astype(F32), needed)
        return at_z, at_x, ready, code, steps, needed

    start = (
        from_z,
        from_x,
        jnp.zeros((1, 128), I32),
        (sender & 1) * 8 + (lane & 7),
        jnp.zeros((1, 128), F32),
        jnp.zeros((1, 1), F32),
    )
    at_z, at_x, ready, code, steps, needed = lax.fori_loop(0, LIMIT, round_step, start)
    undone = jnp.where((at_z == to_z) & (at_x == to_x), 0.0, 1.0)
    undone = jnp.max(undone, axis=1, keepdims=True)
    needed = jnp.where(undone > 0.0, float(LIMIT + 1), needed)
    arrives = (dest >> 1) == chip
    slots = (dest & 1) * 8 + rank
    final = jnp.sum(
        jnp.where((row == slots) & arrives, (code + 1).astype(F32), 0.0), axis=1, keepdims=True
    )
    final = jnp.sum(jnp.where(row == lanes, final, 0.0), axis=0, keepdims=True)
    out[0:1, :] = steps.astype(I32)
    out[1:2, :] = final.astype(I32)
    out[2:3, :] = jnp.broadcast_to(needed, (1, 128)).astype(I32)
    page = (2 * chip + place[1]) * 128 + lane
    requests = jnp.zeros((1, 128), I32)
    bases = jnp.zeros((1, 128), I32)
    end = 0
    for request in range(REQS):
        end = end + lengths[request]
        requests = requests + jnp.where(page >= end, 1, 0)
        bases = bases + jnp.where(lane * 128 >= end, 1, 0)
    bases = jnp.minimum(bases, REQS - SPAN)
    base = jnp.sum(jnp.where(lane == 2 * chip + place[1], bases, 0).astype(F32), axis=1, keepdims=True)
    out[3:4, :] = bases
    out[4:5, :] = requests
    out[5:6, :] = jnp.broadcast_to(base, (1, 128)).astype(I32)
    out[6:8, :] = jnp.zeros((2, 128), I32)


def make_plan(place, lengths, page_owner):
    return pl.pallas_call(
        plan_kernel,
        grid_spec=pltpu.PrefetchScalarGridSpec(
            num_scalar_prefetch=2,
            grid=(1,),
            in_specs=[pl.BlockSpec((16, 128), lambda i, *_: (0, 0))],
            out_specs=pl.BlockSpec((8, 128), lambda i, *_: (0, 0)),
        ),
        out_shape=jax.ShapeDtypeStruct((8, 128), I32),
        name="make_plan",
    )(place, lengths, page_owner.reshape(16, 128))


def halves_kernel(place, owners, anchors, deltas, scales, keep, give, swap, columns, ranks, order, rows, staged, sems):
    step = pl.program_id(0)
    count = PAGE * PAGE

    @pl.when(step == 0)
    def build():
        row = lax.broadcasted_iota(I32, (count, count), 0)
        lane = lax.broadcasted_iota(I32, (count, count), 1)
        swap[...] = jnp.where(lane == (row & 15) * PAGE + (row >> 4), 1.0, 0.0).astype(BF16)
        columns[...] = jnp.transpose(scales[...])
        number = owners.shape[1]
        row = lax.broadcasted_iota(I32, (number, number), 0)
        lane = lax.broadcasted_iota(I32, (number, number), 1)
        across = owners[pl.ds(2 * place[0] + place[1], 1), :].astype(F32)
        down = jnp.sum(jnp.where(row == lane, across, 0.0), axis=1, keepdims=True)
        ahead = (down < across) | ((down == across) & (row < lane))
        ranks[...] = jnp.sum(jnp.where(ahead, 1.0, 0.0), axis=0, keepdims=True).astype(I32)
        pltpu.make_async_copy(ranks, order, sems.at[2]).start()

    core = place[1]
    for part in range(anchors.shape[0] // PAGE):
        pages = slice(part * PAGE, (part + 1) * PAGE)
        for head in range(2 * KVH):
            cols = slice(head * HD, (head + 1) * HD)
            start = pl.multiple_of(step * anchors.shape[0] + part * PAGE, PAGE)
            scale = jnp.broadcast_to(columns[pl.ds(start, PAGE), head : head + 1], (PAGE, HD))
            first = anchors[pages, cols]
            anchor = first.astype(F32)
            rows[0:PAGE, cols] = first
            for token in range(1, PAGE):
                rebuilt = anchor + scale * deltas[token - 1, pages, cols].astype(F32)
                rows[token * PAGE : (token + 1) * PAGE, cols] = rebuilt.astype(BF16)
        turned = jnp.dot(swap[...], rows[...], preferred_element_type=F32).astype(BF16)
        if part == 0:

            @pl.when(step == 0)
            def ordered():
                pltpu.make_async_copy(ranks, order, sems.at[2]).wait()

        for page in range(PAGE):
            rank = order[0, step * anchors.shape[0] + part * PAGE + page]
            half = (rank >> 3) & 1
            slot = (half ^ core) * 64 + (rank >> 4) * HALF + (rank & 7)
            staged[slot] = turned[page * PAGE : (page + 1) * PAGE]

    @pl.when(step == pl.num_programs(0) - 1)
    def flush():
        copies = [
            pltpu.make_async_copy(staged.at[pl.ds(64, 64)], give, sems.at[0]),
            pltpu.make_async_copy(staged.at[pl.ds(0, 64)], keep, sems.at[1]),
        ]
        for copy in copies:
            copy.start()
        for copy in copies:
            copy.wait()


def decode_halves(place, page_owner, anchors, deltas, scales):
    number = anchors.shape[0]
    chunk = 2 * PAGE
    half = jax.ShapeDtypeStruct((number // 2, PAGE, KVW), BF16)
    return pl.pallas_call(
        halves_kernel,
        grid_spec=pltpu.PrefetchScalarGridSpec(
            num_scalar_prefetch=1,
            grid=(number // chunk,),
            in_specs=[
                pl.BlockSpec((16, number), lambda i, *_: (0, 0)),
                pl.BlockSpec((chunk, KVW), lambda i, *_: (i, 0)),
                pl.BlockSpec((PAGE - 1, chunk, KVW), lambda i, *_: (0, i, 0)),
                pl.BlockSpec((2 * KVH, number), lambda i, *_: (0, 0)),
            ],
            out_specs=[pl.BlockSpec(memory_space=pl.ANY)] * 2,
            scratch_shapes=[
                pltpu.VMEM((PAGE * PAGE, PAGE * PAGE), BF16),
                pltpu.VMEM((number, 2 * KVH), F32),
                pltpu.VMEM((1, number), I32),
                pltpu.SMEM((1, number), I32),
                pltpu.VMEM((PAGE * PAGE, KVW), BF16),
                pltpu.VMEM((number, PAGE, KVW), BF16),
                pltpu.SemaphoreType.DMA((3,)),
            ],
        ),
        out_shape=(half, half),
        compiler_params=pltpu.CompilerParams(vmem_limit_bytes=VMEM_LIMIT),
        name="decode_halves",
    )(place, page_owner.reshape(16, number), anchors, deltas, scales)


def fetch(code, core, own, landed, ports, target, sem):
    value = code - 1
    keep, got = own

    @pl.when((value >= 0) & (value < 16))
    def from_own():
        rows = pl.ds((value & 7) * HALF, HALF)

        @pl.when((value >> 3) == core)
        def kept():
            pltpu.make_async_copy(keep.at[rows], target, sem).start()

        @pl.when((value >> 3) != core)
        def gotten():
            pltpu.make_async_copy(got.at[rows], target, sem).start()

    for time, port, arrivals in landed:
        if port in ports:
            offset = value - 16 - SLOTS * time - UNIT * port

            @pl.when((offset >= 0) & (offset < units_of(port, time)))
            def from_round():
                rows = pl.ds(offset * HALF, HALF)
                pltpu.make_async_copy(arrivals.at[rows], target, sem).start()


def settle(code, own, target, sem):
    @pl.when(code > 0)
    def wait():
        pltpu.make_async_copy(own[0].at[pl.ds(0, HALF)], target, sem).wait()


def pick_kernel(time, tags, plan, place, *refs):
    own, landed = refs[:2], [tag + (ref,) for tag, ref in zip(tags, refs[2:])]
    used = [port for port in range(3) if units_of(port, time)]
    outs, sems = refs[-1 - len(used) : -1], refs[-1]
    for phase in range(2):
        for port, out in zip(used, outs):
            ports = (0, 1) if port == 2 else (port, 2)
            for unit in range(units_of(port, time)):
                code = plan[0, SLOTS * time + UNIT * port + unit]
                target = out.at[pl.ds(unit * HALF, HALF)]
                sem = sems.at[UNIT * port + unit]
                if phase == 0:
                    fetch(code, place[1], own, landed, ports, target, sem)
                else:
                    settle(code, own, target, sem)


def pick(time, plan, place, own, landed, after):
    landed = [item for item in landed if item[0] + (SIDE_LAG if item[1] == 2 else LAG) <= time]
    sources = list(own) + [item[2] for item in landed] + [after]
    pieces = [
        jax.ShapeDtypeStruct((units_of(port, time) * HALF, PAGE, KVW), BF16)
        for port in range(3)
        if units_of(port, time)
    ]
    return pl.pallas_call(
        functools.partial(pick_kernel, time, [item[:2] for item in landed]),
        grid_spec=pltpu.PrefetchScalarGridSpec(
            num_scalar_prefetch=2,
            grid=(1,),
            in_specs=[pl.BlockSpec(memory_space=pl.ANY)] * len(sources),
            out_specs=[pl.BlockSpec(piece.shape, lambda i, *_: (0, 0, 0)) for piece in pieces],
            scratch_shapes=[pltpu.SemaphoreType.DMA((SLOTS,))],
        ),
        out_shape=pieces,
        compiler_params=pltpu.CompilerParams(vmem_limit_bytes=VMEM_LIMIT),
        name=f"pick_{time}",
    )(plan, place, *sources)


def gather_kernel(mode, low, tags, plan, place, *refs):
    own, landed = refs[:2], [tag + (ref,) for tag, ref in zip(tags, refs[2:])]
    out, staged, in_sems, out_sems = refs[-4:]
    core = place[1]
    half = core if mode == "own" else 1 - core
    high = 16 + SLOTS * (1 + max(time for time, _ in tags))

    def code_of(slot):
        code = plan[1, half * 8 + slot]
        return jnp.where((code > low) & (code <= high), code, 0)

    def target_of(slot):
        return staged.at[pl.ds(slot * HALF, HALF)]

    def write_of(slot):
        start = slot * PAGE + core * HALF if mode == "own" else slot * HALF
        return pltpu.make_async_copy(
            target_of(slot), out.at[pl.ds(start, HALF)], out_sems.at[slot]
        )

    @pl.loop(0, 8)
    def read(slot):
        fetch(code_of(slot), core, own, landed, (0, 1, 2), target_of(slot), in_sems.at[slot])

    @pl.loop(0, 8)
    def forward(slot):
        settle(code_of(slot), own, target_of(slot), in_sems.at[slot])
        pl.when(code_of(slot) > 0)(write_of(slot).start)

    @pl.loop(0, 8)
    def close(slot):
        pl.when(code_of(slot) > 0)(write_of(slot).wait)


def gather(mode, low, plan, place, own, landed, after, base=None):
    sources = list(own) + [item[2] for item in landed] + [after]
    if base is not None:
        sources.append(base)
    pages = 8 * (PAGE if mode == "own" else HALF)
    return pl.pallas_call(
        functools.partial(gather_kernel, mode, low, [item[:2] for item in landed]),
        grid_spec=pltpu.PrefetchScalarGridSpec(
            num_scalar_prefetch=2,
            grid=(1,),
            in_specs=[pl.BlockSpec(memory_space=pl.ANY)] * len(sources),
            out_specs=pl.BlockSpec(memory_space=pl.ANY),
            scratch_shapes=[
                pltpu.VMEM((8 * HALF, PAGE, KVW), BF16),
                pltpu.SemaphoreType.DMA((8,)),
                pltpu.SemaphoreType.DMA((8,)),
            ],
        ),
        out_shape=jax.ShapeDtypeStruct((pages, PAGE, KVW), BF16),
        input_output_aliases={} if base is None else {1 + len(sources): 0},
        compiler_params=pltpu.CompilerParams(vmem_limit_bytes=VMEM_LIMIT),
        name=f"gather_{mode}",
    )(plan, place, *sources)


def fill_kernel(place, cache, other, out, staged, in_sems, out_sems):
    half = 1 - place[1]
    reads, writes = [], []
    for slot in range(8):
        rows = pl.ds(slot * HALF, HALF)
        reads.append(pltpu.make_async_copy(other.at[rows], staged.at[rows], in_sems.at[slot]))
        writes.append(
            pltpu.make_async_copy(
                staged.at[rows], out.at[pl.ds(slot * PAGE + half * HALF, HALF)], out_sems.at[slot]
            )
        )
    for read in reads:
        read.start()
    for read, write in zip(reads, writes):
        read.wait()
        write.start()
    for write in writes:
        write.wait()


def fill(place, cache, other):
    return pl.pallas_call(
        fill_kernel,
        grid_spec=pltpu.PrefetchScalarGridSpec(
            num_scalar_prefetch=1,
            grid=(1,),
            in_specs=[pl.BlockSpec(memory_space=pl.ANY)] * 2,
            out_specs=pl.BlockSpec(memory_space=pl.ANY),
            scratch_shapes=[
                pltpu.VMEM((8 * HALF, PAGE, KVW), BF16),
                pltpu.SemaphoreType.DMA((8,)),
                pltpu.SemaphoreType.DMA((8,)),
            ],
        ),
        out_shape=jax.ShapeDtypeStruct(cache.shape, cache.dtype),
        input_output_aliases={1: 0},
        compiler_params=pltpu.CompilerParams(vmem_limit_bytes=VMEM_LIMIT),
        name="fill",
    )(place, cache, other)


UP = tuple((i, i + 4) for i in range(12))
DOWN = tuple((i + 4, i) for i in range(12))
ACROSS = tuple((i, i ^ 2) for i in range(16))
TWIN = tuple((i, i ^ 1) for i in range(16))


def ship(time, parts):
    used = [port for port in range(3) if units_of(port, time)]
    hops = (UP, DOWN, ACROSS)
    return [(time, port, lax.ppermute(part, "pool", hops[port])) for port, part in zip(used, parts)]


def finish(plan, place, own, landed, after):
    give = gather("give", 0, plan, place, own, landed, after)
    other = lax.ppermute(give, "pool", TWIN)
    return fill(place, gather("own", 0, plan, place, own, landed, give), other)


def finish_in_two(plan, place, own, landed, after, attention):
    early = [item for item in landed if item[0] < ROUNDS - 1]
    last = [item for item in landed if item[0] >= ROUNDS - 1]
    low = 16 + SLOTS * (ROUNDS - 1)
    give = gather("give", 0, plan, place, own, early, after)
    keep = gather("own", 0, plan, place, own, early, after)
    keep, _ = lax.optimization_barrier((keep, attention))
    give = gather("give", low, plan, place, own, last, keep, give)
    other = lax.ppermute(give, "pool", TWIN)
    return fill(place, gather("own", low, plan, place, own, last, give, keep), other)


def local_lanes(anchors, deltas, scales, queries, lengths, page_owner):
    position = lax.axis_index("pool")
    number = anchors.shape[0]
    by_token = jnp.transpose(deltas, (1, 0, 2))
    place = jnp.stack([position >> 1, position & 1]).astype(I32)
    lines = jnp.transpose(scales)
    keep, give = decode_halves(place, page_owner, anchors, by_token, lines)
    got = lax.ppermute(give, "pool", TWIN)
    plan = make_plan(place, lengths, page_owner)
    own = (keep, got)
    landed = []
    after = partial = plan
    for time in range(ROUNDS):
        parts = pick(time, plan, place, own, landed, after)
        landed += ship(time, parts)
        after = parts[0]
        if 1 <= time <= KVH:
            seen, _ = lax.optimization_barrier((plan, after))
            after = partial = attend(time - 1, seen, queries, anchors, by_token, lines, partial)
    arrived = next(item[2] for item in landed if item[:2] == (ROUNDS - 2, 0))
    partial, _ = lax.optimization_barrier((partial, arrived))
    swapped = lax.all_to_all(partial, "pool", split_axis=0, concat_axis=0, tiled=True)
    attention = merge(plan, place, swapped, after)
    cache = finish_in_two(plan, place, own, landed, after, attention)

    def in_time(cache):
        return cache

    def late(cache):
        more, last = list(landed), plan
        for time in range(ROUNDS, LIMIT):
            parts = pick(time, plan, place, own, more, last)
            more += ship(time, parts)
            last = parts[0]
        return finish(plan, place, own, more, last)

    def padded(cache):
        owners = lax.dynamic_slice_in_dim(page_owner, position * number, number, 0)
        index = jnp.arange(number, dtype=I32)
        ahead = (owners[None, :] < owners[:, None]) | (
            (owners[None, :] == owners[:, None]) & (index[None, :] < index[:, None])
        )
        order = jnp.sum(ahead.astype(I32), axis=1)
        devices = jnp.arange(16, dtype=I32)
        sent = jnp.any(owners[None, :] == devices[:, None], axis=1).astype(I32)
        slabs = decode_sorted(order, sent, jnp.cumsum(sent) - sent, anchors, by_token, scales)
        arrived = lax.all_to_all(slabs, "pool", split_axis=0, concat_axis=0, tiled=True)
        taken = jnp.any((page_owner == position).reshape(16, number), axis=1).astype(I32)
        return assemble(taken, jnp.cumsum(taken) - taken, arrived, number)

    needed = plan[2, 0]
    branch = (needed > ROUNDS).astype(I32) + (needed > LIMIT).astype(I32)
    cache = lax.switch(branch, (in_time, late, padded), cache)
    return (cache, attention)


def decode_pages(anchors, deltas, scales):
    block_scale = jnp.repeat(scales, HD, axis=1)
    rebuilt = anchors[:, None, :].astype(jnp.float32) + block_scale[:, None, :] * deltas.astype(
        jnp.float32
    )
    return jnp.concatenate([anchors[:, None, :], rebuilt.astype(jnp.bfloat16)], axis=1)


def page_scores(work_pages, queries, requests):
    number = work_pages.shape[0]
    key_rows = work_pages[:, :, : KVH * HD].reshape(number, PAGE, KVH, HD)
    picked = jnp.take(queries, requests, axis=0).reshape(number, STEPS, KVH, QH // KVH, HD)
    scores = jnp.einsum(
        "nskgd,ntkd->nskgt", picked, key_rows, preferred_element_type=jnp.float32
    ) * HD ** (-0.5)
    return (scores, jnp.max(scores, axis=4))


def accumulate(scores, page_max, work_pages, requests, shift_max):
    number = work_pages.shape[0]
    rows_out = shift_max.shape[0]
    block_size = min(32, number)
    blocks = number // block_size
    value_rows = work_pages[:, :, KVH * HD :].reshape(blocks, block_size, PAGE, KVH, HD)
    score_blocks = scores.reshape((blocks, block_size) + scores.shape[1:])
    max_blocks = page_max.reshape((blocks, block_size) + page_max.shape[1:])
    request_blocks = requests.reshape(blocks, block_size)

    def block_step(running, pieces):
        totals, numerator = running
        block_scores, block_max, block_values, block_requests = pieces
        exponent = jnp.exp(block_scores - block_max[..., None])
        weights = exponent.astype(jnp.bfloat16)
        page_out = jnp.einsum(
            "nskgt,ntkd->nskgd", weights, block_values, preferred_element_type=jnp.float32
        )
        factor = jnp.exp(block_max - jnp.take(shift_max, block_requests, axis=0))
        select = (block_requests[None, :] == jnp.arange(rows_out, dtype=jnp.int32)[:, None]).astype(
            jnp.float32
        )
        spread = select[:, :, None, None, None] * factor[None]
        totals = totals + jnp.sum(spread * jnp.sum(exponent, axis=4)[None], axis=1)
        numerator = numerator + jnp.einsum(
            "rnskg,nskgd->rskgd", spread, page_out, precision=lax.Precision.HIGHEST
        )
        return ((totals, numerator), None)

    start_totals = jnp.zeros(shift_max.shape, jnp.float32)
    start_numer = jnp.zeros(shift_max.shape + (HD,), jnp.float32)
    finals, ignored = lax.scan(
        block_step,
        (start_totals, start_numer),
        (score_blocks, max_blocks, value_rows, request_blocks),
    )
    return finals


def request_of(index, request_ends):
    return jnp.sum((index[:, None] >= request_ends[None, :]).astype(jnp.int32), axis=1)


def local(anchors, deltas, scales, queries, lengths, page_owner):
    devices = lax.axis_size("pool")
    position = lax.axis_index("pool")
    number = anchors.shape[0]
    capacity = max(2, 2 * number // devices)
    pages = decode_pages(anchors, deltas, scales)
    request_ends = jnp.cumsum(lengths)
    owners = lax.dynamic_slice_in_dim(page_owner, position * number, number, 0)
    marked = (owners[:, None] == jnp.arange(devices, dtype=jnp.int32)[None, :]).astype(jnp.int32)
    ranking = jnp.sum((jnp.cumsum(marked, axis=0) - 1) * marked, axis=1)
    slot_ids = owners * capacity + ranking
    matches = slot_ids[None, :] == jnp.arange(devices * capacity, dtype=jnp.int32)[:, None]
    sources = jnp.sum(jnp.where(matches, jnp.arange(number, dtype=jnp.int32)[None, :], 0), axis=1)
    outgoing = jnp.take(pages, sources, axis=0)
    arrived = lax.all_to_all(outgoing, "pool", split_axis=0, concat_axis=0, tiled=True)
    held_pages = jnp.nonzero(page_owner == position, size=number)[0].astype(jnp.int32)
    senders = held_pages // number
    before = jnp.sum((held_pages[None, :] < (senders * number)[:, None]).astype(jnp.int32), axis=1)
    row_ids = senders * capacity + jnp.arange(number, dtype=jnp.int32) - before
    cache = jnp.take(arrived, row_ids, axis=0)
    columns = QH * HD // devices
    requests = request_of(held_pages, request_ends)
    scores, page_max = page_scores(cache, queries, requests)
    onehot = requests[None, :] == jnp.arange(REQS, dtype=jnp.int32)[:, None]
    local_max = jnp.max(jnp.where(onehot[:, :, None, None, None], page_max[None], -1e30), axis=1)
    global_max = lax.pmax(local_max.astype(jnp.bfloat16), "pool").astype(local_max.dtype)
    totals, numerator = accumulate(scores, page_max, cache, requests, global_max)
    summed, numerator = lax.psum((totals, numerator), "pool")
    whole = (numerator / summed[..., None]).reshape(REQS, STEPS, QH * HD)
    result = lax.dynamic_slice_in_dim(whole, position * columns, columns, 2)
    return (cache, result.astype(jnp.bfloat16))


def solution(mesh):
    placed = (
        P(("groups", "pool"), None),
        P(("groups", "pool"), None, None),
        P(("groups", "pool"), None),
        P("groups", None, None),
        P("groups"),
        P("groups"),
    )
    lanes = mesh.shape["pool"] == 16
    return jax.shard_map(
        local_lanes if lanes else local,
        mesh=mesh,
        in_specs=placed,
        out_specs=(P(("groups", "pool"), None, None), P("groups", None, "pool")),
        check_vma=False,
    )
```
